32 devices in a mesh: seq: 16 (over z, y, x), dp: 2 (over core).
Axes of the slice: x: 2, y: 2, z: 4, core: 2. Of those that a mesh axis runs over, the one named last changes fastest.
Arguments:
- queries: bfloat16 [2, 4096, 1024], P('dp', 'seq'), may hold values from -1000 to 1000, as said below
- key_rows: bfloat16 [2, 4096, 1024], P('dp', 'seq'), may hold values from -1000 to 1000, as said below
- value_rows: bfloat16 [2, 4096, 1024], P('dp', 'seq'), may hold values from -6 to 6
- cotangent: bfloat16 [2, 4096, 1024], P('dp', 'seq'), may hold values from -6 to 6
- w_out: bfloat16 [1024, 1024], P('dp'), may hold values from -0.1875 to 0.1875
- cluster_ids: int32 [2, 4096], P('dp', 'seq'), may hold values from 0 to 63, as said below
Outputs:
- projected: bfloat16 [2, 4096, 1024], P('dp', 'seq')
- grad_queries: bfloat16 [2, 4096, 1024], P('dp', 'seq')
- grad_keys: bfloat16 [2, 4096, 1024], P('dp', 'seq')
- grad_values: bfloat16 [2, 4096, 1024], P('dp', 'seq')
- weight_grad: float32 [1024, 1024], P(('seq', 'dp'))
The draws below stay inside these ranges and needn't reach their ends.
Inputs may be any that keep to these rules, and one draw needn't show every extreme that they name: `cluster_ids`: among the 256 tokens of one index of seq no cluster id occurs more than 8 times; in every sequence some cluster has exactly 8 tokens on every index of seq. `queries`: finite values. `key_rows`: finite values.
All inputs are finite; a program needn't handle non-finite values.
Results may differ from the reference program's by a relative error of at most 0.014.
Values may be sent and summed in bfloat16 or wider, within the bound.
A program may use at most 128 MiB of HBM per device.

```python
import math
import jax
import jax.numpy as jnp
from jax import lax

HEADS = 8
HD = 128
DOUT = 1024
CL_DEV = 4
TOK_DEV = 256
HW = 1024
CLUSTERS = 64
CAP = 8
BLOCK = 128
LEN = 4096
SEQS = 2
ALL = 8192


def scaled_rows(key):
    key_noise = jax.random.fold_in(key, 1)
    key_scale = jax.random.fold_in(key, 2)
    key_column = jax.random.fold_in(key, 3)
    noise = jax.random.normal(key_noise, (SEQS, LEN, HEADS, HD), jnp.float32)
    row_scale = jnp.exp(jax.random.uniform(key_scale, (SEQS, LEN, HEADS, 1), jnp.float32, 0.0, math.log(10.0)))
    column_scale = jnp.exp(jax.random.uniform(key_column, (HEADS, HD), jnp.float32, 0.0, math.log(10.0)))
    noise = jnp.clip(noise, -6.0, 6.0)
    return (noise * row_scale * column_scale).reshape(SEQS, LEN, HW)


def draw_queries(key, part):
    return scaled_rows(jax.random.fold_in(key, 11)).astype(jnp.bfloat16)


def draw_key_rows(key, part):
    return scaled_rows(jax.random.fold_in(key, 23)).astype(jnp.bfloat16)


def draw_cluster_ids(key, part):
    devices = LEN // TOK_DEV
    clusters = CL_DEV * devices
    capacity = 2 * TOK_DEV // clusters
    total_slots = clusters * capacity
    base = jax.random.fold_in(key, 37)
    full_base = jax.random.fold_in(base, 1)
    dev_base = jax.random.fold_in(base, 2)
    seq_index = jnp.arange(SEQS, dtype=jnp.int32)
    dev_index = jnp.arange(devices, dtype=jnp.int32)

    def fullest_of(seq_number):
        return jax.random.randint(jax.random.fold_in(full_base, seq_number), (), 0, clusters)
    fullest = jax.vmap(fullest_of)(seq_index)

    def one_device(seq_number, dev_number, offset):
        sub = jax.random.fold_in(jax.random.fold_in(dev_base, seq_number), dev_number)
        key_pick = jax.random.fold_in(sub, 1)
        key_order = jax.random.fold_in(sub, 2)
        forced = jnp.arange(capacity, dtype=jnp.int32)
        others = capacity + jax.random.permutation(key_pick, total_slots - capacity)[:TOK_DEV - capacity].astype(jnp.int32)
        chosen = jnp.concatenate([forced, others])
        relative = chosen // capacity
        labels = (relative + offset) % clusters
        return jax.random.permutation(key_order, labels).astype(jnp.int32)

    def one_sequence(seq_number, offset):
        return jax.vmap(lambda dev_number: one_device(seq_number, dev_number, offset))(dev_index)
    labels = jax.vmap(one_sequence)(seq_index, fullest)
    return labels.reshape(SEQS, LEN).astype(jnp.int32)


def steps_of(stream_key, extent, split, smallest, high):
    gain, own = 1.0, jax.random.fold_in(stream_key, 6)
    for position, shards_of in split:
        heights = jnp.exp(jax.random.uniform(jax.random.fold_in(own, position), (shards_of,), jnp.float32, smallest / len(split), high / len(split)))
        gain = gain * jnp.repeat(heights, extent[position] // shards_of).reshape([-1 if axis == position else 1 for axis in range(len(extent))])
    return gain


def bell_draw(rng, dims, scale, bound, pieces=(), kind=jnp.bfloat16):
    gain = steps_of(rng, dims, pieces, -0.22, 0.18) if pieces else 1.0
    array = jax.random.normal(rng, dims, jnp.float32) * scale * gain
    return jnp.minimum(jnp.maximum(array, -bound), bound).astype(kind)


def setup_inputs(seed: int = 0) -> dict:
    arg_keys = jax.random.split(jax.random.key(seed), 7)
    return {
        "queries": draw_queries(jax.random.fold_in(arg_keys[6], 71), 0),
        "key_rows": draw_key_rows(jax.random.fold_in(arg_keys[6], 71), 0),
        "value_rows": bell_draw(arg_keys[2], (SEQS, LEN, HW), 1.0, 6.0, ((0, 2), (1, 16))),
        "cotangent": bell_draw(arg_keys[3], (SEQS, LEN, DOUT), 1.0, 6.0, ((0, 2), (1, 16))),
        "w_out": bell_draw(arg_keys[4], (HW, DOUT), HW ** -0.5, 0.1875, ((0, 2),)),
        "cluster_ids": draw_cluster_ids(jax.random.fold_in(arg_keys[6], 71), 0),
    }


EPS = 1e-06

def head_norm(matrix):
    shaped = matrix.astype(jnp.float32).reshape(matrix.shape[0], HW // HD, HD)
    factor = lax.rsqrt(lax.optimization_barrier(jnp.mean(shaped * shaped, axis=-1, keepdims=True)) + EPS)
    return (shaped * factor, factor)

def norm_back(gradient, normed, factor):
    shaped = gradient.astype(jnp.float32).reshape(normed.shape)
    inner = lax.optimization_barrier(jnp.mean(shaped * normed, axis=-1, keepdims=True))
    return (factor * (shaped - normed * inner)).reshape(normed.shape[0], HW)

def block_rows(cluster_row):
    grouped = cluster_row.reshape(LEN // TOK_DEV, TOK_DEV)
    matching = grouped[:, :, None] == grouped[:, None, :]
    positions = jnp.arange(TOK_DEV, dtype=jnp.int32)
    earlier = positions[None, :] < positions[:, None]
    ranks = lax.optimization_barrier(jnp.sum(jnp.logical_and(matching, earlier[None]), axis=2)).astype(jnp.int32)
    devices = jnp.arange(LEN // TOK_DEV, dtype=jnp.int32)[:, None]
    return (devices * CAP + ranks).reshape(LEN).astype(jnp.int32)

def split_heads(blocks):
    return blocks.reshape(blocks.shape[0], blocks.shape[1], HW // HD, HD).astype(jnp.float32)

def attend(q_blk, k_blk, v_blk, key_valid):
    q_four, k_four, v_four = (split_heads(q_blk), split_heads(k_blk), split_heads(v_blk))
    scores = jnp.einsum('cqhd,ckhd->chqk', q_four, k_four) / math.sqrt(HD)
    positions = jnp.arange(BLOCK)
    below_diag = positions[None, :] <= positions[:, None]
    on_diagonal = positions[None, :] == positions[:, None]
    allowed = jnp.logical_or(jnp.logical_and(key_valid[:, None, None, :], below_diag[None, None]), on_diagonal[None, None])
    weights = jnp.where(allowed, jnp.exp(scores), 0.0)
    probs = weights / lax.optimization_barrier(jnp.sum(weights, axis=-1, keepdims=True))
    probs_b = probs.astype(jnp.bfloat16)
    attn = jnp.einsum('chqk,ckhd->cqhd', probs_b.astype(jnp.float32), v_four).astype(jnp.bfloat16)
    return (attn.reshape(q_blk.shape), probs, probs_b)

def attend_back(q_blk, k_blk, v_blk, probs, probs_b, attn, d_blk):
    q_four, k_four, v_four = (split_heads(q_blk), split_heads(k_blk), split_heads(v_blk))
    d_four, a_four = (split_heads(d_blk), split_heads(attn))
    pb_float = probs_b.astype(jnp.float32)
    grad_value = jnp.einsum('chqk,cqhd->ckhd', pb_float, d_four).astype(jnp.bfloat16)
    grad_prob = jnp.einsum('cqhd,ckhd->chqk', d_four, v_four)
    delta_row = lax.optimization_barrier(jnp.sum(d_four * a_four, axis=-1))
    grad_score = (probs * (grad_prob - jnp.transpose(delta_row, (0, 2, 1))[..., None])).astype(jnp.bfloat16)
    gs_float = grad_score.astype(jnp.float32)
    grad_qhat = (jnp.einsum('chqk,ckhd->cqhd', gs_float, k_four) / math.sqrt(HD)).astype(jnp.bfloat16)
    grad_khat = (jnp.einsum('chqk,cqhd->ckhd', gs_float, q_four) / math.sqrt(HD)).astype(jnp.bfloat16)
    shape = q_blk.shape
    return (grad_qhat.reshape(shape), grad_khat.reshape(shape), grad_value.reshape(shape))

def one_sequence(w_out, inputs):
    queries, key_rows, value_rows, cotangent, cluster_row = inputs
    q_norm, q_factor = head_norm(queries)
    k_norm, k_factor = head_norm(key_rows)
    q_hat = q_norm.reshape(LEN, HW).astype(jnp.bfloat16)
    k_hat = k_norm.reshape(LEN, HW).astype(jnp.bfloat16)
    rows_of = block_rows(cluster_row)

    def place(matrix):
        empty = jnp.zeros((CLUSTERS, BLOCK, matrix.shape[1]), matrix.dtype)
        return empty.at[cluster_row, rows_of].set(matrix)

    def take(blocks):
        return blocks[cluster_row, rows_of]
    key_valid = jnp.zeros((CLUSTERS, BLOCK), jnp.bool_).at[cluster_row, rows_of].set(True)
    q_blk, k_blk, v_blk = (place(q_hat), place(k_hat), place(value_rows))
    attn_blk, probs, probs_b = attend(q_blk, k_blk, v_blk, key_valid)
    attn = take(attn_blk)
    projected = jnp.dot(attn, w_out, preferred_element_type=jnp.float32).astype(jnp.bfloat16)
    grad_attn = jnp.dot(cotangent, w_out.T, preferred_element_type=jnp.float32).astype(jnp.bfloat16)
    grad_qblk, grad_kblk, grad_vblk = attend_back(q_blk, k_blk, v_blk, probs, probs_b, attn_blk, place(grad_attn))
    grad_queries = norm_back(take(grad_qblk), q_norm, q_factor).astype(jnp.bfloat16)
    grad_keys = norm_back(take(grad_kblk), k_norm, k_factor).astype(jnp.bfloat16)
    grad_values = take(grad_vblk)
    weight_term = jnp.dot(attn.T, cotangent, preferred_element_type=jnp.float32)
    return (projected, grad_queries, grad_keys, grad_values, weight_term)

def reference(queries, key_rows, value_rows, cotangent, w_out, cluster_ids):
    results = lax.map(partial_sequence(w_out), (queries, key_rows, value_rows, cotangent, cluster_ids))
    projected, grad_queries, grad_keys, grad_values, weight_terms = results
    weight_grad = lax.optimization_barrier(jnp.sum(weight_terms, axis=0)) / math.sqrt(ALL)
    return (projected, grad_queries, grad_keys, grad_values, weight_grad)

def partial_sequence(w_out):

    def runner(inputs):
        return one_sequence(w_out, inputs)
    return runner
```

```python
import functools
import math

import jax
import jax.numpy as jnp
from jax import lax
from jax.experimental import pallas as pl
from jax.experimental.pallas import tpu as pltpu
from jax.sharding import PartitionSpec as P

MESH = pl.DeviceIdType.MESH
HD = 128
CL_DEV = 4


EPS = 1e-06


def head_norm(matrix):
    shaped = matrix.astype(jnp.float32).reshape(matrix.shape[0], matrix.shape[1] // HD, HD)
    factor = lax.rsqrt(jnp.mean(shaped * shaped, axis=-1, keepdims=True) + EPS)
    return (shaped * factor, factor)


def norm_back(gradient, normed, factor):
    shaped = gradient.astype(jnp.float32).reshape(normed.shape)
    inner = jnp.mean(shaped * normed, axis=-1, keepdims=True)
    return (factor * (shaped - normed * inner)).reshape(normed.shape[0], -1)


def split_heads(blocks):
    return blocks.reshape(blocks.shape[0], blocks.shape[1], blocks.shape[2] // HD, HD)


def attend(q_blk, k_blk, v_blk, key_valid):
    q_four, k_four, v_four = (split_heads(q_blk), split_heads(k_blk), split_heads(v_blk))
    scores = jnp.einsum(
        "cqhd,ckhd->chqk", q_four, k_four, preferred_element_type=jnp.float32
    ) / math.sqrt(HD)
    positions = jnp.arange(q_blk.shape[1])
    below_diag = positions[None, :] <= positions[:, None]
    on_diagonal = positions[None, :] == positions[:, None]
    allowed = jnp.logical_or(
        jnp.logical_and(key_valid[:, None, None, :], below_diag[None, None]),
        on_diagonal[None, None],
    )
    weights = jnp.where(allowed, jnp.exp(scores), 0.0)
    probs = weights / jnp.sum(weights, axis=-1, keepdims=True)
    probs_b = probs.astype(jnp.bfloat16)
    attn = jnp.einsum(
        "chqk,ckhd->cqhd", probs_b, v_four, preferred_element_type=jnp.float32
    ).astype(jnp.bfloat16)
    return (attn.reshape(q_blk.shape), probs, probs_b)


def attend_back(q_blk, k_blk, v_blk, probs, probs_b, attn, d_blk):
    q_four, k_four, v_four = (split_heads(q_blk), split_heads(k_blk), split_heads(v_blk))
    d_four, a_four = (split_heads(d_blk), split_heads(attn))
    grad_value = jnp.einsum(
        "chqk,cqhd->ckhd", probs_b, d_four, preferred_element_type=jnp.float32
    ).astype(jnp.bfloat16)
    grad_prob = jnp.einsum("cqhd,ckhd->chqk", d_four, v_four, preferred_element_type=jnp.float32)
    delta_row = jnp.sum(d_four.astype(jnp.float32) * a_four.astype(jnp.float32), axis=-1)
    grad_score = (probs * (grad_prob - jnp.transpose(delta_row, (0, 2, 1))[..., None])).astype(
        jnp.bfloat16
    )
    grad_qhat = jnp.einsum(
        "chqk,ckhd->cqhd", grad_score, k_four, preferred_element_type=jnp.float32
    ) / math.sqrt(HD)
    grad_khat = jnp.einsum(
        "chqk,cqhd->ckhd", grad_score, q_four, preferred_element_type=jnp.float32
    ) / math.sqrt(HD)
    shape = q_blk.shape
    return (
        grad_qhat.astype(jnp.bfloat16).reshape(shape),
        grad_khat.astype(jnp.bfloat16).reshape(shape),
        grad_value.reshape(shape),
    )


def per_device_slots(queries, key_rows, value_rows, cotangent, w_out, cluster_ids):
    token_count = queries.shape[1]
    features = queries.shape[2]
    seq_devices = lax.axis_size("seq")
    data_devices = lax.axis_size("dp")
    capacity = 2 * token_count // (CL_DEV * seq_devices)
    total_slots = 2 * token_count
    labels = cluster_ids[0]
    positions = jnp.arange(token_count)
    matching = labels[:, None] == labels[None, :]
    earlier = positions[None, :] < positions[:, None]
    ranks = jnp.sum(jnp.logical_and(matching, earlier), axis=1)
    slot_index = labels * capacity + ranks

    def pack(matrix):
        empty = jnp.zeros((total_slots, matrix.shape[1]), matrix.dtype)
        return (
            empty.at[slot_index].set(matrix).reshape(seq_devices, CL_DEV, capacity, matrix.shape[1])
        )

    def unpack(returned):
        return returned.reshape(total_slots, -1)[slot_index]

    taken_slots = (
        jnp.zeros((total_slots,), jnp.bfloat16)
        .at[slot_index]
        .set(1.0)
        .reshape(seq_devices, CL_DEV, capacity)
    )
    q_norm, q_factor = head_norm(queries[0])
    k_norm, k_factor = head_norm(key_rows[0])
    q_hat = q_norm.reshape(token_count, features).astype(jnp.bfloat16)
    k_hat = k_norm.reshape(token_count, features).astype(jnp.bfloat16)
    cotan = cotangent[0]
    w_full = lax.all_gather(w_out, "dp", axis=0, tiled=True)
    received = (
        lax.all_to_all(pack(q_hat), "seq", split_axis=0, concat_axis=2, tiled=True),
        lax.all_to_all(pack(k_hat), "seq", split_axis=0, concat_axis=2, tiled=True),
        lax.all_to_all(pack(value_rows[0]), "seq", split_axis=0, concat_axis=2, tiled=True),
        lax.all_to_all(taken_slots, "seq", split_axis=0, concat_axis=2, tiled=True),
    )
    q_blk, k_blk, v_blk = (received[0][0], received[1][0], received[2][0])
    key_valid = received[3][0] > 0
    attn_blk, probs, probs_b = attend(q_blk, k_blk, v_blk, key_valid)
    attn_back = lax.all_to_all(attn_blk[None], "seq", split_axis=2, concat_axis=0, tiled=True)
    attn = unpack(attn_back)
    grad_attn = lax.dot_general(
        cotan, w_full, (((1,), (1,)), ((), ())), preferred_element_type=jnp.float32
    ).astype(jnp.bfloat16)
    grad_recv = lax.all_to_all(pack(grad_attn), "seq", split_axis=0, concat_axis=2, tiled=True)
    grad_qblk, grad_kblk, grad_vblk = attend_back(
        q_blk, k_blk, v_blk, probs, probs_b, attn_blk, grad_recv[0]
    )
    grads_back = (
        lax.all_to_all(grad_qblk[None], "seq", split_axis=2, concat_axis=0, tiled=True),
        lax.all_to_all(grad_kblk[None], "seq", split_axis=2, concat_axis=0, tiled=True),
        lax.all_to_all(grad_vblk[None], "seq", split_axis=2, concat_axis=0, tiled=True),
    )
    grad_qhat, grad_khat, grad_values = (
        unpack(grads_back[0]),
        unpack(grads_back[1]),
        unpack(grads_back[2]),
    )
    projected = jnp.dot(attn, w_full, preferred_element_type=jnp.float32).astype(jnp.bfloat16)
    grad_queries = norm_back(grad_qhat, q_norm, q_factor).astype(jnp.bfloat16)
    grad_keys = norm_back(grad_khat, k_norm, k_factor).astype(jnp.bfloat16)
    local_term = lax.dot_general(
        attn, cotan, (((0,), (0,)), ((), ())), preferred_element_type=jnp.float32
    )
    summed = lax.psum_scatter(local_term, ("seq", "dp"), scatter_dimension=0, tiled=True)
    weight_grad = summed / math.sqrt(token_count * seq_devices * data_devices)
    return (projected[None], grad_queries[None], grad_keys[None], grad_values[None], weight_grad)


def remote(source, target, sent, landed, device):
    return pltpu.make_async_remote_copy(
        src_ref=source,
        dst_ref=target,
        send_sem=sent,
        recv_sem=landed,
        device_id=device,
        device_id_type=MESH,
    )


def normalize(rows):
    wide = rows.astype(jnp.float32)
    factor = lax.rsqrt(jnp.mean(wide * wide, axis=-1, keepdims=True) + EPS)
    return wide * factor, factor


def lanes(head):
    return pl.ds(pl.multiple_of(head * HD, HD), HD)


def dot(a, b, ca, cb):
    return lax.dot_general(a, b, (((ca,), (cb,)), ((), ())), preferred_element_type=jnp.float32)


def layer_kernel(
    heads, scale,
    q_in, k_in, v_in, c_in, w_in, labels_ref,
    gq_ref, gk_ref, gv_ref, out_ref, grad_ref,
    q_ref, k_ref, v_ref, c_ref, w_full, x_ref, full, xfull, ids_ref, slots,
    onehot_t, qk, gv, e_ref, num, den, own_out, cross_out, st_mine, st_got,
    stage_a, stage_g, stage_x, got_a, got_g, got_x,
    a_ref, w_ref, w_held, kept, x_stage, x_got, y_stage, y_got, z_stage, z_got,
    loaded, w_sent, w_landed, sent, landed, xsent, xlanded, id_sent, id_landed, st_sent, st_landed,
    a_sent, a_landed, g_sent, g_landed, cx_sent, cx_landed,
    w_swap_sent, w_swap_landed, x_sent, x_landed, y_sent, y_landed, z_sent, z_landed,
):
    n = 2 * heads
    quarter = n // 4
    pairs = heads // 2
    chip, core = lax.axis_index("seq"), lax.axis_index("dp")
    other = 1 - core
    side, here = chip // heads, lax.rem(chip, heads)
    base, far = side * heads, (1 - side) * heads
    x, y, z = lax.rem(chip, 2), lax.rem(chip // 2, 2), chip // 4
    heavy = side == core
    light = jnp.logical_not(heavy)
    first = core == 0
    tokens = q_ref.shape[0]
    kind = q_ref.dtype
    clusters = qk.shape[1]
    rows_of = qk.shape[2]
    blocks = clusters // 2
    cap = rows_of // heads
    nslots = clusters * cap
    inv = 1.0 / math.sqrt(HD)

    ins = ((q_in, q_ref), (k_in, k_ref), (v_in, v_ref), (c_in, c_ref), (w_in, w_full.at[core]))
    loads = [
        pltpu.make_async_copy(source, target, loaded.at[i])
        for i, (source, target) in enumerate(ins)
    ]
    for load in loads:
        load.start()

    barrier = pltpu.get_barrier_semaphore()

    def greet(step, carry):
        pl.semaphore_signal(
            barrier, inc=1, device_id=(lax.rem(chip + step, n), core), device_id_type=MESH
        )
        return carry

    lax.fori_loop(1, n, greet, 0)
    pl.semaphore_signal(barrier, inc=1, device_id=(chip, other), device_id_type=MESH)

    wide = jnp.broadcast_to(labels_ref[...].astype(jnp.float32), (tokens, tokens))
    before = lax.broadcasted_iota(jnp.int32, wide.shape, 0) < lax.broadcasted_iota(
        jnp.int32, wide.shape, 1
    )
    same = jnp.logical_and(wide.T == wide, before)
    rank = jnp.sum(jnp.where(same, 1.0, 0.0), axis=0, keepdims=True)
    ids_ref[...] = jnp.broadcast_to(wide[0:1] * cap + rank, ids_ref.shape)
    slots[chip] = ids_ref[...]

    pl.semaphore_wait(barrier, n)
    w_copy = remote(w_in, w_full.at[core], w_sent, w_landed, (chip, other))
    w_copy.start()

    def data_copy(head):
        return remote(
            x_ref.at[head], full.at[here], sent.at[head], landed.at[here], (base + head, core)
        )

    def cross_copy(head):
        lane = pl.ds(pl.multiple_of(core * 2 * HD, 2 * HD), 2 * HD)
        return remote(
            x_ref.at[head, :, lane], xfull.at[here], xsent.at[head], xlanded.at[here],
            (far + head, core),
        )

    def id_copy(peer):
        return remote(ids_ref, slots.at[chip], id_sent.at[peer], id_landed.at[chip], (peer, core))

    def send_ids(step, carry):
        head = lax.rem(here + step, heads)

        @pl.when(step > 0)
        def _():
            id_copy(base + head).start()

        @pl.when(light)
        def _():
            id_copy(far + head).start()

        return carry

    lax.fori_loop(0, heads, send_ids, 0)
    for load in loads:
        load.wait()

    per_core = heads // 2

    def prepare(step, carry):
        head = lax.rem(here + step + 1, heads)
        x_ref[head, :, 0:HD] = normalize(q_ref[:, lanes(head)])[0].astype(kind)
        x_ref[head, :, 2 * HD : 3 * HD] = normalize(k_ref[:, lanes(head)])[0].astype(kind)
        x_ref[head, :, 3 * HD : 4 * HD] = v_ref[:, lanes(head)]

        @pl.when(step == 0)
        def _():
            remote(w_in, w_full.at[other], w_sent, w_landed, (chip, other)).wait_recv()

        w_rows = w_full[head // per_core, lanes(lax.rem(head, per_core)), :]
        x_ref[head, :, HD : 2 * HD] = dot(c_ref[...], w_rows, 1, 1).astype(kind)

        @pl.when(light)
        def _():
            cross_copy(head).start()

        @pl.when(step < heads - 1)
        def _():
            data_copy(head).start()

        @pl.when(step == heads - 1)
        def _():
            full[here] = x_ref[here]

        return carry

    lax.fori_loop(0, heads, prepare, 0)

    def wait_ids(peer):
        remote(ids_ref, slots.at[peer], id_sent.at[0], id_landed.at[peer], (chip, other)).wait_recv()

    def pack_one(peer, rows):
        slot_row = slots[peer]
        down = lax.broadcasted_iota(jnp.int32, (nslots, tokens), 0).astype(jnp.float32)
        hot = jnp.where(down == slot_row[0:1], 1.0, 0.0)
        along = lax.broadcasted_iota(jnp.int32, (tokens, nslots), 1).astype(jnp.float32)
        onehot_t[peer] = jnp.where(along == slot_row.T[:, 0:1], 1.0, 0.0).astype(kind)
        valid = jnp.broadcast_to(jnp.sum(hot, axis=1, keepdims=True), (nslots, HD))
        packed = dot(hot.astype(kind), rows, 1, 0)
        packed = packed.reshape(clusters, cap, packed.shape[1])
        return packed, valid.reshape(clusters, cap, HD)

    def pair_rows(pair):
        return pl.ds(pl.multiple_of(pair * 2 * cap, 2 * cap), 2 * cap)

    def pack_own(step, carry):
        pair = lax.rem(here // 2 + pairs - step, pairs)
        parts, valids = [], []
        for index in range(2):
            source = 2 * pair + index

            @pl.when(source != here)
            def _():
                wait_ids(base + source)
                remote(
                    x_ref.at[0], full.at[source], sent.at[0], landed.at[source], (chip, other)
                ).wait_recv()

            packed, valid = pack_one(base + source, full[source])
            parts.append(packed)
            valids.append(valid)
        both = jnp.concatenate(parts, axis=1).astype(kind)
        rows = pair_rows(pair)
        qk[0, :, rows, :] = both[:, :, 0:HD]
        gv[0, :, rows, 0:HD] = both[:, :, HD : 2 * HD]
        qk[1, :, rows, :] = both[:, :, 2 * HD : 3 * HD]
        gv[1, :, rows, 0:HD] = both[:, :, 3 * HD :]
        gv[1, :, rows, HD:] = jnp.concatenate(valids, axis=1).astype(kind)
        return carry

    def pack_cross(step, carry):
        pair = lax.rem(here // 2 + pairs - step, pairs)
        parts, valids = [], []
        for index in range(2):
            source = 2 * pair + index
            wait_ids(far + source)
            remote(
                x_ref.at[0, :, 0 : 2 * HD], xfull.at[source], xsent.at[0], xlanded.at[source],
                (chip, other),
            ).wait_recv()
            packed, valid = pack_one(far + source, xfull[source])
            parts.append(packed)
            valids.append(valid)
        both = jnp.concatenate(parts, axis=1).astype(kind)
        rows = pair_rows(pair)
        qk[2, :, rows, :] = both[:, :, 0:HD]
        gv[2, :, rows, 0:HD] = both[:, :, HD:]
        gv[2, :, rows, HD:] = jnp.concatenate(valids, axis=1).astype(kind)
        return carry

    size = 2 * rows_of
    down = lax.broadcasted_iota(jnp.int32, (size, size), 0)
    along = lax.broadcasted_iota(jnp.int32, (size, size), 1)
    lane = lax.broadcasted_iota(jnp.int32, (size, HD), 1)
    group = 2

    def one_cluster():
        return down // rows_of == along // rows_of

    def of(ref, index, block, low, high):
        part = ref[index, pl.ds(2 * block, 2), :, low:high]
        return part.reshape(size, high - low)

    def put(ref, block, low, value):
        width = value.shape[1]
        ref[pl.ds(2 * block, 2), :, low : low + width] = value.astype(kind).reshape(
            2, rows_of, width
        )

    def forward(block, qi, ki, vi, allowed):
        scores = dot(of(qk, qi, block, 0, HD), of(qk, ki, block, 0, HD), 1, 1)
        weights = jnp.where(allowed, jnp.exp(scores * inv), 0.0).astype(kind)
        both = dot(weights, of(gv, vi, block, 0, 2 * HD), 1, 0)
        return weights, both[:, :HD], both[:, HD:]

    def diagonal(step, carry):
        allowed = jnp.logical_and(one_cluster(), along <= down)
        found = [forward(step * group + i, 0, 1, 1, allowed) for i in range(group)]
        for i, (weights, top, total) in enumerate(found):
            e_ref[0, step * group + i] = weights
            num[0, step * group + i] = top
            den[0, step * group + i] = total
        return carry

    cross_rows = other
    cross_q, cross_k = 2 * other, 1 + core
    cross_g, cross_v = 2 * other, 1 + core

    def across(step, carry):
        found = []
        for i in range(group):
            block = step * group + i
            weights, top, total = forward(block, cross_q, cross_k, cross_v, one_cluster())
            share = core.astype(jnp.float32)
            found.append((weights, top + num[0, block] * share, total + den[0, block] * share))
        for i, (weights, top, total) in enumerate(found):
            e_ref[1, step * group + i] = weights
            num[cross_rows, step * group + i] = top
            den[cross_rows, step * group + i] = total
        return carry

    def inner(block, rows, grads):
        return jnp.sum(
            of(gv, grads, block, 0, HD).astype(jnp.float32) * num[rows, block],
            axis=1, keepdims=True,
        )

    def settle(block, rows, total, top):
        factor = 1.0 / jnp.where(total > 0, total, 1.0)
        attn = num[rows, block] * factor
        den[rows, block] = jnp.broadcast_to(factor, (size, HD))
        num[rows, block] = jnp.broadcast_to(top * factor * factor, (size, HD))
        return attn

    def settle_own(step, carry):
        tops = [inner(step * group + i, 0, 0) for i in range(group)]
        for i in range(group):
            block = step * group + i
            put(own_out, block, 0, settle(block, 0, den[0, block], tops[i]))
        return carry

    shared_rows = heavy.astype(jnp.int32)
    partner = (far + here, core)

    def st_copy():
        return remote(st_mine, st_got, st_sent, st_landed, partner)

    def measure_rows(block, carry):
        top = inner(block, shared_rows, 2 * shared_rows)
        total = den[shared_rows, block]
        return jnp.where(lane == block, total, jnp.where(lane == blocks + block, top, carry))

    def settle_shared(target):
        def body(step, carry):
            for i in range(group):
                block = step * group + i
                both = st_mine[...] + st_got[...]
                total = jnp.sum(jnp.where(lane == block, both, 0.0), axis=1, keepdims=True)
                top = jnp.sum(jnp.where(lane == blocks + block, both, 0.0), axis=1, keepdims=True)
                put(target, block, 0, settle(block, shared_rows, total, top))
            return carry

        return body

    def backward(block, which, rows, qi, ki, vi, gi):
        weights = e_ref[which, block]
        grads = (of(gv, gi, block, 0, HD).astype(jnp.float32) * den[rows, block]).astype(kind)
        product = dot(grads, of(gv, vi, block, 0, HD), 1, 1)
        delta = num[rows, block]
        slope = (weights.astype(jnp.float32) * (product - delta)).astype(kind)
        return (
            dot(slope, of(qk, ki, block, 0, HD), 1, 0) * inv,
            dot(slope, of(qk, qi, block, 0, HD), 0, 0) * inv,
            dot(weights, grads, 0, 0),
        )

    def back_light(step, carry):
        found = [backward(step * group + i, 0, 0, 0, 1, 1, 0) for i in range(group)]
        for i, grads in enumerate(found):
            for j in range(3):
                put(own_out, step * group + i, (j + 1) * HD, grads[j])
        return carry

    def back_heavy(step, carry):
        found = []
        for i in range(group):
            block = step * group + i
            found.append(
                (
                    backward(block, 0, 0, 0, 1, 1, 0),
                    backward(block, 1, cross_rows, cross_q, cross_k, cross_v, cross_g),
                )
            )
        share = core.astype(jnp.float32)
        for i, (near, away) in enumerate(found):
            block = step * group + i
            put(own_out, block, HD, near[0] + away[0] * share)
            put(own_out, block, 2 * HD, near[1] + away[1] * (1.0 - share))
            put(own_out, block, 3 * HD, near[2] + away[2] * (1.0 - share))

            @pl.when(first)
            def _(away=away, block=block):
                put(cross_out, block, HD, away[0])

            @pl.when(jnp.logical_not(first))
            def _(away=away, block=block):
                put(cross_out, block, 0, away[1])
                put(cross_out, block, HD, away[2])

        return carry

    def unpack(peer, ref, pair, low, high, index):
        both = ref[:, pair_rows(pair), low:high].astype(jnp.float32)
        part = both[:, index * cap : (index + 1) * cap, :].reshape(nslots, high - low)
        return dot(onehot_t[peer], part.astype(kind), 1, 0).astype(kind)

    def a_copy(head):
        return remote(
            stage_a.at[head], got_a.at[here], a_sent.at[head], a_landed.at[here],
            (base + head, core),
        )

    def g_copy(head):
        return remote(
            stage_g.at[head], got_g.at[here], g_sent.at[head], g_landed.at[here],
            (base + head, core),
        )

    def cx_copy(index, head):
        return remote(
            stage_x.at[index, head], got_x.at[index, here], cx_sent.at[index, head],
            cx_landed.at[index, here], (far + head, core),
        )

    def return_own(low, high, stage, got, copy):
        def body(step, carry):
            pair = lax.rem(here // 2 + step + 1, pairs)
            for index in range(2):
                target = 2 * pair + index
                stage[target] = unpack(base + target, own_out, pair, low, high, index)

                @pl.when(target != here)
                def _():
                    copy(target).start()

                @pl.when(target == here)
                def _():
                    got[target] = stage[target]

            return carry

        lax.fori_loop(0, pairs, body, 0)

    def return_cross(part):
        def body(step, carry):
            pair = lax.rem(here // 2 + step, pairs)
            for index in range(2):
                target = 2 * pair + index
                stage_x[part, target] = unpack(
                    far + target, cross_out, pair, part * HD, (part + 1) * HD, index
                )
                cx_copy(part, target).start()
            return carry

        lax.fori_loop(0, pairs, body, 0)

    lax.fori_loop(0, pairs, pack_own, 0)
    lax.fori_loop(0, blocks // group, diagonal, 0)

    @pl.when(heavy)
    def _():
        lax.fori_loop(0, pairs, pack_cross, 0)
        lax.fori_loop(0, blocks // group, across, 0)

    @pl.when(first)
    def _():
        st_mine[...] = lax.fori_loop(0, blocks, measure_rows, jnp.zeros((size, HD), jnp.float32))
        st_copy().start()

    @pl.when(jnp.logical_not(jnp.logical_and(first, light)))
    def _():
        lax.fori_loop(0, blocks // group, settle_own, 0)

    @pl.when(first)
    def _():
        st_copy().wait_recv()

        @pl.when(heavy)
        def _():
            lax.fori_loop(0, blocks // group, settle_shared(cross_out), 0)
            return_cross(0)

        @pl.when(light)
        def _():
            lax.fori_loop(0, blocks // group, settle_shared(own_out), 0)

    return_own(0, HD, stage_a, got_a, a_copy)

    @pl.when(light)
    def _():
        lax.fori_loop(0, blocks // group, back_light, 0)

    @pl.when(heavy)
    def _():
        lax.fori_loop(0, blocks // group, back_heavy, 0)

        @pl.when(jnp.logical_not(first))
        def _():
            return_cross(0)

        return_cross(1)

    return_own(HD, 4 * HD, stage_g, got_g, g_copy)

    piece = w_ref.shape[2]

    def w_swap(peer):
        return remote(
            w_ref.at[peer, other], w_held.at[peer], w_swap_sent.at[peer], w_swap_landed.at[peer],
            (chip, other),
        )

    def x_copy(j):
        return remote(
            x_stage.at[j], x_got.at[j], x_sent.at[j], x_landed.at[j], (chip + 1 - 2 * x, core)
        )

    def y_copy(j):
        return remote(
            y_stage.at[j], y_got.at[j], y_sent.at[j], y_landed.at[j], (chip + 2 - 4 * y, core)
        )

    def z_copy(j):
        return remote(
            z_stage.at[j], z_got.at[z], z_sent.at[j], z_landed.at[z], (4 * j + 2 * y + x, core)
        )

    def wait_cross(part, head):
        remote(
            stage_x.at[part, 0], got_x.at[part, head], cx_sent.at[part, 0],
            cx_landed.at[part, head], (chip, other),
        ).wait_recv()

    def term(step, carry):
        head = lax.rem(here + heads - step, heads)

        @pl.when(head != here)
        def _():
            remote(
                stage_a.at[0], got_a.at[head], a_sent.at[0], a_landed.at[head], (chip, other)
            ).wait_recv()

        @pl.when(jnp.logical_and(first, light))
        def _():
            wait_cross(0, head)
            a_ref[:, lanes(head)] = (
                got_a[head].astype(jnp.float32) + got_x[0, head].astype(jnp.float32)
            ).astype(kind)

        @pl.when(jnp.logical_not(jnp.logical_and(first, light)))
        def _():
            a_ref[:, lanes(head)] = got_a[head]

        total = dot(a_ref[:, lanes(head)], c_ref[...], 0, 0)
        for index in range(4):
            w_ref[2 * head + index // 2, index % 2] = total[
                index * piece : (index + 1) * piece
            ].astype(w_ref.dtype)
        w_swap(2 * head).start()
        w_swap(2 * head + 1).start()
        return carry

    def both_cores(peer):
        w_swap(peer).wait_recv()
        return w_ref[peer, core].astype(jnp.float32) + w_held[peer].astype(jnp.float32)

    def x_phase(j, carry):
        x_stage[j] = both_cores(2 * j + 1 - x).astype(x_stage.dtype)
        x_copy(j).start()
        kept[j] = both_cores(2 * j + x)
        return carry

    def y_phase(j, carry):
        away, stay = 2 * j + 1 - y, 2 * j + y
        x_copy(away).wait_recv()
        y_stage[j] = (kept[away] + x_got[away].astype(jnp.float32)).astype(y_stage.dtype)
        y_copy(j).start()
        x_copy(stay).wait_recv()
        kept[stay] += x_got[stay].astype(jnp.float32)
        return carry

    def z_phase(j, carry):
        y_copy(j).wait_recv()
        total = kept[2 * j + y] + y_got[j].astype(jnp.float32)

        @pl.when(j != z)
        def _():
            z_stage[j] = total.astype(z_stage.dtype)
            z_copy(j).start()

        @pl.when(j == z)
        def _():
            grad_ref[...] = total

        return carry

    def z_sum(j, carry):
        @pl.when(j != z)
        def _():
            remote(
                z_stage.at[j], z_got.at[j], z_sent.at[j], z_landed.at[j], (4 * j + 2 * y + x, core)
            ).wait_recv()
            grad_ref[...] += z_got[j].astype(jnp.float32)
            z_copy(j).wait_send()

        y_copy(j).wait_send()
        return carry

    def ends(j, carry):
        x_copy(j).wait_send()
        w_swap(2 * j).wait_send()
        w_swap(2 * j + 1).wait_send()
        return carry

    lax.fori_loop(0, heads, term, 0)
    lax.fori_loop(0, n // 2, x_phase, 0)

    depth = w_full.shape[1]
    tile = 2 * HD

    def project(step, carry):
        columns = pl.ds(pl.multiple_of(step * tile, tile), tile)
        total = jnp.dot(
            a_ref[:, :depth], w_full[0, :, columns], preferred_element_type=jnp.float32
        ) + jnp.dot(a_ref[:, depth:], w_full[1, :, columns], preferred_element_type=jnp.float32)
        out_ref[:, columns] = total.astype(out_ref.dtype)
        return carry

    lax.fori_loop(0, out_ref.shape[1] // tile, project, 0)
    lax.fori_loop(0, quarter, y_phase, 0)

    def finish(step, carry):
        head = lax.rem(here + heads - step, heads)

        @pl.when(head != here)
        def _():
            remote(
                stage_g.at[0], got_g.at[head], g_sent.at[0], g_landed.at[head], (chip, other)
            ).wait_recv()

        grads = [got_g[head, :, i * HD : (i + 1) * HD].astype(jnp.float32) for i in range(3)]

        @pl.when(light)
        def _():
            wait_cross(1, head)

            @pl.when(jnp.logical_not(first))
            def _():
                wait_cross(0, head)

        extra = [
            jnp.where(light, got_x[i, head].astype(jnp.float32), 0.0) for i in range(2)
        ]
        grads[0] = grads[0] + jnp.where(first, extra[1], 0.0)
        grads[1] = grads[1] + jnp.where(first, 0.0, extra[0])
        grads[2] = grads[2] + jnp.where(first, 0.0, extra[1])
        for gradient, source, target in ((grads[0], q_ref, gq_ref), (grads[1], k_ref, gk_ref)):
            normed, factor = normalize(source[:, lanes(head)])
            mean = jnp.mean(gradient * normed, axis=-1, keepdims=True)
            target[:, lanes(head)] = (factor * (gradient - normed * mean)).astype(target.dtype)
        gv_ref[:, lanes(head)] = grads[2].astype(gv_ref.dtype)
        return carry

    lax.fori_loop(0, quarter, z_phase, 0)
    lax.fori_loop(0, heads, finish, 0)
    lax.fori_loop(0, quarter, z_sum, 0)
    grad_ref[...] = grad_ref[...] * scale
    lax.fori_loop(0, n // 2, ends, 0)

    def sends_done(head, carry):
        @pl.when(head != here)
        def _():
            id_copy(base + head).wait_send()
            data_copy(head).wait_send()
            a_copy(head).wait_send()
            g_copy(head).wait_send()

        @pl.when(light)
        def _():
            id_copy(far + head).wait_send()
            cross_copy(head).wait_send()

        @pl.when(heavy)
        def _():
            cx_copy(0, head).wait_send()
            cx_copy(1, head).wait_send()

        return carry

    lax.fori_loop(0, heads, sends_done, 0)
    w_copy.wait_send()

    @pl.when(first)
    def _():
        st_copy().wait_send()


def layer_call(q, k, v, c, w, labels, clusters, scale):
    tokens, features = q.shape
    heads = features // HD
    n = 2 * heads
    rows = heads * (2 * tokens // clusters)
    blocks = clusters // 2
    kind = q.dtype
    wide = jnp.float32
    vmem = pl.BlockSpec(memory_space=pltpu.VMEM)
    piece = (features // (2 * n), c.shape[1])
    like = jax.ShapeDtypeStruct(q.shape, kind)
    nslots = 2 * tokens
    pair = 2 * rows
    buffers = [
        (q.shape, kind), (q.shape, kind), (q.shape, kind), (c.shape, kind),
        ((2,) + w.shape, kind),
        ((heads, tokens, 4 * HD), kind),
        ((heads, tokens, 4 * HD), kind),
        ((heads, tokens, 2 * HD), kind),
        ((8, tokens), wide),
        ((n, 8, tokens), wide),
        ((n, tokens, nslots), kind),
        ((3, clusters, rows, HD), kind),
        ((3, clusters, rows, 2 * HD), kind),
        ((2, blocks, pair, pair), kind),
        ((2, blocks, pair, HD), wide),
        ((2, blocks, pair, HD), wide),
        ((clusters, rows, 4 * HD), kind),
        ((clusters, rows, 2 * HD), kind),
        ((pair, HD), wide),
        ((pair, HD), wide),
        ((heads, tokens, HD), kind),
        ((heads, tokens, 3 * HD), kind),
        ((2, heads, tokens, HD), kind),
        ((heads, tokens, HD), kind),
        ((heads, tokens, 3 * HD), kind),
        ((2, heads, tokens, HD), kind),
        (q.shape, kind),
        ((n, 2) + piece, kind),
        ((n,) + piece, kind),
        ((n // 2,) + piece, wide),
        ((n // 2,) + piece, kind),
        ((n // 2,) + piece, kind),
    ] + [((n // 4,) + piece, kind)] * 4
    one = pltpu.SemaphoreType.DMA

    def many(*count):
        return pltpu.SemaphoreType.DMA(count)

    semaphores = (
        [many(5), one, one, many(heads), many(heads), many(heads), many(heads), many(n), many(n)]
        + [one, one]
        + [many(heads)] * 4
        + [many(2, heads)] * 2
        + [many(n)] * 2
        + [many(n // 2)] * 2
        + [many(n // 4)] * 4
    )
    return pl.pallas_call(
        functools.partial(layer_kernel, heads, scale),
        out_shape=(
            like, like, like, jax.ShapeDtypeStruct(c.shape, kind),
            jax.ShapeDtypeStruct(piece, wide),
        ),
        in_specs=[pl.BlockSpec(memory_space=pl.ANY)] * 5 + [vmem],
        out_specs=(vmem,) * 5,
        scratch_shapes=[pltpu.VMEM(shape, dtype) for shape, dtype in buffers] + semaphores,
        compiler_params=pltpu.CompilerParams(
            collective_id=0, has_side_effects=True, vmem_limit_bytes=60 << 20
        ),
    )(q, k, v, c, w, labels)


def per_device_heads(queries, key_rows, value_rows, cotangent, w_out, cluster_ids):
    tokens = queries.shape[1]
    seq_devices = lax.axis_size("seq")
    scale = 1.0 / math.sqrt(tokens * seq_devices * 2)
    grad_queries, grad_keys, grad_values, projected, weight_grad = layer_call(
        queries[0], key_rows[0], value_rows[0], cotangent[0], w_out, cluster_ids,
        CL_DEV * seq_devices, scale,
    )
    return (projected[None], grad_queries[None], grad_keys[None], grad_values[None], weight_grad)


def per_device(queries, *rest):
    heads = queries.shape[2] // HD
    if lax.axis_size("dp") == 2 and lax.axis_size("seq") == 2 * heads:
        return per_device_heads(queries, *rest)
    return per_device_slots(queries, *rest)


def solution(mesh):
    in_specs = (
        P("dp", "seq", None),
        P("dp", "seq", None),
        P("dp", "seq", None),
        P("dp", "seq", None),
        P("dp", None),
        P("dp", "seq"),
    )
    out_specs = (
        P("dp", "seq", None),
        P("dp", "seq", None),
        P("dp", "seq", None),
        P("dp", "seq", None),
        P(("seq", "dp"), None),
    )
    return jax.shard_map(
        per_device, mesh=mesh, in_specs=in_specs, out_specs=out_specs, check_vma=False
    )
```

```python
import functools
import math

import jax
import jax.numpy as jnp
from jax import lax
from jax.experimental import pallas as pl
from jax.experimental.pallas import tpu as pltpu
from jax.sharding import PartitionSpec as P

MESH = pl.DeviceIdType.MESH
HD = 128
CL_DEV = 4


EPS = 1e-06


def head_norm(matrix):
    shaped = matrix.astype(jnp.float32).reshape(matrix.shape[0], matrix.shape[1] // HD, HD)
    factor = lax.rsqrt(jnp.mean(shaped * shaped, axis=-1, keepdims=True) + EPS)
    return (shaped * factor, factor)


def norm_back(gradient, normed, factor):
    shaped = gradient.astype(jnp.float32).reshape(normed.shape)
    inner = jnp.mean(shaped * normed, axis=-1, keepdims=True)
    return (factor * (shaped - normed * inner)).reshape(normed.shape[0], -1)


def split_heads(blocks):
    return blocks.reshape(blocks.shape[0], blocks.shape[1], blocks.shape[2] // HD, HD)


def attend(q_blk, k_blk, v_blk, key_valid):
    q_four, k_four, v_four = (split_heads(q_blk), split_heads(k_blk), split_heads(v_blk))
    scores = jnp.einsum(
        "cqhd,ckhd->chqk", q_four, k_four, preferred_element_type=jnp.float32
    ) / math.sqrt(HD)
    positions = jnp.arange(q_blk.shape[1])
    below_diag = positions[None, :] <= positions[:, None]
    on_diagonal = positions[None, :] == positions[:, None]
    allowed = jnp.logical_or(
        jnp.logical_and(key_valid[:, None, None, :], below_diag[None, None]),
        on_diagonal[None, None],
    )
    weights = jnp.where(allowed, jnp.exp(scores), 0.0)
    probs = weights / jnp.sum(weights, axis=-1, keepdims=True)
    probs_b = probs.astype(jnp.bfloat16)
    attn = jnp.einsum(
        "chqk,ckhd->cqhd", probs_b, v_four, preferred_element_type=jnp.float32
    ).astype(jnp.bfloat16)
    return (attn.reshape(q_blk.shape), probs, probs_b)


def attend_back(q_blk, k_blk, v_blk, probs, probs_b, attn, d_blk):
    q_four, k_four, v_four = (split_heads(q_blk), split_heads(k_blk), split_heads(v_blk))
    d_four, a_four = (split_heads(d_blk), split_heads(attn))
    grad_value = jnp.einsum(
        "chqk,cqhd->ckhd", probs_b, d_four, preferred_element_type=jnp.float32
    ).astype(jnp.bfloat16)
    grad_prob = jnp.einsum("cqhd,ckhd->chqk", d_four, v_four, preferred_element_type=jnp.float32)
    delta_row = jnp.sum(d_four.astype(jnp.float32) * a_four.astype(jnp.float32), axis=-1)
    grad_score = (probs * (grad_prob - jnp.transpose(delta_row, (0, 2, 1))[..., None])).astype(
        jnp.bfloat16
    )
    grad_qhat = jnp.einsum(
        "chqk,ckhd->cqhd", grad_score, k_four, preferred_element_type=jnp.float32
    ) / math.sqrt(HD)
    grad_khat = jnp.einsum(
        "chqk,cqhd->ckhd", grad_score, q_four, preferred_element_type=jnp.float32
    ) / math.sqrt(HD)
    shape = q_blk.shape
    return (
        grad_qhat.astype(jnp.bfloat16).reshape(shape),
        grad_khat.astype(jnp.bfloat16).reshape(shape),
        grad_value.reshape(shape),
    )


def per_device_slots(queries, key_rows, value_rows, cotangent, w_out, cluster_ids):
    token_count = queries.shape[1]
    features = queries.shape[2]
    seq_devices = lax.axis_size("seq")
    data_devices = lax.axis_size("dp")
    capacity = 2 * token_count // (CL_DEV * seq_devices)
    total_slots = 2 * token_count
    labels = cluster_ids[0]
    positions = jnp.arange(token_count)
    matching = labels[:, None] == labels[None, :]
    earlier = positions[None, :] < positions[:, None]
    ranks = jnp.sum(jnp.logical_and(matching, earlier), axis=1)
    slot_index = labels * capacity + ranks

    def pack(matrix):
        empty = jnp.zeros((total_slots, matrix.shape[1]), matrix.dtype)
        return (
            empty.at[slot_index].set(matrix).reshape(seq_devices, CL_DEV, capacity, matrix.shape[1])
        )

    def unpack(returned):
        return returned.reshape(total_slots, -1)[slot_index]

    taken_slots = (
        jnp.zeros((total_slots,), jnp.bfloat16)
        .at[slot_index]
        .set(1.0)
        .reshape(seq_devices, CL_DEV, capacity)
    )
    q_norm, q_factor = head_norm(queries[0])
    k_norm, k_factor = head_norm(key_rows[0])
    q_hat = q_norm.reshape(token_count, features).astype(jnp.bfloat16)
    k_hat = k_norm.reshape(token_count, features).astype(jnp.bfloat16)
    cotan = cotangent[0]
    w_full = lax.all_gather(w_out, "dp", axis=0, tiled=True)
    received = (
        lax.all_to_all(pack(q_hat), "seq", split_axis=0, concat_axis=2, tiled=True),
        lax.all_to_all(pack(k_hat), "seq", split_axis=0, concat_axis=2, tiled=True),
        lax.all_to_all(pack(value_rows[0]), "seq", split_axis=0, concat_axis=2, tiled=True),
        lax.all_to_all(taken_slots, "seq", split_axis=0, concat_axis=2, tiled=True),
    )
    q_blk, k_blk, v_blk = (received[0][0], received[1][0], received[2][0])
    key_valid = received[3][0] > 0
    attn_blk, probs, probs_b = attend(q_blk, k_blk, v_blk, key_valid)
    attn_back = lax.all_to_all(attn_blk[None], "seq", split_axis=2, concat_axis=0, tiled=True)
    attn = unpack(attn_back)
    grad_attn = lax.dot_general(
        cotan, w_full, (((1,), (1,)), ((), ())), preferred_element_type=jnp.float32
    ).astype(jnp.bfloat16)
    grad_recv = lax.all_to_all(pack(grad_attn), "seq", split_axis=0, concat_axis=2, tiled=True)
    grad_qblk, grad_kblk, grad_vblk = attend_back(
        q_blk, k_blk, v_blk, probs, probs_b, attn_blk, grad_recv[0]
    )
    grads_back = (
        lax.all_to_all(grad_qblk[None], "seq", split_axis=2, concat_axis=0, tiled=True),
        lax.all_to_all(grad_kblk[None], "seq", split_axis=2, concat_axis=0, tiled=True),
        lax.all_to_all(grad_vblk[None], "seq", split_axis=2, concat_axis=0, tiled=True),
    )
    grad_qhat, grad_khat, grad_values = (
        unpack(grads_back[0]),
        unpack(grads_back[1]),
        unpack(grads_back[2]),
    )
    projected = jnp.dot(attn, w_full, preferred_element_type=jnp.float32).astype(jnp.bfloat16)
    grad_queries = norm_back(grad_qhat, q_norm, q_factor).astype(jnp.bfloat16)
    grad_keys = norm_back(grad_khat, k_norm, k_factor).astype(jnp.bfloat16)
    local_term = lax.dot_general(
        attn, cotan, (((0,), (0,)), ((), ())), preferred_element_type=jnp.float32
    )
    summed = lax.psum_scatter(local_term, ("seq", "dp"), scatter_dimension=0, tiled=True)
    weight_grad = summed / math.sqrt(token_count * seq_devices * data_devices)
    return (projected[None], grad_queries[None], grad_keys[None], grad_values[None], weight_grad)


def remote(source, target, sent, landed, device):
    return pltpu.make_async_remote_copy(
        src_ref=source,
        dst_ref=target,
        send_sem=sent,
        recv_sem=landed,
        device_id=device,
        device_id_type=MESH,
    )


def normalize(rows):
    wide = rows.astype(jnp.float32)
    factor = lax.rsqrt(jnp.mean(wide * wide, axis=-1, keepdims=True) + EPS)
    return wide * factor, factor


def lanes(head):
    return pl.ds(pl.multiple_of(head * HD, HD), HD)


def dot(a, b, ca, cb):
    return lax.dot_general(a, b, (((ca,), (cb,)), ((), ())), preferred_element_type=jnp.float32)


def layer_kernel(
    heads, scale,
    q_in, k_in, v_in, c_in, w_in, labels_ref,
    gq_out, gk_out, gv_out, out_out, grad_out,
    gq_ref, gk_ref, gv_ref, out_ref, grad_ref,
    q_ref, k_ref, v_ref, c_ref, w_full, x_ref, full, xfull, ids_ref, slots,
    onehot_t, allow_ref, qk, gv, e_ref, num, den, own_out, cross_out, st_mine, st_got,
    stage_a, stage_g, stage_x, got_a, got_g, got_x,
    a_ref, w_ref, w_held, kept, x_stage, x_got, y_stage, y_got, z_stage, z_got,
    stored, stored_heads, loaded, w_sent, w_landed, sent, landed, xsent, xlanded, id_sent, id_landed, st_sent, st_landed,
    a_sent, a_landed, g_sent, g_landed, cx_sent, cx_landed,
    w_swap_sent, w_swap_landed, x_sent, x_landed, y_sent, y_landed, z_sent, z_landed,
):
    n = 2 * heads
    quarter = n // 4
    pairs = heads // 2
    chip, core = lax.axis_index("seq"), lax.axis_index("dp")
    other = 1 - core
    side, here = chip // heads, lax.rem(chip, heads)
    base, far = side * heads, (1 - side) * heads
    x, y, z = lax.rem(chip, 2), lax.rem(chip // 2, 2), chip // 4
    heavy = side == core
    light = jnp.logical_not(heavy)
    first = core == 0
    tokens = q_ref.shape[0]
    kind = q_ref.dtype
    clusters = qk.shape[1]
    rows_of = qk.shape[2]
    blocks = clusters // 2
    cap = rows_of // heads
    nslots = clusters * cap
    inv = 1.0 / math.sqrt(HD)
    zl = here // 4
    near_first = zl == core

    def toward(mask_a, mask_b):
        x_bit, y_bit, z_bit = [
            jnp.where(near_first, (mask_a >> b) & 1, (mask_b >> b) & 1) for b in range(3)
        ]
        return lax.rem(zl + z_bit, 2) * 4 + lax.rem(y + y_bit, 2) * 2 + lax.rem(x + x_bit, 2)

    order = tuple(zip((3, 1, 2, 0, 4, 6, 5, 7), (4, 6, 5, 7, 3, 1, 2, 0)))

    ins = ((q_in, q_ref), (k_in, k_ref), (v_in, v_ref), (c_in, c_ref), (w_in, w_full.at[core]))
    loads = [
        pltpu.make_async_copy(source, target, loaded.at[i])
        for i, (source, target) in enumerate(ins)
    ]
    for load in loads:
        load.start()

    barrier = pltpu.get_barrier_semaphore()

    def greet(step, carry):
        pl.semaphore_signal(
            barrier, inc=1, device_id=(lax.rem(chip + step, n), core), device_id_type=MESH
        )
        return carry

    lax.fori_loop(1, n, greet, 0)
    pl.semaphore_signal(barrier, inc=1, device_id=(chip, other), device_id_type=MESH)

    wide = jnp.broadcast_to(labels_ref[...].astype(jnp.float32), (tokens, tokens))
    before = lax.broadcasted_iota(jnp.int32, wide.shape, 0) < lax.broadcasted_iota(
        jnp.int32, wide.shape, 1
    )
    same = jnp.logical_and(wide.T == wide, before)
    rank = jnp.sum(jnp.where(same, 1.0, 0.0), axis=0, keepdims=True)
    ids_ref[...] = jnp.broadcast_to(wide[0:1] * cap + rank, ids_ref.shape)
    slots[chip] = ids_ref[...]

    pl.semaphore_wait(barrier, n)
    w_copy = remote(w_in, w_full.at[core], w_sent, w_landed, (chip, other))
    w_copy.start()

    def data_copy(head):
        return remote(
            x_ref.at[head], full.at[here], sent.at[head], landed.at[here], (base + head, core)
        )

    def cross_copy(head):
        lane = pl.ds(pl.multiple_of(core * 2 * HD, 2 * HD), 2 * HD)
        return remote(
            x_ref.at[head, :, lane], xfull.at[here], xsent.at[head], xlanded.at[here],
            (far + head, core),
        )

    def id_copy(peer):
        return remote(ids_ref, slots.at[chip], id_sent.at[peer], id_landed.at[chip], (peer, core))

    def send_ids(step, carry):
        head = lax.rem(here + step, heads)

        @pl.when(step > 0)
        def _():
            id_copy(base + head).start()

        @pl.when(light)
        def _():
            id_copy(far + head).start()

        return carry

    lax.fori_loop(0, heads, send_ids, 0)
    for load in loads:
        load.wait()

    per_core = heads // 2

    def prepare(head):
        x_ref[head, :, 0:HD] = normalize(q_ref[:, lanes(head)])[0].astype(kind)
        x_ref[head, :, 2 * HD : 3 * HD] = normalize(k_ref[:, lanes(head)])[0].astype(kind)
        x_ref[head, :, 3 * HD : 4 * HD] = v_ref[:, lanes(head)]
        w_rows = w_full[head // per_core, lanes(lax.rem(head, per_core)), :]
        x_ref[head, :, HD : 2 * HD] = dot(c_ref[...], w_rows, 1, 1).astype(kind)

    def send_data(head):
        @pl.when(head != here)
        def _():
            data_copy(head).start()

    for step, masks in enumerate(order):
        head = toward(*masks)
        if step == per_core:
            remote(w_in, w_full.at[other], w_sent, w_landed, (chip, other)).wait_recv()
        prepare(head)

        @pl.when(light)
        def _(head=head):
            cross_copy(head).start()

        @pl.when(heavy)
        def _(head=head):
            send_data(head)

    @pl.when(light)
    def _():
        for masks in order:
            send_data(toward(*masks))

    full[here] = x_ref[here]

    def wait_ids(peer):
        remote(ids_ref, slots.at[peer], id_sent.at[0], id_landed.at[peer], (chip, other)).wait_recv()

    def pack_one(peer, rows):
        slot_row = slots[peer]
        down = lax.broadcasted_iota(jnp.int32, (nslots, tokens), 0).astype(jnp.float32)
        hot = jnp.where(down == slot_row[0:1], 1.0, 0.0)
        along = lax.broadcasted_iota(jnp.int32, (tokens, nslots), 1).astype(jnp.float32)
        onehot_t[peer] = jnp.where(along == slot_row.T[:, 0:1], 1.0, 0.0).astype(kind)
        valid = jnp.broadcast_to(jnp.sum(hot, axis=1, keepdims=True), (nslots, HD))
        packed = dot(hot.astype(kind), rows, 1, 0)
        packed = packed.reshape(clusters, cap, packed.shape[1])
        return packed, valid.reshape(clusters, cap, HD)

    def pair_rows(pair):
        return pl.ds(pl.multiple_of(pair * 2 * cap, 2 * cap), 2 * cap)

    def pair_toward(step):
        z_bit = lax.rem(step // 2 + jnp.where(near_first, 0, 1), 2)
        y_bit = lax.rem(step + jnp.where(near_first, 1, 0) * (1 - step // 2), 2)
        return lax.rem(zl + z_bit, 2) * 2 + lax.rem(y + y_bit, 2)

    def pack_own(step, carry):
        pair = pair_toward(step)
        parts, valids = [], []
        for index in range(2):
            source = 2 * pair + index

            @pl.when(source != here)
            def _():
                wait_ids(base + source)
                remote(
                    x_ref.at[0], full.at[source], sent.at[0], landed.at[source], (chip, other)
                ).wait_recv()

            packed, valid = pack_one(base + source, full[source])
            parts.append(packed)
            valids.append(valid)
        both = jnp.concatenate(parts, axis=1).astype(kind)
        rows = pair_rows(pair)
        qk[0, :, rows, :] = both[:, :, 0:HD]
        gv[0, :, rows, 0:HD] = both[:, :, HD : 2 * HD]
        qk[1, :, rows, :] = both[:, :, 2 * HD : 3 * HD]
        gv[1, :, rows, 0:HD] = both[:, :, 3 * HD :]
        gv[1, :, rows, HD:] = jnp.concatenate(valids, axis=1).astype(kind)
        return carry

    def pack_cross(step, carry):
        pair = pair_toward(step)
        parts, valids = [], []
        for index in range(2):
            source = 2 * pair + index
            wait_ids(far + source)
            remote(
                x_ref.at[0, :, 0 : 2 * HD], xfull.at[source], xsent.at[0], xlanded.at[source],
                (chip, other),
            ).wait_recv()
            packed, valid = pack_one(far + source, xfull[source])
            parts.append(packed)
            valids.append(valid)
        both = jnp.concatenate(parts, axis=1).astype(kind)
        rows = pair_rows(pair)
        qk[2, :, rows, :] = both[:, :, 0:HD]
        gv[2, :, rows, 0:HD] = both[:, :, HD:]
        gv[2, :, rows, HD:] = jnp.concatenate(valids, axis=1).astype(kind)
        return carry

    size = 2 * rows_of
    down = lax.broadcasted_iota(jnp.int32, (size, size), 0)
    along = lax.broadcasted_iota(jnp.int32, (size, size), 1)
    lane = lax.broadcasted_iota(jnp.int32, (size, HD), 1)
    group = 4

    one_cluster = (down < rows_of) == (along < rows_of)
    allow_ref[0] = jnp.where(jnp.logical_and(one_cluster, along <= down), 1.0, 0.0)
    allow_ref[1] = jnp.where(one_cluster, 1.0, 0.0)

    def of(ref, index, block, low, high):
        part = ref[index, pl.ds(2 * block, 2), :, low:high]
        return part.reshape(size, high - low)

    def put(ref, block, low, value):
        width = value.shape[1]
        ref[pl.ds(2 * block, 2), :, low : low + width] = value.astype(kind).reshape(
            2, rows_of, width
        )

    def forward(block, qi, ki, vi, allowed):
        scores = dot(of(qk, qi, block, 0, HD), of(qk, ki, block, 0, HD), 1, 1)
        weights = (jnp.exp(scores * inv) * allow_ref[allowed]).astype(kind)
        both = dot(weights, of(gv, vi, block, 0, 2 * HD), 1, 0)
        return weights, both[:, :HD], both[:, HD:]

    def inner(block, grads, top):
        return jnp.sum(
            of(gv, grads, block, 0, HD).astype(jnp.float32) * top, axis=1, keepdims=True
        )

    def settle(target, block, rows, top, total, product):
        factor = 1.0 / jnp.where(total > 0, total, 1.0)
        den[rows, block] = jnp.broadcast_to(factor, (size, HD))
        num[rows, block] = jnp.broadcast_to(product * (factor * factor), (size, HD))
        put(target, block, 0, top * factor)

    def sums(carry, block, total, product):
        return jnp.where(lane == block, total, jnp.where(lane == blocks + block, product, carry))

    cross_rows = other
    cross_q, cross_k = 2 * other, 1 + core
    cross_g, cross_v = 2 * other, 1 + core
    shared_rows = heavy.astype(jnp.int32)

    def each(step, one):
        return [one(step * group + i) for i in range(group)]

    def diagonal_whole(step, carry):
        def one(block):
            weights, top, total = forward(block, 0, 1, 1, 0)
            return block, weights, top, total, inner(block, 0, top)

        for block, weights, top, total, product in each(step, one):
            e_ref[0, block] = weights
            settle(own_out, block, 0, top, total, product)
        return carry

    def diagonal_part(step, carry):
        def one(block):
            weights, top, total = forward(block, 0, 1, 1, 0)
            return block, weights, top, total, inner(block, 0, top)

        for block, weights, top, total, product in each(step, one):
            e_ref[0, block] = weights
            num[0, block] = top
            den[0, block] = total
            carry = sums(carry, block, total, product)
        return carry

    def across_keys(step, carry):
        def one(block):
            weights, top, total = forward(block, 0, 2, 2, 1)
            top, total = top + num[0, block], total + den[0, block]
            return block, weights, top, total, inner(block, 0, top)

        for block, weights, top, total, product in each(step, one):
            e_ref[1, block] = weights
            settle(own_out, block, 0, top, total, product)
        return carry

    def across_queries(step, carry):
        def one(block):
            weights, top, total = forward(block, 2, 1, 1, 1)
            return block, weights, top, total, inner(block, 2, top)

        for block, weights, top, total, product in each(step, one):
            e_ref[1, block] = weights
            num[1, block] = top
            carry = sums(carry, block, total, product)
        return carry

    def st_copy():
        return remote(st_mine, st_got, st_sent, st_landed, (far + here, core))

    def settle_shared(target):
        def body(step, carry):
            both = st_mine[...] + st_got[...]

            def one(block):
                total = jnp.sum(jnp.where(lane == block, both, 0.0), axis=1, keepdims=True)
                product = jnp.sum(
                    jnp.where(lane == blocks + block, both, 0.0), axis=1, keepdims=True
                )
                return block, num[shared_rows, block], total, product

            for block, top, total, product in each(step, one):
                settle(target, block, shared_rows, top, total, product)
            return carry

        return body

    def backward(block, which, rows, qi, ki, vi, gi):
        weights = e_ref[which, block]
        grads = (of(gv, gi, block, 0, HD).astype(jnp.float32) * den[rows, block]).astype(kind)
        product = dot(grads, of(gv, vi, block, 0, HD), 1, 1)
        delta = num[rows, block]
        slope = (weights.astype(jnp.float32) * (product - delta)).astype(kind)
        return (
            dot(slope, of(qk, ki, block, 0, HD), 1, 0) * inv,
            dot(slope, of(qk, qi, block, 0, HD), 0, 0) * inv,
            dot(weights, grads, 0, 0),
        )

    def back_light(step, carry):
        found = [backward(step * group + i, 0, 0, 0, 1, 1, 0) for i in range(group)]
        for i, grads in enumerate(found):
            for j in range(3):
                put(own_out, step * group + i, (j + 1) * HD, grads[j])
        return carry

    def back_heavy(step, carry):
        found = []
        for i in range(group):
            block = step * group + i
            found.append(
                (
                    backward(block, 0, 0, 0, 1, 1, 0),
                    backward(block, 1, cross_rows, cross_q, cross_k, cross_v, cross_g),
                )
            )
        share = core.astype(jnp.float32)
        for i, (near, away) in enumerate(found):
            block = step * group + i
            put(own_out, block, HD, near[0] + away[0] * share)
            put(own_out, block, 2 * HD, near[1] + away[1] * (1.0 - share))
            put(own_out, block, 3 * HD, near[2] + away[2] * (1.0 - share))

            @pl.when(first)
            def _(away=away, block=block):
                put(cross_out, block, HD, away[0])

            @pl.when(jnp.logical_not(first))
            def _(away=away, block=block):
                put(cross_out, block, 0, away[1])
                put(cross_out, block, HD, away[2])

        return carry

    def unpack(peer, ref, pair, low, high, index):
        both = ref[:, pair_rows(pair), low:high].astype(jnp.float32)
        part = both[:, index * cap : (index + 1) * cap, :].reshape(nslots, high - low)
        return dot(onehot_t[peer], part.astype(kind), 1, 0).astype(kind)

    def a_copy(head):
        return remote(
            stage_a.at[head], got_a.at[here], a_sent.at[head], a_landed.at[here],
            (base + head, core),
        )

    def g_copy(head):
        return remote(
            stage_g.at[head], got_g.at[here], g_sent.at[head], g_landed.at[here],
            (base + head, core),
        )

    def cx_copy(index, head):
        return remote(
            stage_x.at[index, head], got_x.at[index, here], cx_sent.at[index, head],
            cx_landed.at[index, here], (far + head, core),
        )

    def return_own(low, high, stage, got, copy):
        def body(step, carry):
            pair = pair_toward(step)
            for index in range(2):
                target = 2 * pair + index
                stage[target] = unpack(base + target, own_out, pair, low, high, index)

                @pl.when(target != here)
                def _():
                    copy(target).start()

                @pl.when(target == here)
                def _():
                    got[target] = stage[target]

            return carry

        lax.fori_loop(0, pairs, body, 0)

    def return_cross(part):
        def body(step, carry):
            pair = pair_toward(step)
            for index in range(2):
                target = 2 * pair + index
                stage_x[part, target] = unpack(
                    far + target, cross_out, pair, part * HD, (part + 1) * HD, index
                )
                cx_copy(part, target).start()
            return carry

        lax.fori_loop(0, pairs, body, 0)

    rounds = blocks // group
    nothing = jnp.zeros((size, HD), jnp.float32)
    lax.fori_loop(0, pairs, pack_own, 0)

    @pl.when(heavy == first)
    def _():
        lax.fori_loop(0, rounds, diagonal_whole, 0)

    @pl.when(heavy != first)
    def _():
        st_mine[...] = lax.fori_loop(0, rounds, diagonal_part, nothing)

    @pl.when(heavy)
    def _():
        lax.fori_loop(0, pairs, pack_cross, 0)

        @pl.when(jnp.logical_not(first))
        def _():
            lax.fori_loop(0, rounds, across_keys, 0)

        @pl.when(first)
        def _():
            st_mine[...] = lax.fori_loop(0, rounds, across_queries, nothing)

    @pl.when(first)
    def _():
        st_copy().start()
        st_copy().wait_recv()

        @pl.when(heavy)
        def _():
            lax.fori_loop(0, rounds, settle_shared(cross_out), 0)
            return_cross(0)

        @pl.when(light)
        def _():
            lax.fori_loop(0, rounds, settle_shared(own_out), 0)

    return_own(0, HD, stage_a, got_a, a_copy)

    @pl.when(light)
    def _():
        lax.fori_loop(0, blocks // group, back_light, 0)

    @pl.when(heavy)
    def _():
        lax.fori_loop(0, blocks // group, back_heavy, 0)

        @pl.when(jnp.logical_not(first))
        def _():
            return_cross(0)

        return_cross(1)

    return_own(HD, 4 * HD, stage_g, got_g, g_copy)

    piece = w_ref.shape[2]

    def w_swap(peer):
        return remote(
            w_ref.at[peer, other], w_held.at[peer], w_swap_sent.at[peer], w_swap_landed.at[peer],
            (chip, other),
        )

    turn, turn_next = jnp.where(first, x, y), jnp.where(first, y, x)
    step_x, step_y = chip + 1 - 2 * x, chip + 2 - 4 * y

    def piece_of(j, bit):
        return (j // 2) * 4 + jnp.where(
            first, 2 * lax.rem(j, 2) + bit, lax.rem(j, 2) + 2 * bit
        )

    def x_copy(j):
        return remote(
            x_stage.at[j], x_got.at[j], x_sent.at[j], x_landed.at[j],
            (jnp.where(first, step_x, step_y), core),
        )

    def y_copy(j):
        return remote(
            y_stage.at[j], y_got.at[j], y_sent.at[j], y_landed.at[j],
            (jnp.where(first, step_y, step_x), core),
        )

    def z_copy(j):
        return remote(
            z_stage.at[j], z_got.at[z], z_sent.at[j], z_landed.at[z], (4 * j + 2 * y + x, core)
        )

    def wait_cross(part, head):
        remote(
            stage_x.at[part, 0], got_x.at[part, head], cx_sent.at[part, 0],
            cx_landed.at[part, head], (chip, other),
        ).wait_recv()

    def term(step, carry):
        head = lax.rem(here + heads - step, heads)

        @pl.when(head != here)
        def _():
            remote(
                stage_a.at[0], got_a.at[head], a_sent.at[0], a_landed.at[head], (chip, other)
            ).wait_recv()

        @pl.when(jnp.logical_and(first, light))
        def _():
            wait_cross(0, head)
            a_ref[:, lanes(head)] = (
                got_a[head].astype(jnp.float32) + got_x[0, head].astype(jnp.float32)
            ).astype(kind)

        @pl.when(jnp.logical_not(jnp.logical_and(first, light)))
        def _():
            a_ref[:, lanes(head)] = got_a[head]

        total = dot(a_ref[:, lanes(head)], c_ref[...], 0, 0)
        for index in range(4):
            w_ref[2 * head + index // 2, index % 2] = total[
                index * piece : (index + 1) * piece
            ].astype(w_ref.dtype)
        w_swap(2 * head).start()
        w_swap(2 * head + 1).start()
        return carry

    def both_cores(peer):
        w_swap(peer).wait_recv()
        return w_ref[peer, core].astype(jnp.float32) + w_held[peer].astype(jnp.float32)

    def x_phase(j, carry):
        x_stage[j] = both_cores(piece_of(j, 1 - turn)).astype(x_stage.dtype)
        x_copy(j).start()
        kept[j] = both_cores(piece_of(j, turn))
        return carry

    def y_phase(j, carry):
        away, stay = 2 * j + 1 - turn_next, 2 * j + turn_next
        x_copy(away).wait_recv()
        y_stage[j] = (kept[away] + x_got[away].astype(jnp.float32)).astype(y_stage.dtype)
        y_copy(j).start()
        x_copy(stay).wait_recv()
        kept[stay] += x_got[stay].astype(jnp.float32)
        return carry

    def z_phase(j, carry):
        y_copy(j).wait_recv()
        total = kept[2 * j + turn_next] + y_got[j].astype(jnp.float32)

        @pl.when(j != z)
        def _():
            z_stage[j] = total.astype(z_stage.dtype)
            z_copy(j).start()

        @pl.when(j == z)
        def _():
            grad_ref[...] = total

        return carry

    def z_sum(j, carry):
        @pl.when(j != z)
        def _():
            remote(
                z_stage.at[j], z_got.at[j], z_sent.at[j], z_landed.at[j], (4 * j + 2 * y + x, core)
            ).wait_recv()
            grad_ref[...] += z_got[j].astype(jnp.float32)
            z_copy(j).wait_send()

        y_copy(j).wait_send()
        return carry

    def ends(j, carry):
        x_copy(j).wait_send()
        w_swap(2 * j).wait_send()
        w_swap(2 * j + 1).wait_send()
        return carry

    lax.fori_loop(0, heads, term, 0)
    lax.fori_loop(0, n // 2, x_phase, 0)

    depth = w_full.shape[1]
    tile = 2 * HD

    def project(step, carry):
        columns = pl.ds(pl.multiple_of(step * tile, tile), tile)
        total = jnp.dot(
            a_ref[:, :depth], w_full[0, :, columns], preferred_element_type=jnp.float32
        ) + jnp.dot(a_ref[:, depth:], w_full[1, :, columns], preferred_element_type=jnp.float32)
        out_ref[:, columns] = total.astype(out_ref.dtype)
        return carry

    lax.fori_loop(0, out_ref.shape[1] // tile, project, 0)
    keep_out = pltpu.make_async_copy(out_ref, out_out, stored.at[0])
    keep_out.start()
    lax.fori_loop(0, quarter, y_phase, 0)

    results = ((gq_ref, gq_out), (gk_ref, gk_out), (gv_ref, gv_out))

    def keep(index, head):
        source, target = results[index]
        return pltpu.make_async_copy(
            source.at[:, lanes(head)], target.at[:, lanes(head)], stored_heads.at[index, head]
        )

    def finish(step, carry):
        head = lax.rem(here + heads - step, heads)

        @pl.when(head != here)
        def _():
            remote(
                stage_g.at[0], got_g.at[head], g_sent.at[0], g_landed.at[head], (chip, other)
            ).wait_recv()

        grads = [got_g[head, :, i * HD : (i + 1) * HD].astype(jnp.float32) for i in range(3)]

        @pl.when(light)
        def _():
            wait_cross(1, head)

            @pl.when(jnp.logical_not(first))
            def _():
                wait_cross(0, head)

        extra = [
            jnp.where(light, got_x[i, head].astype(jnp.float32), 0.0) for i in range(2)
        ]
        grads[0] = grads[0] + jnp.where(first, extra[1], 0.0)
        grads[1] = grads[1] + jnp.where(first, 0.0, extra[0])
        grads[2] = grads[2] + jnp.where(first, 0.0, extra[1])
        for gradient, source, target in ((grads[0], q_ref, gq_ref), (grads[1], k_ref, gk_ref)):
            normed, factor = normalize(source[:, lanes(head)])
            mean = jnp.mean(gradient * normed, axis=-1, keepdims=True)
            target[:, lanes(head)] = (factor * (gradient - normed * mean)).astype(target.dtype)
        gv_ref[:, lanes(head)] = grads[2].astype(gv_ref.dtype)
        for index in range(3):
            keep(index, head).start()
        return carry

    lax.fori_loop(0, quarter, z_phase, 0)
    lax.fori_loop(0, heads, finish, 0)
    lax.fori_loop(0, quarter, z_sum, 0)
    grad_ref[...] = grad_ref[...] * scale
    keep_grad = pltpu.make_async_copy(grad_ref, grad_out, stored.at[1])
    keep_grad.start()
    lax.fori_loop(0, n // 2, ends, 0)

    def sends_done(head, carry):
        for index in range(3):
            keep(index, head).wait()

        @pl.when(head != here)
        def _():
            id_copy(base + head).wait_send()
            data_copy(head).wait_send()
            a_copy(head).wait_send()
            g_copy(head).wait_send()

        @pl.when(light)
        def _():
            id_copy(far + head).wait_send()
            cross_copy(head).wait_send()

        @pl.when(heavy)
        def _():
            cx_copy(0, head).wait_send()
            cx_copy(1, head).wait_send()

        return carry

    lax.fori_loop(0, heads, sends_done, 0)
    w_copy.wait_send()
    keep_out.wait()
    keep_grad.wait()

    @pl.when(first)
    def _():
        st_copy().wait_send()


def layer_call(q, k, v, c, w, labels, clusters, scale):
    tokens, features = q.shape
    heads = features // HD
    n = 2 * heads
    rows = heads * (2 * tokens // clusters)
    blocks = clusters // 2
    kind = q.dtype
    wide = jnp.float32
    vmem = pl.BlockSpec(memory_space=pltpu.VMEM)
    piece = (features // (2 * n), c.shape[1])
    like = jax.ShapeDtypeStruct(q.shape, kind)
    nslots = 2 * tokens
    pair = 2 * rows
    buffers = [(q.shape, kind)] * 3 + [
        (c.shape, kind), (piece, wide),
        (q.shape, kind), (q.shape, kind), (q.shape, kind), (c.shape, kind),
        ((2,) + w.shape, kind),
        ((heads, tokens, 4 * HD), kind),
        ((heads, tokens, 4 * HD), kind),
        ((heads, tokens, 2 * HD), kind),
        ((8, tokens), wide),
        ((n, 8, tokens), wide),
        ((n, tokens, nslots), kind),
        ((2, pair, pair), wide),
        ((3, clusters, rows, HD), kind),
        ((3, clusters, rows, 2 * HD), kind),
        ((2, blocks, pair, pair), kind),
        ((2, blocks, pair, HD), wide),
        ((2, blocks, pair, HD), wide),
        ((clusters, rows, 4 * HD), kind),
        ((clusters, rows, 2 * HD), kind),
        ((pair, HD), wide),
        ((pair, HD), wide),
        ((heads, tokens, HD), kind),
        ((heads, tokens, 3 * HD), kind),
        ((2, heads, tokens, HD), kind),
        ((heads, tokens, HD), kind),
        ((heads, tokens, 3 * HD), kind),
        ((2, heads, tokens, HD), kind),
        (q.shape, kind),
        ((n, 2) + piece, kind),
        ((n,) + piece, kind),
        ((n // 2,) + piece, wide),
        ((n // 2,) + piece, kind),
        ((n // 2,) + piece, kind),
    ] + [((n // 4,) + piece, kind)] * 4
    one = pltpu.SemaphoreType.DMA

    def many(*count):
        return pltpu.SemaphoreType.DMA(count)

    semaphores = (
        [many(2), many(3, heads), many(5), one, one, many(heads), many(heads), many(heads), many(heads), many(n), many(n)]
        + [one, one]
        + [many(heads)] * 4
        + [many(2, heads)] * 2
        + [many(n)] * 2
        + [many(n // 2)] * 2
        + [many(n // 4)] * 4
    )
    return pl.pallas_call(
        functools.partial(layer_kernel, heads, scale),
        out_shape=(
            like, like, like, jax.ShapeDtypeStruct(c.shape, kind),
            jax.ShapeDtypeStruct(piece, wide),
        ),
        in_specs=[pl.BlockSpec(memory_space=pl.ANY)] * 5 + [vmem],
        out_specs=(pl.BlockSpec(memory_space=pl.ANY),) * 5,
        scratch_shapes=[pltpu.VMEM(shape, dtype) for shape, dtype in buffers] + semaphores,
        compiler_params=pltpu.CompilerParams(
            collective_id=0, has_side_effects=True, vmem_limit_bytes=60 << 20
        ),
    )(q, k, v, c, w, labels)


def hand_over_kernel(count, *refs):
    sources, targets, held = refs[:count], refs[count : 2 * count], refs[2 * count : 3 * count]
    done_in, done_out = refs[3 * count :]
    loads = [pltpu.make_async_copy(sources[i], held[i], done_in.at[i]) for i in range(count)]
    stores = [pltpu.make_async_copy(held[i], targets[i], done_out.at[i]) for i in range(count)]
    for load in loads:
        load.start()
    for load, store in zip(loads, stores):
        load.wait()
        store.start()
    for store in stores:
        store.wait()


def hand_over(*arrays):
    anywhere = pl.BlockSpec(memory_space=pl.ANY)
    count = len(arrays)
    return pl.pallas_call(
        functools.partial(hand_over_kernel, count),
        out_shape=tuple(jax.ShapeDtypeStruct(a.shape, a.dtype) for a in arrays),
        in_specs=[anywhere] * count,
        out_specs=(anywhere,) * count,
        scratch_shapes=[pltpu.VMEM(a.shape, a.dtype) for a in arrays]
        + [pltpu.SemaphoreType.DMA((count,))] * 2,
    )(*arrays)


def per_device_heads(queries, key_rows, value_rows, cotangent, w_out, cluster_ids):
    tokens = queries.shape[1]
    seq_devices = lax.axis_size("seq")
    scale = 1.0 / math.sqrt(tokens * seq_devices * 2)
    grad_queries, grad_keys, grad_values, projected, weight_grad = hand_over(*layer_call(
        queries[0], key_rows[0], value_rows[0], cotangent[0], w_out, cluster_ids,
        CL_DEV * seq_devices, scale,
    ))
    return (projected[None], grad_queries[None], grad_keys[None], grad_values[None], weight_grad)


def per_device(queries, *rest):
    heads = queries.shape[2] // HD
    if lax.axis_size("dp") == 2 and lax.axis_size("seq") == 2 * heads:
        return per_device_heads(queries, *rest)
    return per_device_slots(queries, *rest)


def solution(mesh):
    in_specs = (
        P("dp", "seq", None),
        P("dp", "seq", None),
        P("dp", "seq", None),
        P("dp", "seq", None),
        P("dp", None),
        P("dp", "seq"),
    )
    out_specs = (
        P("dp", "seq", None),
        P("dp", "seq", None),
        P("dp", "seq", None),
        P("dp", "seq", None),
        P(("seq", "dp"), None),
    )
    return jax.shard_map(
        per_device, mesh=mesh, in_specs=in_specs, out_specs=out_specs, check_vma=False
    )
```

```python
import functools
import math

import jax
import jax.numpy as jnp
from jax import lax
from jax.experimental import pallas as pl
from jax.experimental.pallas import tpu as pltpu
from jax.sharding import PartitionSpec as P

MESH = pl.DeviceIdType.MESH
HD = 128
CL_DEV = 4


EPS = 1e-06


def head_norm(matrix):
    shaped = matrix.astype(jnp.float32).reshape(matrix.shape[0], matrix.shape[1] // HD, HD)
    factor = lax.rsqrt(jnp.mean(shaped * shaped, axis=-1, keepdims=True) + EPS)
    return (shaped * factor, factor)


def norm_back(gradient, normed, factor):
    shaped = gradient.astype(jnp.float32).reshape(normed.shape)
    inner = jnp.mean(shaped * normed, axis=-1, keepdims=True)
    return (factor * (shaped - normed * inner)).reshape(normed.shape[0], -1)


def split_heads(blocks):
    return blocks.reshape(blocks.shape[0], blocks.shape[1], blocks.shape[2] // HD, HD)


def attend(q_blk, k_blk, v_blk, key_valid):
    q_four, k_four, v_four = (split_heads(q_blk), split_heads(k_blk), split_heads(v_blk))
    scores = jnp.einsum(
        "cqhd,ckhd->chqk", q_four, k_four, preferred_element_type=jnp.float32
    ) / math.sqrt(HD)
    positions = jnp.arange(q_blk.shape[1])
    below_diag = positions[None, :] <= positions[:, None]
    on_diagonal = positions[None, :] == positions[:, None]
    allowed = jnp.logical_or(
        jnp.logical_and(key_valid[:, None, None, :], below_diag[None, None]),
        on_diagonal[None, None],
    )
    weights = jnp.where(allowed, jnp.exp(scores), 0.0)
    probs = weights / jnp.sum(weights, axis=-1, keepdims=True)
    probs_b = probs.astype(jnp.bfloat16)
    attn = jnp.einsum(
        "chqk,ckhd->cqhd", probs_b, v_four, preferred_element_type=jnp.float32
    ).astype(jnp.bfloat16)
    return (attn.reshape(q_blk.shape), probs, probs_b)


def attend_back(q_blk, k_blk, v_blk, probs, probs_b, attn, d_blk):
    q_four, k_four, v_four = (split_heads(q_blk), split_heads(k_blk), split_heads(v_blk))
    d_four, a_four = (split_heads(d_blk), split_heads(attn))
    grad_value = jnp.einsum(
        "chqk,cqhd->ckhd", probs_b, d_four, preferred_element_type=jnp.float32
    ).astype(jnp.bfloat16)
    grad_prob = jnp.einsum("cqhd,ckhd->chqk", d_four, v_four, preferred_element_type=jnp.float32)
    delta_row = jnp.sum(d_four.astype(jnp.float32) * a_four.astype(jnp.float32), axis=-1)
    grad_score = (probs * (grad_prob - jnp.transpose(delta_row, (0, 2, 1))[..., None])).astype(
        jnp.bfloat16
    )
    grad_qhat = jnp.einsum(
        "chqk,ckhd->cqhd", grad_score, k_four, preferred_element_type=jnp.float32
    ) / math.sqrt(HD)
    grad_khat = jnp.einsum(
        "chqk,cqhd->ckhd", grad_score, q_four, preferred_element_type=jnp.float32
    ) / math.sqrt(HD)
    shape = q_blk.shape
    return (
        grad_qhat.astype(jnp.bfloat16).reshape(shape),
        grad_khat.astype(jnp.bfloat16).reshape(shape),
        grad_value.reshape(shape),
    )


def per_device_slots(queries, key_rows, value_rows, cotangent, w_out, cluster_ids):
    token_count = queries.shape[1]
    features = queries.shape[2]
    seq_devices = lax.axis_size("seq")
    data_devices = lax.axis_size("dp")
    capacity = 2 * token_count // (CL_DEV * seq_devices)
    total_slots = 2 * token_count
    labels = cluster_ids[0]
    positions = jnp.arange(token_count)
    matching = labels[:, None] == labels[None, :]
    earlier = positions[None, :] < positions[:, None]
    ranks = jnp.sum(jnp.logical_and(matching, earlier), axis=1)
    slot_index = labels * capacity + ranks

    def pack(matrix):
        empty = jnp.zeros((total_slots, matrix.shape[1]), matrix.dtype)
        return (
            empty.at[slot_index].set(matrix).reshape(seq_devices, CL_DEV, capacity, matrix.shape[1])
        )

    def unpack(returned):
        return returned.reshape(total_slots, -1)[slot_index]

    taken_slots = (
        jnp.zeros((total_slots,), jnp.bfloat16)
        .at[slot_index]
        .set(1.0)
        .reshape(seq_devices, CL_DEV, capacity)
    )
    q_norm, q_factor = head_norm(queries[0])
    k_norm, k_factor = head_norm(key_rows[0])
    q_hat = q_norm.reshape(token_count, features).astype(jnp.bfloat16)
    k_hat = k_norm.reshape(token_count, features).astype(jnp.bfloat16)
    cotan = cotangent[0]
    w_full = lax.all_gather(w_out, "dp", axis=0, tiled=True)
    received = (
        lax.all_to_all(pack(q_hat), "seq", split_axis=0, concat_axis=2, tiled=True),
        lax.all_to_all(pack(k_hat), "seq", split_axis=0, concat_axis=2, tiled=True),
        lax.all_to_all(pack(value_rows[0]), "seq", split_axis=0, concat_axis=2, tiled=True),
        lax.all_to_all(taken_slots, "seq", split_axis=0, concat_axis=2, tiled=True),
    )
    q_blk, k_blk, v_blk = (received[0][0], received[1][0], received[2][0])
    key_valid = received[3][0] > 0
    attn_blk, probs, probs_b = attend(q_blk, k_blk, v_blk, key_valid)
    attn_back = lax.all_to_all(attn_blk[None], "seq", split_axis=2, concat_axis=0, tiled=True)
    attn = unpack(attn_back)
    grad_attn = lax.dot_general(
        cotan, w_full, (((1,), (1,)), ((), ())), preferred_element_type=jnp.float32
    ).astype(jnp.bfloat16)
    grad_recv = lax.all_to_all(pack(grad_attn), "seq", split_axis=0, concat_axis=2, tiled=True)
    grad_qblk, grad_kblk, grad_vblk = attend_back(
        q_blk, k_blk, v_blk, probs, probs_b, attn_blk, grad_recv[0]
    )
    grads_back = (
        lax.all_to_all(grad_qblk[None], "seq", split_axis=2, concat_axis=0, tiled=True),
        lax.all_to_all(grad_kblk[None], "seq", split_axis=2, concat_axis=0, tiled=True),
        lax.all_to_all(grad_vblk[None], "seq", split_axis=2, concat_axis=0, tiled=True),
    )
    grad_qhat, grad_khat, grad_values = (
        unpack(grads_back[0]),
        unpack(grads_back[1]),
        unpack(grads_back[2]),
    )
    projected = jnp.dot(attn, w_full, preferred_element_type=jnp.float32).astype(jnp.bfloat16)
    grad_queries = norm_back(grad_qhat, q_norm, q_factor).astype(jnp.bfloat16)
    grad_keys = norm_back(grad_khat, k_norm, k_factor).astype(jnp.bfloat16)
    local_term = lax.dot_general(
        attn, cotan, (((0,), (0,)), ((), ())), preferred_element_type=jnp.float32
    )
    summed = lax.psum_scatter(local_term, ("seq", "dp"), scatter_dimension=0, tiled=True)
    weight_grad = summed / math.sqrt(token_count * seq_devices * data_devices)
    return (projected[None], grad_queries[None], grad_keys[None], grad_values[None], weight_grad)


def remote(source, target, sent, landed, device):
    return pltpu.make_async_remote_copy(
        src_ref=source,
        dst_ref=target,
        send_sem=sent,
        recv_sem=landed,
        device_id=device,
        device_id_type=MESH,
    )


def normalize(rows):
    wide = rows.astype(jnp.float32)
    factor = lax.rsqrt(jnp.mean(wide * wide, axis=-1, keepdims=True) + EPS)
    return wide * factor, factor


def lanes(head):
    return pl.ds(pl.multiple_of(head * HD, HD), HD)


def dot(a, b, ca, cb):
    return lax.dot_general(a, b, (((ca,), (cb,)), ((), ())), preferred_element_type=jnp.float32)


def layer_kernel(
    heads, scale,
    q_in, k_in, v_in, c_in, w_in, labels_ref,
    gq_out, gk_out, gv_out, out_out, grad_out,
    gq_ref, gk_ref, gv_ref, out_ref, grad_ref,
    q_ref, k_ref, v_ref, c_ref, w_full, x_ref, full, xfull, ids_ref, slots,
    onehot_t, onehot, allow_ref, qk, gv, e_ref, num, den, own_out, cross_out, st_mine, st_got,
    stage_a, stage_g, stage_x, got_a, got_g, got_x,
    a_ref, w_ref, w_held, kept, x_stage, x_got, y_stage, y_got, z_stage, z_got,
    stored, stored_heads, loaded, w_sent, w_landed, sent, landed, xsent, xlanded, id_sent, id_landed, st_sent, st_landed,
    a_sent, a_landed, g_sent, g_landed, v_sent, v_landed, cx_sent, cx_landed,
    w_swap_sent, w_swap_landed, x_sent, x_landed, y_sent, y_landed, z_sent, z_landed,
):
    n = 2 * heads
    quarter = n // 4
    pairs = heads // 2
    chip, core = lax.axis_index("seq"), lax.axis_index("dp")
    other = 1 - core
    side, here = chip // heads, lax.rem(chip, heads)
    base, far = side * heads, (1 - side) * heads
    x, y, z = lax.rem(chip, 2), lax.rem(chip // 2, 2), chip // 4
    heavy = side == core
    light = jnp.logical_not(heavy)
    first = core == 0
    tokens = q_ref.shape[0]
    kind = q_ref.dtype
    clusters = qk.shape[1]
    rows_of = qk.shape[2]
    blocks = clusters // 2
    cap = rows_of // heads
    nslots = clusters * cap
    inv = 1.0 / math.sqrt(HD)
    zl = here // 4
    near_first = zl == core

    def toward(mask_a, mask_b):
        x_bit, y_bit, z_bit = [
            jnp.where(near_first, (mask_a >> b) & 1, (mask_b >> b) & 1) for b in range(3)
        ]
        return lax.rem(zl + z_bit, 2) * 4 + lax.rem(y + y_bit, 2) * 2 + lax.rem(x + x_bit, 2)

    order = tuple(zip((3, 1, 2, 0, 4, 6, 5, 7), (4, 6, 5, 7, 3, 1, 2, 0)))

    ins = ((q_in, q_ref), (k_in, k_ref), (v_in, v_ref), (c_in, c_ref), (w_in, w_full.at[core]))
    loads = [
        pltpu.make_async_copy(source, target, loaded.at[i])
        for i, (source, target) in enumerate(ins)
    ]
    for load in loads:
        load.start()

    barrier = pltpu.get_barrier_semaphore()

    def greet(step, carry):
        pl.semaphore_signal(
            barrier, inc=1, device_id=(lax.rem(chip + step, n), core), device_id_type=MESH
        )
        return carry

    lax.fori_loop(1, n, greet, 0)
    pl.semaphore_signal(barrier, inc=1, device_id=(chip, other), device_id_type=MESH)

    wide = jnp.broadcast_to(labels_ref[...].astype(jnp.float32), (tokens, tokens))
    before = lax.broadcasted_iota(jnp.int32, wide.shape, 0) < lax.broadcasted_iota(
        jnp.int32, wide.shape, 1
    )
    same = jnp.logical_and(wide.T == wide, before)
    rank = jnp.sum(jnp.where(same, 1.0, 0.0), axis=0, keepdims=True)
    ids_ref[...] = jnp.broadcast_to(wide[0:1] * cap + rank, ids_ref.shape)
    slots[chip] = ids_ref[...]

    pl.semaphore_wait(barrier, n)
    w_copy = remote(w_in, w_full.at[core], w_sent, w_landed, (chip, other))
    w_copy.start()

    def data_copy(wave, head):
        span = pl.ds(2 * wave, 2)
        return remote(
            x_ref.at[head, span], full.at[here, span], sent.at[wave, head],
            landed.at[wave, here], (base + head, core),
        )

    def cross_copy(wave, head):
        return remote(
            x_ref.at[head, 2 * wave + core], xfull.at[here, wave],
            xsent.at[wave, head], xlanded.at[wave, here], (far + head, core),
        )

    def id_copy(peer):
        return remote(ids_ref, slots.at[chip], id_sent.at[peer], id_landed.at[chip], (peer, core))

    def send_ids(step, carry):
        head = lax.rem(here + step, heads)

        @pl.when(step > 0)
        def _():
            id_copy(base + head).start()

        @pl.when(light)
        def _():
            id_copy(far + head).start()

        return carry

    lax.fori_loop(0, heads, send_ids, 0)
    for load in loads:
        load.wait()

    per_core = heads // 2

    def prepare(wave, head):
        if wave == 0:
            x_ref[head, 0] = normalize(q_ref[:, lanes(head)])[0].astype(kind)
            x_ref[head, 1] = normalize(k_ref[:, lanes(head)])[0].astype(kind)
        else:
            w_rows = w_full[head // per_core, lanes(lax.rem(head, per_core)), :]
            x_ref[head, 2] = dot(c_ref[...], w_rows, 1, 1).astype(kind)
            x_ref[head, 3] = v_ref[:, lanes(head)]

    def send_data(wave, head):
        @pl.when(head != here)
        def _():
            data_copy(wave, head).start()

    for wave in range(2):
        if wave == 1:
            remote(w_in, w_full.at[other], w_sent, w_landed, (chip, other)).wait_recv()
        for masks in order:
            head = toward(*masks)
            prepare(wave, head)

            @pl.when(light)
            def _(head=head, wave=wave):
                cross_copy(wave, head).start()

            @pl.when(heavy)
            def _(head=head, wave=wave):
                send_data(wave, head)

        @pl.when(light)
        def _(wave=wave):
            for masks in order:
                send_data(wave, toward(*masks))

    full[here] = x_ref[here]

    def wait_ids(peer):
        remote(ids_ref, slots.at[peer], id_sent.at[0], id_landed.at[peer], (chip, other)).wait_recv()

    def mark(peer):
        slot_row = slots[peer]
        down = lax.broadcasted_iota(jnp.int32, (nslots, tokens), 0).astype(jnp.float32)
        hot = jnp.where(down == slot_row[0:1], 1.0, 0.0)
        along = lax.broadcasted_iota(jnp.int32, (tokens, nslots), 1).astype(jnp.float32)
        onehot_t[peer] = jnp.where(along == slot_row.T[:, 0:1], 1.0, 0.0).astype(kind)
        onehot[peer] = hot.astype(kind)
        valid = jnp.broadcast_to(jnp.sum(hot, axis=1, keepdims=True), (nslots, HD))
        return valid.reshape(clusters, cap, HD)

    def pack_one(peer, rows):
        packed = dot(onehot[peer], rows, 1, 0)
        return packed.reshape(clusters, cap, packed.shape[1])

    def pair_rows(pair):
        return pl.ds(pl.multiple_of(pair * 2 * cap, 2 * cap), 2 * cap)

    def pair_toward(step):
        z_bit = lax.rem(step // 2 + jnp.where(near_first, 0, 1), 2)
        y_bit = lax.rem(step + jnp.where(near_first, 1, 0) * (1 - step // 2), 2)
        return lax.rem(zl + z_bit, 2) * 2 + lax.rem(y + y_bit, 2)

    def pack_own(wave):
        span = pl.ds(2 * wave, 2)

        def body(step, carry):
            pair = pair_toward(step)
            parts, valids = [], []
            for index in range(2):
                source = 2 * pair + index

                @pl.when(source != here)
                def _():
                    if wave == 0:
                        wait_ids(base + source)
                    remote(
                        x_ref.at[0, span], full.at[source, span], sent.at[wave, 0],
                        landed.at[wave, source], (chip, other),
                    ).wait_recv()

                if wave == 0:
                    valids.append(mark(base + source))
                rows = jnp.concatenate(
                    [full[source, 2 * wave], full[source, 2 * wave + 1]], axis=1
                )
                parts.append(pack_one(base + source, rows))
            both = jnp.concatenate(parts, axis=1).astype(kind)
            rows = pair_rows(pair)
            if wave == 0:
                qk[0, :, rows, :] = both[:, :, 0:HD]
                qk[1, :, rows, :] = both[:, :, HD:]
                gv[1, :, rows, HD:] = jnp.concatenate(valids, axis=1).astype(kind)
            else:
                gv[0, :, rows, 0:HD] = both[:, :, 0:HD]
                gv[1, :, rows, 0:HD] = both[:, :, HD:]
            return carry

        lax.fori_loop(0, pairs, body, 0)

    def pack_cross(wave):
        def body(step, carry):
            pair = pair_toward(step)
            parts, valids = [], []
            for index in range(2):
                source = 2 * pair + index
                if wave == 0:
                    wait_ids(far + source)
                remote(
                    x_ref.at[0, wave], xfull.at[source, wave], xsent.at[wave, 0],
                    xlanded.at[wave, source], (chip, other),
                ).wait_recv()
                if wave == 0:
                    valids.append(mark(far + source))
                parts.append(pack_one(far + source, xfull[source, wave]))
            both = jnp.concatenate(parts, axis=1).astype(kind)
            rows = pair_rows(pair)
            if wave == 0:
                qk[2, :, rows, :] = both
                gv[2, :, rows, HD:] = jnp.concatenate(valids, axis=1).astype(kind)
            else:
                gv[2, :, rows, 0:HD] = both
            return carry

        lax.fori_loop(0, pairs, body, 0)

    size = 2 * rows_of
    down = lax.broadcasted_iota(jnp.int32, (size, size), 0)
    along = lax.broadcasted_iota(jnp.int32, (size, size), 1)
    lane = lax.broadcasted_iota(jnp.int32, (size, HD), 1)
    group = 4

    one_cluster = (down < rows_of) == (along < rows_of)
    allow_ref[0] = jnp.where(jnp.logical_and(one_cluster, along <= down), 1.0, 0.0)
    allow_ref[1] = jnp.where(one_cluster, 1.0, 0.0)

    def of(ref, index, block, low, high):
        part = ref[index, pl.ds(2 * block, 2), :, low:high]
        return part.reshape(size, high - low)

    def put(ref, block, low, value):
        width = value.shape[1]
        ref[pl.ds(2 * block, 2), :, low : low + width] = value.astype(kind).reshape(
            2, rows_of, width
        )

    def scores(which, qi, ki):
        def body(step, carry):
            def one(block):
                found = dot(of(qk, qi, block, 0, HD), of(qk, ki, block, 0, HD), 1, 1)
                return block, (jnp.exp(found * inv) * allow_ref[which]).astype(kind)

            for block, weights in each(step, one):
                e_ref[which, block] = weights
            return carry

        lax.fori_loop(0, rounds, body, 0)

    def gather(which, block, vi):
        both = dot(e_ref[which, block], of(gv, vi, block, 0, 2 * HD), 1, 0)
        return both[:, :HD], both[:, HD:]

    def inner(block, grads, top):
        return jnp.sum(
            of(gv, grads, block, 0, HD).astype(jnp.float32) * top, axis=1, keepdims=True
        )

    def settle(target, block, rows, top, total, product):
        factor = 1.0 / jnp.where(total > 0, total, 1.0)
        den[rows, block] = jnp.broadcast_to(factor, (size, HD))
        num[rows, block] = jnp.broadcast_to(product * (factor * factor), (size, HD))
        put(target, block, 0, top * factor)

    def sums(carry, block, total, product):
        return jnp.where(lane == block, total, jnp.where(lane == blocks + block, product, carry))

    shared_rows = heavy.astype(jnp.int32)
    rounds = blocks // group
    nothing = jnp.zeros((size, HD), jnp.float32)

    def each(step, one):
        return [one(step * group + i) for i in range(group)]

    def diagonal_whole(step, carry):
        def one(block):
            top, total = gather(0, block, 1)
            return block, top, total, inner(block, 0, top)

        for block, top, total, product in each(step, one):
            settle(own_out, block, 0, top, total, product)
        return carry

    def diagonal_part(step, carry):
        def one(block):
            top, total = gather(0, block, 1)
            return block, top, total, inner(block, 0, top)

        for block, top, total, product in each(step, one):
            num[0, block] = top
            carry = sums(carry, block, total, product)
        return carry

    def across_keys(step, carry):
        def one(block):
            top, total = gather(0, block, 1)
            top_x, total_x = gather(1, block, 2)
            top, total = top + top_x, total + total_x
            return block, top, total, inner(block, 0, top)

        for block, top, total, product in each(step, one):
            settle(own_out, block, 0, top, total, product)
        return carry

    def across_queries(step, carry):
        def one(block):
            top, total = gather(1, block, 1)
            return block, top, total, inner(block, 2, top)

        for block, top, total, product in each(step, one):
            num[1, block] = top
            carry = sums(carry, block, total, product)
        return carry

    def st_copy():
        return remote(st_mine, st_got, st_sent, st_landed, (far + here, core))

    def settle_shared(target):
        def body(step, carry):
            both = st_mine[...] + st_got[...]

            def one(block):
                total = jnp.sum(jnp.where(lane == block, both, 0.0), axis=1, keepdims=True)
                product = jnp.sum(
                    jnp.where(lane == blocks + block, both, 0.0), axis=1, keepdims=True
                )
                return block, num[shared_rows, block], total, product

            for block, top, total, product in each(step, one):
                settle(target, block, shared_rows, top, total, product)
            return carry

        return body

    def scaled(block, rows, gi):
        return (of(gv, gi, block, 0, HD).astype(jnp.float32) * den[rows, block]).astype(kind)

    def value_light(step, carry):
        for block, found in each(
            step, lambda block: (block, dot(e_ref[0, block], scaled(block, 0, 0), 0, 0))
        ):
            put(own_out, block, 3 * HD, found)
        return carry

    def value_keys(step, carry):
        def one(block):
            grads = scaled(block, 0, 0)
            return block, dot(e_ref[0, block], grads, 0, 0), dot(e_ref[1, block], grads, 0, 0)

        for block, near, away in each(step, one):
            put(own_out, block, 3 * HD, near)
            put(cross_out, block, HD, away)
        return carry

    def value_queries(step, carry):
        def one(block):
            near = dot(e_ref[0, block], scaled(block, 0, 0), 0, 0)
            return block, near + dot(e_ref[1, block], scaled(block, 1, 2), 0, 0)

        for block, found in each(step, one):
            put(own_out, block, 3 * HD, found)
        return carry

    def slopes(block, which, rows, qi, ki, vi, gi):
        product = dot(scaled(block, rows, gi), of(gv, vi, block, 0, HD), 1, 1)
        delta = num[rows, block]
        slope = (e_ref[which, block].astype(jnp.float32) * (product - delta)).astype(kind)
        return (
            dot(slope, of(qk, ki, block, 0, HD), 1, 0) * inv,
            dot(slope, of(qk, qi, block, 0, HD), 0, 0) * inv,
        )

    def slope_light(step, carry):
        def one(block):
            return (block,) + slopes(block, 0, 0, 0, 1, 1, 0)

        for block, grad_q, grad_k in each(step, one):
            put(own_out, block, HD, grad_q)
            put(own_out, block, 2 * HD, grad_k)
        return carry

    def slope_keys(step, carry):
        def one(block):
            return (block,) + slopes(block, 0, 0, 0, 1, 1, 0) + slopes(block, 1, 0, 0, 2, 2, 0)

        for block, grad_q, grad_k, cross_q, cross_k in each(step, one):
            put(own_out, block, HD, grad_q + cross_q)
            put(own_out, block, 2 * HD, grad_k)
            put(cross_out, block, 0, cross_k)
        return carry

    def slope_queries(step, carry):
        def one(block):
            return (block,) + slopes(block, 0, 0, 0, 1, 1, 0) + slopes(block, 1, 1, 2, 1, 1, 2)

        for block, grad_q, grad_k, cross_q, cross_k in each(step, one):
            put(own_out, block, HD, grad_q)
            put(own_out, block, 2 * HD, grad_k + cross_k)
            put(cross_out, block, HD, cross_q)
        return carry

    def by_role(for_light, for_queries, for_keys):
        @pl.when(light)
        def _():
            lax.fori_loop(0, rounds, for_light, 0)

        @pl.when(jnp.logical_and(heavy, first))
        def _():
            lax.fori_loop(0, rounds, for_queries, 0)

        @pl.when(jnp.logical_and(heavy, jnp.logical_not(first)))
        def _():
            lax.fori_loop(0, rounds, for_keys, 0)

    def unpack(peer, ref, pair, low, high, index):
        both = ref[:, pair_rows(pair), low:high].astype(jnp.float32)
        part = both[:, index * cap : (index + 1) * cap, :].reshape(nslots, high - low)
        return dot(onehot_t[peer], part.astype(kind), 1, 0).astype(kind)

    def a_copy(head):
        return remote(
            stage_a.at[head, 0], got_a.at[here, 0], a_sent.at[head], a_landed.at[here],
            (base + head, core),
        )

    def g_copy(head):
        return remote(
            stage_g.at[head, pl.ds(0, 2)], got_g.at[here, pl.ds(0, 2)], g_sent.at[head],
            g_landed.at[here], (base + head, core),
        )

    def v_copy(head):
        return remote(
            stage_g.at[head, 2], got_g.at[here, 2], v_sent.at[head], v_landed.at[here], (base + head, core),
        )

    def cx_copy(index, head):
        return remote(
            stage_x.at[index, head], got_x.at[index, here], cx_sent.at[index, head],
            cx_landed.at[index, here], (far + head, core),
        )

    def return_own(low, high, stage, got, at, copy):
        def body(step, carry):
            pair = pair_toward(step)
            for index in range(2):
                target = 2 * pair + index
                found = unpack(base + target, own_out, pair, low, high, index)
                for part in range((high - low) // HD):
                    stage[target, at + part] = found[:, part * HD : (part + 1) * HD]

                @pl.when(target != here)
                def _():
                    copy(target).start()

                @pl.when(target == here)
                def _():
                    for part in range((high - low) // HD):
                        got[target, at + part] = stage[target, at + part]

            return carry

        lax.fori_loop(0, pairs, body, 0)

    def return_cross(part):
        def body(step, carry):
            pair = pair_toward(step)
            for index in range(2):
                target = 2 * pair + index
                stage_x[part, target] = unpack(
                    far + target, cross_out, pair, part * HD, (part + 1) * HD, index
                )
                cx_copy(part, target).start()
            return carry

        lax.fori_loop(0, pairs, body, 0)

    pack_own(0)
    scores(0, 0, 1)

    @pl.when(heavy)
    def _():
        pack_cross(0)
        scores(1, 2 * other, 1 + core)

    @pl.when(heavy)
    def _():
        pack_cross(1)

    pack_own(1)

    @pl.when(first)
    def _():
        @pl.when(heavy)
        def _():
            st_mine[...] = lax.fori_loop(0, rounds, across_queries, nothing)
            st_copy().start()
            lax.fori_loop(0, rounds, diagonal_whole, 0)
            return_own(0, HD, stage_a, got_a, 0, a_copy)
            st_copy().wait_recv()
            lax.fori_loop(0, rounds, settle_shared(cross_out), 0)
            return_cross(0)

        @pl.when(light)
        def _():
            st_mine[...] = lax.fori_loop(0, rounds, diagonal_part, nothing)
            st_copy().start()
            st_copy().wait_recv()
            lax.fori_loop(0, rounds, settle_shared(own_out), 0)

    @pl.when(jnp.logical_not(first))
    def _():
        @pl.when(heavy)
        def _():
            lax.fori_loop(0, rounds, across_keys, 0)

        @pl.when(light)
        def _():
            lax.fori_loop(0, rounds, diagonal_whole, 0)

    @pl.when(jnp.logical_not(jnp.logical_and(first, heavy)))
    def _():
        return_own(0, HD, stage_a, got_a, 0, a_copy)

    by_role(value_light, value_queries, value_keys)

    @pl.when(jnp.logical_and(heavy, jnp.logical_not(first)))
    def _():
        return_cross(1)

    return_own(3 * HD, 4 * HD, stage_g, got_g, 2, v_copy)

    piece = w_ref.shape[2]

    def w_swap(peer):
        return remote(
            w_ref.at[peer, other], w_held.at[peer], w_swap_sent.at[peer], w_swap_landed.at[peer],
            (chip, other),
        )

    turn, turn_next = jnp.where(first, x, y), jnp.where(first, y, x)
    step_x, step_y = chip + 1 - 2 * x, chip + 2 - 4 * y

    def piece_of(j, bit):
        return (j // 2) * 4 + jnp.where(
            first, 2 * lax.rem(j, 2) + bit, lax.rem(j, 2) + 2 * bit
        )

    def x_copy(j):
        return remote(
            x_stage.at[j], x_got.at[j], x_sent.at[j], x_landed.at[j],
            (jnp.where(first, step_x, step_y), core),
        )

    def y_copy(j):
        return remote(
            y_stage.at[j], y_got.at[j], y_sent.at[j], y_landed.at[j],
            (jnp.where(first, step_y, step_x), core),
        )

    def z_copy(j):
        return remote(
            z_stage.at[j], z_got.at[z], z_sent.at[j], z_landed.at[z], (4 * j + 2 * y + x, core)
        )

    def wait_cross(part, head):
        remote(
            stage_x.at[part, 0], got_x.at[part, head], cx_sent.at[part, 0],
            cx_landed.at[part, head], (chip, other),
        ).wait_recv()

    def term(step, carry):
        head = lax.rem(here + heads - step, heads)

        @pl.when(head != here)
        def _():
            remote(
                stage_a.at[0, 0], got_a.at[head, 0], a_sent.at[0], a_landed.at[head], (chip, other)
            ).wait_recv()

        @pl.when(jnp.logical_and(first, light))
        def _():
            wait_cross(0, head)
            a_ref[:, lanes(head)] = (
                got_a[head, 0].astype(jnp.float32) + got_x[0, head].astype(jnp.float32)
            ).astype(kind)

        @pl.when(jnp.logical_not(jnp.logical_and(first, light)))
        def _():
            a_ref[:, lanes(head)] = got_a[head, 0]

        total = dot(a_ref[:, lanes(head)], c_ref[...], 0, 0)
        for index in range(4):
            w_ref[2 * head + index // 2, index % 2] = total[
                index * piece : (index + 1) * piece
            ].astype(w_ref.dtype)
        w_swap(2 * head).start()
        w_swap(2 * head + 1).start()
        return carry

    def both_cores(peer):
        w_swap(peer).wait_recv()
        return w_ref[peer, core].astype(jnp.float32) + w_held[peer].astype(jnp.float32)

    def x_phase(j, carry):
        x_stage[j] = both_cores(piece_of(j, 1 - turn)).astype(x_stage.dtype)
        x_copy(j).start()
        kept[j] = both_cores(piece_of(j, turn))
        return carry

    def y_phase(j, carry):
        away, stay = 2 * j + 1 - turn_next, 2 * j + turn_next
        x_copy(away).wait_recv()
        y_stage[j] = (kept[away] + x_got[away].astype(jnp.float32)).astype(y_stage.dtype)
        y_copy(j).start()
        x_copy(stay).wait_recv()
        kept[stay] += x_got[stay].astype(jnp.float32)
        return carry

    def z_phase(j, carry):
        y_copy(j).wait_recv()
        total = kept[2 * j + turn_next] + y_got[j].astype(jnp.float32)

        @pl.when(j != z)
        def _():
            z_stage[j] = total.astype(z_stage.dtype)
            z_copy(j).start()

        @pl.when(j == z)
        def _():
            grad_ref[...] = total

        return carry

    def z_sum(j, carry):
        @pl.when(j != z)
        def _():
            remote(
                z_stage.at[j], z_got.at[j], z_sent.at[j], z_landed.at[j], (4 * j + 2 * y + x, core)
            ).wait_recv()
            grad_ref[...] += z_got[j].astype(jnp.float32)
            z_copy(j).wait_send()

        y_copy(j).wait_send()
        return carry

    def ends(j, carry):
        x_copy(j).wait_send()
        w_swap(2 * j).wait_send()
        w_swap(2 * j + 1).wait_send()
        return carry

    lax.fori_loop(0, heads, term, 0)
    lax.fori_loop(0, n // 2, x_phase, 0)
    by_role(slope_light, slope_queries, slope_keys)

    @pl.when(jnp.logical_and(heavy, first))
    def _():
        return_cross(1)

    @pl.when(jnp.logical_and(heavy, jnp.logical_not(first)))
    def _():
        return_cross(0)

    return_own(HD, 3 * HD, stage_g, got_g, 0, g_copy)
    lax.fori_loop(0, quarter, y_phase, 0)
    lax.fori_loop(0, quarter, z_phase, 0)

    depth = w_full.shape[1]
    tile = 2 * HD

    def project(step, carry):
        columns = pl.ds(pl.multiple_of(step * tile, tile), tile)
        total = jnp.dot(
            a_ref[:, :depth], w_full[0, :, columns], preferred_element_type=jnp.float32
        ) + jnp.dot(a_ref[:, depth:], w_full[1, :, columns], preferred_element_type=jnp.float32)
        out_ref[:, columns] = total.astype(out_ref.dtype)
        return carry

    lax.fori_loop(0, out_ref.shape[1] // tile, project, 0)
    keep_out = pltpu.make_async_copy(out_ref, out_out, stored.at[0])
    keep_out.start()

    results = ((gq_ref, gq_out), (gk_ref, gk_out), (gv_ref, gv_out))

    def keep(index, head):
        source, target = results[index]
        return pltpu.make_async_copy(
            source.at[:, lanes(head)], target.at[:, lanes(head)], stored_heads.at[index, head]
        )

    def finish(step, carry):
        head = lax.rem(here + heads - step, heads)

        @pl.when(head != here)
        def _():
            for span, gone, come in (
                (pl.ds(2, 1), v_sent, v_landed), (pl.ds(0, 2), g_sent, g_landed)
            ):
                remote(
                    stage_g.at[0, span], got_g.at[head, span], gone.at[0], come.at[head],
                    (chip, other),
                ).wait_recv()

        grads = [got_g[head, i].astype(jnp.float32) for i in range(3)]

        @pl.when(light)
        def _():
            wait_cross(1, head)

            @pl.when(jnp.logical_not(first))
            def _():
                wait_cross(0, head)

        extra = [
            jnp.where(light, got_x[i, head].astype(jnp.float32), 0.0) for i in range(2)
        ]
        grads[0] = grads[0] + jnp.where(first, extra[1], 0.0)
        grads[1] = grads[1] + jnp.where(first, 0.0, extra[0])
        grads[2] = grads[2] + jnp.where(first, 0.0, extra[1])
        for gradient, source, target in ((grads[0], q_ref, gq_ref), (grads[1], k_ref, gk_ref)):
            normed, factor = normalize(source[:, lanes(head)])
            mean = jnp.mean(gradient * normed, axis=-1, keepdims=True)
            target[:, lanes(head)] = (factor * (gradient - normed * mean)).astype(target.dtype)
        gv_ref[:, lanes(head)] = grads[2].astype(gv_ref.dtype)
        for index in range(3):
            keep(index, head).start()
        return carry

    lax.fori_loop(0, heads, finish, 0)
    lax.fori_loop(0, quarter, z_sum, 0)
    grad_ref[...] = grad_ref[...] * scale
    keep_grad = pltpu.make_async_copy(grad_ref, grad_out, stored.at[1])
    keep_grad.start()
    lax.fori_loop(0, n // 2, ends, 0)

    def sends_done(head, carry):
        for index in range(3):
            keep(index, head).wait()

        @pl.when(head != here)
        def _():
            id_copy(base + head).wait_send()
            data_copy(0, head).wait_send()
            data_copy(1, head).wait_send()
            a_copy(head).wait_send()
            g_copy(head).wait_send()
            v_copy(head).wait_send()

        @pl.when(light)
        def _():
            id_copy(far + head).wait_send()
            cross_copy(0, head).wait_send()
            cross_copy(1, head).wait_send()

        @pl.when(heavy)
        def _():
            cx_copy(0, head).wait_send()
            cx_copy(1, head).wait_send()

        return carry

    lax.fori_loop(0, heads, sends_done, 0)
    w_copy.wait_send()
    keep_out.wait()
    keep_grad.wait()

    @pl.when(first)
    def _():
        st_copy().wait_send()


def layer_call(q, k, v, c, w, labels, clusters, scale):
    tokens, features = q.shape
    heads = features // HD
    n = 2 * heads
    rows = heads * (2 * tokens // clusters)
    blocks = clusters // 2
    kind = q.dtype
    wide = jnp.float32
    vmem = pl.BlockSpec(memory_space=pltpu.VMEM)
    piece = (features // (2 * n), c.shape[1])
    like = jax.ShapeDtypeStruct(q.shape, kind)
    nslots = 2 * tokens
    pair = 2 * rows
    buffers = [(q.shape, kind)] * 3 + [
        (c.shape, kind), (piece, wide),
        (q.shape, kind), (q.shape, kind), (q.shape, kind), (c.shape, kind),
        ((2,) + w.shape, kind),
        ((heads, 4, tokens, HD), kind),
        ((heads, 4, tokens, HD), kind),
        ((heads, 2, tokens, HD), kind),
        ((8, tokens), wide),
        ((n, 8, tokens), wide),
        ((n, tokens, nslots), kind),
        ((n, nslots, tokens), kind),
        ((2, pair, pair), wide),
        ((3, clusters, rows, HD), kind),
        ((3, clusters, rows, 2 * HD), kind),
        ((2, blocks, pair, pair), kind),
        ((2, blocks, pair, HD), wide),
        ((2, blocks, pair, HD), wide),
        ((clusters, rows, 4 * HD), kind),
        ((clusters, rows, 2 * HD), kind),
        ((pair, HD), wide),
        ((pair, HD), wide),
        ((heads, 1, tokens, HD), kind),
        ((heads, 3, tokens, HD), kind),
        ((2, heads, tokens, HD), kind),
        ((heads, 1, tokens, HD), kind),
        ((heads, 3, tokens, HD), kind),
        ((2, heads, tokens, HD), kind),
        (q.shape, kind),
        ((n, 2) + piece, kind),
        ((n,) + piece, kind),
        ((n // 2,) + piece, wide),
        ((n // 2,) + piece, kind),
        ((n // 2,) + piece, kind),
    ] + [((n // 4,) + piece, kind)] * 4
    one = pltpu.SemaphoreType.DMA

    def many(*count):
        return pltpu.SemaphoreType.DMA(count)

    semaphores = (
        [many(2), many(3, heads), many(5), one, one] + [many(2, heads)] * 4 + [many(n)] * 2
        + [one, one]
        + [many(heads)] * 6
        + [many(2, heads)] * 2
        + [many(n)] * 2
        + [many(n // 2)] * 2
        + [many(n // 4)] * 4
    )
    return pl.pallas_call(
        functools.partial(layer_kernel, heads, scale),
        out_shape=(
            like, like, like, jax.ShapeDtypeStruct(c.shape, kind),
            jax.ShapeDtypeStruct(piece, wide),
        ),
        in_specs=[pl.BlockSpec(memory_space=pl.ANY)] * 5 + [vmem],
        out_specs=(pl.BlockSpec(memory_space=pl.ANY),) * 5,
        scratch_shapes=[pltpu.VMEM(shape, dtype) for shape, dtype in buffers] + semaphores,
        compiler_params=pltpu.CompilerParams(
            collective_id=0, has_side_effects=True, vmem_limit_bytes=60 << 20
        ),
    )(q, k, v, c, w, labels)


def hand_over_kernel(count, *refs):
    sources, targets, held = refs[:count], refs[count : 2 * count], refs[2 * count : 3 * count]
    done_in, done_out = refs[3 * count :]
    loads = [pltpu.make_async_copy(sources[i], held[i], done_in.at[i]) for i in range(count)]
    stores = [pltpu.make_async_copy(held[i], targets[i], done_out.at[i]) for i in range(count)]
    for load in loads:
        load.start()
    for load, store in zip(loads, stores):
        load.wait()
        store.start()
    for store in stores:
        store.wait()


def hand_over(*arrays):
    anywhere = pl.BlockSpec(memory_space=pl.ANY)
    count = len(arrays)
    return pl.pallas_call(
        functools.partial(hand_over_kernel, count),
        out_shape=tuple(jax.ShapeDtypeStruct(a.shape, a.dtype) for a in arrays),
        in_specs=[anywhere] * count,
        out_specs=(anywhere,) * count,
        scratch_shapes=[pltpu.VMEM(a.shape, a.dtype) for a in arrays]
        + [pltpu.SemaphoreType.DMA((count,))] * 2,
    )(*arrays)


def per_device_heads(queries, key_rows, value_rows, cotangent, w_out, cluster_ids):
    tokens = queries.shape[1]
    seq_devices = lax.axis_size("seq")
    scale = 1.0 / math.sqrt(tokens * seq_devices * 2)
    grad_queries, grad_keys, grad_values, projected, weight_grad = hand_over(*layer_call(
        queries[0], key_rows[0], value_rows[0], cotangent[0], w_out, cluster_ids,
        CL_DEV * seq_devices, scale,
    ))
    return (projected[None], grad_queries[None], grad_keys[None], grad_values[None], weight_grad)


def per_device(queries, *rest):
    heads = queries.shape[2] // HD
    if lax.axis_size("dp") == 2 and lax.axis_size("seq") == 2 * heads:
        return per_device_heads(queries, *rest)
    return per_device_slots(queries, *rest)


def solution(mesh):
    in_specs = (
        P("dp", "seq", None),
        P("dp", "seq", None),
        P("dp", "seq", None),
        P("dp", "seq", None),
        P("dp", None),
        P("dp", "seq"),
    )
    out_specs = (
        P("dp", "seq", None),
        P("dp", "seq", None),
        P("dp", "seq", None),
        P("dp", "seq", None),
        P(("seq", "dp"), None),
    )
    return jax.shard_map(
        per_device, mesh=mesh, in_specs=in_specs, out_specs=out_specs, check_vma=False
    )
```

```python
import functools
import math

import jax
import jax.numpy as jnp
from jax import lax
from jax.experimental import pallas as pl
from jax.experimental.pallas import tpu as pltpu
from jax.sharding import PartitionSpec as P

MESH = pl.DeviceIdType.MESH
HD = 128
CL_DEV = 4


EPS = 1e-06


def head_norm(matrix):
    shaped = matrix.astype(jnp.float32).reshape(matrix.shape[0], matrix.shape[1] // HD, HD)
    factor = lax.rsqrt(jnp.mean(shaped * shaped, axis=-1, keepdims=True) + EPS)
    return (shaped * factor, factor)


def norm_back(gradient, normed, factor):
    shaped = gradient.astype(jnp.float32).reshape(normed.shape)
    inner = jnp.mean(shaped * normed, axis=-1, keepdims=True)
    return (factor * (shaped - normed * inner)).reshape(normed.shape[0], -1)


def split_heads(blocks):
    return blocks.reshape(blocks.shape[0], blocks.shape[1], blocks.shape[2] // HD, HD)


def attend(q_blk, k_blk, v_blk, key_valid):
    q_four, k_four, v_four = (split_heads(q_blk), split_heads(k_blk), split_heads(v_blk))
    scores = jnp.einsum(
        "cqhd,ckhd->chqk", q_four, k_four, preferred_element_type=jnp.float32
    ) / math.sqrt(HD)
    positions = jnp.arange(q_blk.shape[1])
    below_diag = positions[None, :] <= positions[:, None]
    on_diagonal = positions[None, :] == positions[:, None]
    allowed = jnp.logical_or(
        jnp.logical_and(key_valid[:, None, None, :], below_diag[None, None]),
        on_diagonal[None, None],
    )
    weights = jnp.where(allowed, jnp.exp(scores), 0.0)
    probs = weights / jnp.sum(weights, axis=-1, keepdims=True)
    probs_b = probs.astype(jnp.bfloat16)
    attn = jnp.einsum(
        "chqk,ckhd->cqhd", probs_b, v_four, preferred_element_type=jnp.float32
    ).astype(jnp.bfloat16)
    return (attn.reshape(q_blk.shape), probs, probs_b)


def attend_back(q_blk, k_blk, v_blk, probs, probs_b, attn, d_blk):
    q_four, k_four, v_four = (split_heads(q_blk), split_heads(k_blk), split_heads(v_blk))
    d_four, a_four = (split_heads(d_blk), split_heads(attn))
    grad_value = jnp.einsum(
        "chqk,cqhd->ckhd", probs_b, d_four, preferred_element_type=jnp.float32
    ).astype(jnp.bfloat16)
    grad_prob = jnp.einsum("cqhd,ckhd->chqk", d_four, v_four, preferred_element_type=jnp.float32)
    delta_row = jnp.sum(d_four.astype(jnp.float32) * a_four.astype(jnp.float32), axis=-1)
    grad_score = (probs * (grad_prob - jnp.transpose(delta_row, (0, 2, 1))[..., None])).astype(
        jnp.bfloat16
    )
    grad_qhat = jnp.einsum(
        "chqk,ckhd->cqhd", grad_score, k_four, preferred_element_type=jnp.float32
    ) / math.sqrt(HD)
    grad_khat = jnp.einsum(
        "chqk,cqhd->ckhd", grad_score, q_four, preferred_element_type=jnp.float32
    ) / math.sqrt(HD)
    shape = q_blk.shape
    return (
        grad_qhat.astype(jnp.bfloat16).reshape(shape),
        grad_khat.astype(jnp.bfloat16).reshape(shape),
        grad_value.reshape(shape),
    )


def per_device_slots(queries, key_rows, value_rows, cotangent, w_out, cluster_ids):
    token_count = queries.shape[1]
    features = queries.shape[2]
    seq_devices = lax.axis_size("seq")
    data_devices = lax.axis_size("dp")
    capacity = 2 * token_count // (CL_DEV * seq_devices)
    total_slots = 2 * token_count
    labels = cluster_ids[0]
    positions = jnp.arange(token_count)
    matching = labels[:, None] == labels[None, :]
    earlier = positions[None, :] < positions[:, None]
    ranks = jnp.sum(jnp.logical_and(matching, earlier), axis=1)
    slot_index = labels * capacity + ranks

    def pack(matrix):
        empty = jnp.zeros((total_slots, matrix.shape[1]), matrix.dtype)
        return (
            empty.at[slot_index].set(matrix).reshape(seq_devices, CL_DEV, capacity, matrix.shape[1])
        )

    def unpack(returned):
        return returned.reshape(total_slots, -1)[slot_index]

    taken_slots = (
        jnp.zeros((total_slots,), jnp.bfloat16)
        .at[slot_index]
        .set(1.0)
        .reshape(seq_devices, CL_DEV, capacity)
    )
    q_norm, q_factor = head_norm(queries[0])
    k_norm, k_factor = head_norm(key_rows[0])
    q_hat = q_norm.reshape(token_count, features).astype(jnp.bfloat16)
    k_hat = k_norm.reshape(token_count, features).astype(jnp.bfloat16)
    cotan = cotangent[0]
    w_full = lax.all_gather(w_out, "dp", axis=0, tiled=True)
    received = (
        lax.all_to_all(pack(q_hat), "seq", split_axis=0, concat_axis=2, tiled=True),
        lax.all_to_all(pack(k_hat), "seq", split_axis=0, concat_axis=2, tiled=True),
        lax.all_to_all(pack(value_rows[0]), "seq", split_axis=0, concat_axis=2, tiled=True),
        lax.all_to_all(taken_slots, "seq", split_axis=0, concat_axis=2, tiled=True),
    )
    q_blk, k_blk, v_blk = (received[0][0], received[1][0], received[2][0])
    key_valid = received[3][0] > 0
    attn_blk, probs, probs_b = attend(q_blk, k_blk, v_blk, key_valid)
    attn_back = lax.all_to_all(attn_blk[None], "seq", split_axis=2, concat_axis=0, tiled=True)
    attn = unpack(attn_back)
    grad_attn = lax.dot_general(
        cotan, w_full, (((1,), (1,)), ((), ())), preferred_element_type=jnp.float32
    ).astype(jnp.bfloat16)
    grad_recv = lax.all_to_all(pack(grad_attn), "seq", split_axis=0, concat_axis=2, tiled=True)
    grad_qblk, grad_kblk, grad_vblk = attend_back(
        q_blk, k_blk, v_blk, probs, probs_b, attn_blk, grad_recv[0]
    )
    grads_back = (
        lax.all_to_all(grad_qblk[None], "seq", split_axis=2, concat_axis=0, tiled=True),
        lax.all_to_all(grad_kblk[None], "seq", split_axis=2, concat_axis=0, tiled=True),
        lax.all_to_all(grad_vblk[None], "seq", split_axis=2, concat_axis=0, tiled=True),
    )
    grad_qhat, grad_khat, grad_values = (
        unpack(grads_back[0]),
        unpack(grads_back[1]),
        unpack(grads_back[2]),
    )
    projected = jnp.dot(attn, w_full, preferred_element_type=jnp.float32).astype(jnp.bfloat16)
    grad_queries = norm_back(grad_qhat, q_norm, q_factor).astype(jnp.bfloat16)
    grad_keys = norm_back(grad_khat, k_norm, k_factor).astype(jnp.bfloat16)
    local_term = lax.dot_general(
        attn, cotan, (((0,), (0,)), ((), ())), preferred_element_type=jnp.float32
    )
    summed = lax.psum_scatter(local_term, ("seq", "dp"), scatter_dimension=0, tiled=True)
    weight_grad = summed / math.sqrt(token_count * seq_devices * data_devices)
    return (projected[None], grad_queries[None], grad_keys[None], grad_values[None], weight_grad)


def remote(source, target, sent, landed, device):
    return pltpu.make_async_remote_copy(
        src_ref=source,
        dst_ref=target,
        send_sem=sent,
        recv_sem=landed,
        device_id=device,
        device_id_type=MESH,
    )


def normalize(rows):
    wide = rows.astype(jnp.float32)
    factor = lax.rsqrt(jnp.mean(wide * wide, axis=-1, keepdims=True) + EPS)
    return wide * factor, factor


def lanes(head):
    return pl.ds(pl.multiple_of(head * HD, HD), HD)


def dot(a, b, ca, cb):
    return lax.dot_general(a, b, (((ca,), (cb,)), ((), ())), preferred_element_type=jnp.float32)


def layer_kernel(
    heads, scale,
    q_in, k_in, v_in, c_in, w_in, labels_ref,
    gq_out, gk_out, gv_out, out_out, grad_out,
    gq_ref, gk_ref, gv_ref, out_ref, grad_ref,
    q_ref, k_ref, v_ref, c_ref, w_full, x_ref, full, xfull, ids_ref, slots,
    onehot_t, onehot, allow_ref, qk, gv, e_ref, num, den, own_out, cross_out, st_mine, st_got,
    stage_a, stage_g, stage_x, got_a, got_g, got_x,
    a_ref, w_ref, w_held, kept, x_stage, x_got, y_stage, y_got, z_stage, z_got,
    stored, stored_heads, loaded, w_sent, w_landed, sent, landed, xsent, xlanded, id_sent, id_landed, st_sent, st_landed,
    a_sent, a_landed, g_sent, g_landed, v_sent, v_landed, cx_sent, cx_landed,
    w_swap_sent, w_swap_landed, x_sent, x_landed, y_sent, y_landed, z_sent, z_landed,
):
    n = 2 * heads
    quarter = n // 4
    pairs = heads // 2
    chip, core = lax.axis_index("seq"), lax.axis_index("dp")
    other = 1 - core
    side, here = chip // heads, lax.rem(chip, heads)
    base, far = side * heads, (1 - side) * heads
    x, y, z = lax.rem(chip, 2), lax.rem(chip // 2, 2), chip // 4
    heavy = side == core
    light = jnp.logical_not(heavy)
    first = core == 0
    tokens = q_ref.shape[0]
    kind = q_ref.dtype
    clusters = qk.shape[1]
    rows_of = qk.shape[2]
    blocks = clusters // 2
    cap = rows_of // heads
    nslots = clusters * cap
    inv = 1.0 / math.sqrt(HD)
    zl = here // 4
    near_first = zl == core

    def toward(mask_a, mask_b):
        x_bit, y_bit, z_bit = [
            jnp.where(near_first, (mask_a >> b) & 1, (mask_b >> b) & 1) for b in range(3)
        ]
        return lax.rem(zl + z_bit, 2) * 4 + lax.rem(y + y_bit, 2) * 2 + lax.rem(x + x_bit, 2)

    order = tuple(zip((3, 1, 2, 0, 4, 6, 5, 7), (4, 6, 5, 7, 3, 1, 2, 0)))

    ins = ((q_in, q_ref), (k_in, k_ref), (v_in, v_ref), (c_in, c_ref), (w_in, w_full.at[core]))
    loads = [
        pltpu.make_async_copy(source, target, loaded.at[i])
        for i, (source, target) in enumerate(ins)
    ]
    for load in loads:
        load.start()

    barrier = pltpu.get_barrier_semaphore()

    def greet(step, carry):
        pl.semaphore_signal(
            barrier, inc=1, device_id=(lax.rem(chip + step, n), core), device_id_type=MESH
        )
        return carry

    lax.fori_loop(1, n, greet, 0)
    pl.semaphore_signal(barrier, inc=1, device_id=(chip, other), device_id_type=MESH)

    wide = jnp.broadcast_to(labels_ref[...].astype(jnp.float32), (tokens, tokens))
    before = lax.broadcasted_iota(jnp.int32, wide.shape, 0) < lax.broadcasted_iota(
        jnp.int32, wide.shape, 1
    )
    same = jnp.logical_and(wide.T == wide, before)
    rank = jnp.sum(jnp.where(same, 1.0, 0.0), axis=0, keepdims=True)
    ids_ref[...] = jnp.broadcast_to(wide[0:1] * cap + rank, ids_ref.shape)
    slots[chip] = ids_ref[...]

    pl.semaphore_wait(barrier, n)
    w_copy = remote(w_in, w_full.at[core], w_sent, w_landed, (chip, other))
    w_copy.start()

    spans = (pl.ds(0, 2), pl.ds(2, 1), pl.ds(3, 1))

    def data_copy(wave, head):
        span = spans[wave]
        return remote(
            x_ref.at[head, span], full.at[here, span], sent.at[wave, head],
            landed.at[wave, here], (base + head, core),
        )

    def cross_copy(wave, head):
        row = core if wave == 0 else 3 - core
        return remote(
            x_ref.at[head, row], xfull.at[here, wave],
            xsent.at[wave, head], xlanded.at[wave, here], (far + head, core),
        )

    def id_copy(peer):
        return remote(ids_ref, slots.at[chip], id_sent.at[peer], id_landed.at[chip], (peer, core))

    def send_ids(step, carry):
        head = lax.rem(here + step, heads)

        @pl.when(step > 0)
        def _():
            id_copy(base + head).start()

        @pl.when(light)
        def _():
            id_copy(far + head).start()

        return carry

    lax.fori_loop(0, heads, send_ids, 0)
    for load in loads:
        load.wait()

    per_core = heads // 2

    def prepare(wave, head):
        if wave == 0:
            x_ref[head, 0] = normalize(q_ref[:, lanes(head)])[0].astype(kind)
            x_ref[head, 1] = normalize(k_ref[:, lanes(head)])[0].astype(kind)
        elif wave == 1:
            x_ref[head, 2] = v_ref[:, lanes(head)]
        else:
            w_rows = w_full[head // per_core, lanes(lax.rem(head, per_core)), :]
            x_ref[head, 3] = dot(c_ref[...], w_rows, 1, 1).astype(kind)

    def send_data(wave, head):
        @pl.when(head != here)
        def _():
            data_copy(wave, head).start()

    for wave in range(3):
        if wave == 2:
            remote(w_in, w_full.at[other], w_sent, w_landed, (chip, other)).wait_recv()
        to_cross = (light, jnp.logical_and(light, other == 0), jnp.logical_and(light, first))[wave]
        for masks in order:
            head = toward(*masks)
            prepare(wave, head)

            @pl.when(to_cross)
            def _(head=head, wave=wave):
                cross_copy(min(wave, 1), head).start()

            @pl.when(heavy)
            def _(head=head, wave=wave):
                send_data(wave, head)

        @pl.when(light)
        def _(wave=wave):
            for masks in order:
                send_data(wave, toward(*masks))

    full[here] = x_ref[here]

    def wait_ids(peer):
        remote(ids_ref, slots.at[peer], id_sent.at[0], id_landed.at[peer], (chip, other)).wait_recv()

    def mark(peer):
        slot_row = slots[peer]
        down = lax.broadcasted_iota(jnp.int32, (nslots, tokens), 0).astype(jnp.float32)
        hot = jnp.where(down == slot_row[0:1], 1.0, 0.0)
        along = lax.broadcasted_iota(jnp.int32, (tokens, nslots), 1).astype(jnp.float32)
        onehot_t[peer] = jnp.where(along == slot_row.T[:, 0:1], 1.0, 0.0).astype(kind)
        onehot[peer] = hot.astype(kind)
        valid = jnp.broadcast_to(jnp.sum(hot, axis=1, keepdims=True), (nslots, HD))
        return valid.reshape(clusters, cap, HD)

    def pack_one(peer, rows):
        packed = dot(onehot[peer], rows, 1, 0)
        return packed.reshape(clusters, cap, packed.shape[1])

    def pair_rows(pair):
        return pl.ds(pl.multiple_of(pair * 2 * cap, 2 * cap), 2 * cap)

    def pair_toward(step):
        z_bit = lax.rem(step // 2 + jnp.where(near_first, 0, 1), 2)
        y_bit = lax.rem(step + jnp.where(near_first, 1, 0) * (1 - step // 2), 2)
        return lax.rem(zl + z_bit, 2) * 2 + lax.rem(y + y_bit, 2)

    def pack_own(wave):
        span = spans[wave]

        def body(step, carry):
            pair = pair_toward(step)
            parts, valids = [], []
            for index in range(2):
                source = 2 * pair + index

                @pl.when(source != here)
                def _():
                    if wave == 0:
                        wait_ids(base + source)
                    remote(
                        x_ref.at[0, span], full.at[source, span], sent.at[wave, 0],
                        landed.at[wave, source], (chip, other),
                    ).wait_recv()

                if wave == 0:
                    valids.append(mark(base + source))
                if wave == 0:
                    rows = jnp.concatenate([full[source, 0], full[source, 1]], axis=1)
                else:
                    rows = full[source, wave + 1]
                parts.append(pack_one(base + source, rows))
            both = jnp.concatenate(parts, axis=1).astype(kind)
            rows = pair_rows(pair)
            if wave == 0:
                qk[0, :, rows, :] = both[:, :, 0:HD]
                qk[1, :, rows, :] = both[:, :, HD:]
                gv[1, :, rows, HD:] = jnp.concatenate(valids, axis=1).astype(kind)
            else:
                gv[2 - wave, :, rows, 0:HD] = both
            return carry

        lax.fori_loop(0, pairs, body, 0)

    def pack_cross(wave):
        def body(step, carry):
            pair = pair_toward(step)
            parts, valids = [], []
            for index in range(2):
                source = 2 * pair + index
                if wave == 0:
                    wait_ids(far + source)
                remote(
                    x_ref.at[0, wave], xfull.at[source, wave], xsent.at[wave, 0],
                    xlanded.at[wave, source], (chip, other),
                ).wait_recv()
                if wave == 0:
                    valids.append(mark(far + source))
                parts.append(pack_one(far + source, xfull[source, wave]))
            both = jnp.concatenate(parts, axis=1).astype(kind)
            rows = pair_rows(pair)
            if wave == 0:
                qk[2, :, rows, :] = both
                gv[2, :, rows, HD:] = jnp.concatenate(valids, axis=1).astype(kind)
            else:
                gv[2, :, rows, 0:HD] = both
            return carry

        lax.fori_loop(0, pairs, body, 0)

    size = 2 * rows_of
    down = lax.broadcasted_iota(jnp.int32, (size, size), 0)
    along = lax.broadcasted_iota(jnp.int32, (size, size), 1)
    lane = lax.broadcasted_iota(jnp.int32, (size, HD), 1)
    group = 8

    one_cluster = (down < rows_of) == (along < rows_of)
    allow_ref[0] = jnp.where(jnp.logical_and(one_cluster, along <= down), 1.0, 0.0)
    allow_ref[1] = jnp.where(one_cluster, 1.0, 0.0)

    def of(ref, index, block, low, high):
        part = ref[index, pl.ds(2 * block, 2), :, low:high]
        return part.reshape(size, high - low)

    def put(ref, block, low, value):
        width = value.shape[1]
        ref[pl.ds(2 * block, 2), :, low : low + width] = value.astype(kind).reshape(
            2, rows_of, width
        )

    def scores(which, qi, ki):
        def body(step, carry):
            def one(block):
                found = dot(of(qk, qi, block, 0, HD), of(qk, ki, block, 0, HD), 1, 1)
                return block, (jnp.exp(found * inv) * allow_ref[which]).astype(kind)

            for block, weights in each(step, one):
                e_ref[which, block] = weights
            return carry

        lax.fori_loop(0, rounds, body, 0)

    def gather(which, block, vi):
        both = dot(e_ref[which, block], of(gv, vi, block, 0, 2 * HD), 1, 0)
        return both[:, :HD], both[:, HD:]

    def inner(block, grads, top):
        return jnp.sum(
            of(gv, grads, block, 0, HD).astype(jnp.float32) * top, axis=1, keepdims=True
        )

    def settle(target, block, rows, top, total):
        factor = 1.0 / jnp.where(total > 0, total, 1.0)
        den[rows, block] = jnp.broadcast_to(factor, (size, HD))
        put(target, block, 0, top * factor)

    def pick(found, block):
        return jnp.sum(jnp.where(lane == block, found, 0.0), axis=1, keepdims=True)

    shared_rows = heavy.astype(jnp.int32)
    rounds = blocks // group
    nothing = jnp.zeros((size, HD), jnp.float32)

    def each(step, one):
        return [one(step * group + i) for i in range(group)]

    def diagonal_whole(step, carry):
        for block, top, total in each(step, lambda block: (block,) + gather(0, block, 1)):
            num[0, block] = top
            settle(own_out, block, 0, top, total)
        return carry

    def diagonal_part(step, carry):
        for block, top, total in each(step, lambda block: (block,) + gather(0, block, 1)):
            num[0, block] = top
            carry = jnp.where(lane == block, total, carry)
        return carry

    def across_keys(step, carry):
        def one(block):
            top, total = gather(0, block, 1)
            top_x, total_x = gather(1, block, 2)
            return block, top + top_x, total + total_x

        for block, top, total in each(step, one):
            num[0, block] = top
            settle(own_out, block, 0, top, total)
        return carry

    def across_queries(step, carry):
        for block, top, total in each(step, lambda block: (block,) + gather(1, block, 1)):
            num[1, block] = top
            carry = jnp.where(lane == block, total, carry)
        return carry

    def st_copy(index):
        return remote(
            st_mine.at[index], st_got.at[index], st_sent.at[index], st_landed.at[index],
            (far + here, core),
        )

    def settle_shared(target):
        def body(step, carry):
            both = st_mine[0] + st_got[0]

            def one(block):
                return block, num[shared_rows, block], pick(both, block)

            for block, top, total in each(step, one):
                settle(target, block, shared_rows, top, total)
            return carry

        return body

    def shared_inner(step, carry):
        def one(block):
            return block, inner(block, 2 * shared_rows, num[shared_rows, block])

        for block, product in each(step, one):
            carry = jnp.where(lane == block, product, carry)
        return carry

    def scaled(block, rows, gi):
        return (of(gv, gi, block, 0, HD).astype(jnp.float32) * den[rows, block]).astype(kind)

    def value_light(step, carry):
        for block, found in each(
            step, lambda block: (block, dot(e_ref[0, block], scaled(block, 0, 0), 0, 0))
        ):
            put(own_out, block, 3 * HD, found)
        return carry

    def value_keys(step, carry):
        def one(block):
            grads = scaled(block, 0, 0)
            return block, dot(e_ref[0, block], grads, 0, 0), dot(e_ref[1, block], grads, 0, 0)

        for block, near, away in each(step, one):
            put(own_out, block, 3 * HD, near)
            put(cross_out, block, HD, away)
        return carry

    def value_queries(step, carry):
        def one(block):
            near = dot(e_ref[0, block], scaled(block, 0, 0), 0, 0)
            return block, near + dot(e_ref[1, block], scaled(block, 1, 2), 0, 0)

        for block, found in each(step, one):
            put(own_out, block, 3 * HD, found)
        return carry

    def slopes(block, which, rows, qi, ki, vi, gi, shared=False):
        product = dot(scaled(block, rows, gi), of(gv, vi, block, 0, HD), 1, 1)
        if shared:
            total = pick(st_mine[1] + st_got[1], block)
        else:
            total = inner(block, gi, num[rows, block])
        factor = den[rows, block]
        delta = total * factor * factor
        slope = (e_ref[which, block].astype(jnp.float32) * (product - delta)).astype(kind)
        return (
            dot(slope, of(qk, ki, block, 0, HD), 1, 0) * inv,
            dot(slope, of(qk, qi, block, 0, HD), 0, 0) * inv,
        )

    def slope_light(shared):
        def body(step, carry):
            def one(block):
                return (block,) + slopes(block, 0, 0, 0, 1, 1, 0, shared)

            for block, grad_q, grad_k in each(step, one):
                put(own_out, block, HD, grad_q)
                put(own_out, block, 2 * HD, grad_k)
            return carry

        return body

    def slope_keys(step, carry):
        def one(block):
            return (block,) + slopes(block, 0, 0, 0, 1, 1, 0) + slopes(block, 1, 0, 0, 2, 2, 0)

        for block, grad_q, grad_k, cross_q, cross_k in each(step, one):
            put(own_out, block, HD, grad_q + cross_q)
            put(own_out, block, 2 * HD, grad_k)
            put(cross_out, block, 0, cross_k)
        return carry

    def slope_queries(step, carry):
        def one(block):
            near = slopes(block, 0, 0, 0, 1, 1, 0)
            return (block,) + near + slopes(block, 1, 1, 2, 1, 1, 2, True)

        for block, grad_q, grad_k, cross_q, cross_k in each(step, one):
            put(own_out, block, HD, grad_q)
            put(own_out, block, 2 * HD, grad_k + cross_k)
            put(cross_out, block, HD, cross_q)
        return carry

    def by_role(light_queries, light_keys, heavy_queries, heavy_keys):
        for role, sequence, body in (
            (light, first, light_queries), (light, other == 0, light_keys),
            (heavy, first, heavy_queries), (heavy, other == 0, heavy_keys),
        ):
            @pl.when(jnp.logical_and(role, sequence))
            def _(body=body):
                lax.fori_loop(0, rounds, body, 0)

    def unpack(peer, ref, pair, low, high, index):
        both = ref[:, pair_rows(pair), low:high].astype(jnp.float32)
        part = both[:, index * cap : (index + 1) * cap, :].reshape(nslots, high - low)
        return dot(onehot_t[peer], part.astype(kind), 1, 0).astype(kind)

    def a_copy(head):
        return remote(
            stage_a.at[head, 0], got_a.at[here, 0], a_sent.at[head], a_landed.at[here],
            (base + head, core),
        )

    def g_copy(head):
        return remote(
            stage_g.at[head, pl.ds(0, 2)], got_g.at[here, pl.ds(0, 2)], g_sent.at[head],
            g_landed.at[here], (base + head, core),
        )

    def v_copy(head):
        return remote(
            stage_g.at[head, 2], got_g.at[here, 2], v_sent.at[head], v_landed.at[here], (base + head, core),
        )

    def cx_copy(index, head):
        return remote(
            stage_x.at[index, head], got_x.at[index, here], cx_sent.at[index, head],
            cx_landed.at[index, here], (far + head, core),
        )

    def return_own(low, high, stage, got, at, copy):
        def body(step, carry):
            pair = pair_toward(step)
            for index in range(2):
                target = 2 * pair + index
                found = unpack(base + target, own_out, pair, low, high, index)
                for part in range((high - low) // HD):
                    stage[target, at + part] = found[:, part * HD : (part + 1) * HD]

                @pl.when(target != here)
                def _():
                    copy(target).start()

                @pl.when(target == here)
                def _():
                    for part in range((high - low) // HD):
                        got[target, at + part] = stage[target, at + part]

            return carry

        lax.fori_loop(0, pairs, body, 0)

    def return_cross(part):
        def body(step, carry):
            pair = pair_toward(step)
            for index in range(2):
                target = 2 * pair + index
                stage_x[part, target] = unpack(
                    far + target, cross_out, pair, part * HD, (part + 1) * HD, index
                )
                cx_copy(part, target).start()
            return carry

        lax.fori_loop(0, pairs, body, 0)

    pack_own(0)
    scores(0, 0, 1)

    @pl.when(heavy)
    def _():
        pack_cross(0)
        scores(1, 2 * other, 1 + core)

    @pl.when(jnp.logical_and(heavy, other == 0))
    def _():
        pack_cross(1)

    pack_own(1)

    def return_attn():
        return_own(0, HD, stage_a, got_a, 0, a_copy)

    @pl.when(first)
    def _():
        @pl.when(heavy)
        def _():
            st_mine[0] = lax.fori_loop(0, rounds, across_queries, nothing)
            st_copy(0).start()
            lax.fori_loop(0, rounds, diagonal_whole, 0)
            return_attn()
            st_copy(0).wait_recv()
            lax.fori_loop(0, rounds, settle_shared(cross_out), 0)
            return_cross(0)
            pack_cross(1)

        @pl.when(light)
        def _():
            st_mine[0] = lax.fori_loop(0, rounds, diagonal_part, nothing)
            st_copy(0).start()
            st_copy(0).wait_recv()
            lax.fori_loop(0, rounds, settle_shared(own_out), 0)
            return_attn()

    @pl.when(other == 0)
    def _():
        @pl.when(heavy)
        def _():
            lax.fori_loop(0, rounds, across_keys, 0)

        @pl.when(light)
        def _():
            lax.fori_loop(0, rounds, diagonal_whole, 0)

        return_attn()

    pack_own(2)

    @pl.when(first)
    def _():
        st_mine[1] = lax.fori_loop(0, rounds, shared_inner, nothing)
        st_copy(1).start()

    by_role(value_light, value_light, value_queries, value_keys)

    @pl.when(jnp.logical_and(heavy, jnp.logical_not(first)))
    def _():
        return_cross(1)

    return_own(3 * HD, 4 * HD, stage_g, got_g, 2, v_copy)

    piece = w_ref.shape[2]

    def w_swap(peer):
        return remote(
            w_ref.at[peer, other], w_held.at[peer], w_swap_sent.at[peer], w_swap_landed.at[peer],
            (chip, other),
        )

    turn, turn_next = jnp.where(first, x, y), jnp.where(first, y, x)
    step_x, step_y = chip + 1 - 2 * x, chip + 2 - 4 * y

    def piece_of(j, bit):
        return (j // 2) * 4 + jnp.where(
            first, 2 * lax.rem(j, 2) + bit, lax.rem(j, 2) + 2 * bit
        )

    def x_copy(j):
        return remote(
            x_stage.at[j], x_got.at[j], x_sent.at[j], x_landed.at[j],
            (jnp.where(first, step_x, step_y), core),
        )

    def y_copy(j):
        return remote(
            y_stage.at[j], y_got.at[j], y_sent.at[j], y_landed.at[j],
            (jnp.where(first, step_y, step_x), core),
        )

    def z_copy(j):
        return remote(
            z_stage.at[j], z_got.at[z], z_sent.at[j], z_landed.at[z], (4 * j + 2 * y + x, core)
        )

    def wait_cross(part, head):
        remote(
            stage_x.at[part, 0], got_x.at[part, head], cx_sent.at[part, 0],
            cx_landed.at[part, head], (chip, other),
        ).wait_recv()

    def term(step, carry):
        head = lax.rem(here + heads - step, heads)

        @pl.when(head != here)
        def _():
            remote(
                stage_a.at[0, 0], got_a.at[head, 0], a_sent.at[0], a_landed.at[head], (chip, other)
            ).wait_recv()

        @pl.when(jnp.logical_and(first, light))
        def _():
            wait_cross(0, head)
            a_ref[:, lanes(head)] = (
                got_a[head, 0].astype(jnp.float32) + got_x[0, head].astype(jnp.float32)
            ).astype(kind)

        @pl.when(jnp.logical_not(jnp.logical_and(first, light)))
        def _():
            a_ref[:, lanes(head)] = got_a[head, 0]

        total = dot(a_ref[:, lanes(head)], c_ref[...], 0, 0)
        for index in range(4):
            w_ref[2 * head + index // 2, index % 2] = total[
                index * piece : (index + 1) * piece
            ].astype(w_ref.dtype)
        w_swap(2 * head).start()
        w_swap(2 * head + 1).start()
        return carry

    def both_cores(peer):
        w_swap(peer).wait_recv()
        return w_ref[peer, core].astype(jnp.float32) + w_held[peer].astype(jnp.float32)

    def x_phase(j, carry):
        x_stage[j] = both_cores(piece_of(j, 1 - turn)).astype(x_stage.dtype)
        x_copy(j).start()
        kept[j] = both_cores(piece_of(j, turn))
        return carry

    def y_phase(j, carry):
        away, stay = 2 * j + 1 - turn_next, 2 * j + turn_next
        x_copy(away).wait_recv()
        y_stage[j] = (kept[away] + x_got[away].astype(jnp.float32)).astype(y_stage.dtype)
        y_copy(j).start()
        x_copy(stay).wait_recv()
        kept[stay] += x_got[stay].astype(jnp.float32)
        return carry

    def z_phase(j, carry):
        y_copy(j).wait_recv()
        total = kept[2 * j + turn_next] + y_got[j].astype(jnp.float32)

        @pl.when(j != z)
        def _():
            z_stage[j] = total.astype(z_stage.dtype)
            z_copy(j).start()

        @pl.when(j == z)
        def _():
            grad_ref[...] = total

        return carry

    def z_sum(j, carry):
        @pl.when(j != z)
        def _():
            remote(
                z_stage.at[j], z_got.at[j], z_sent.at[j], z_landed.at[j], (4 * j + 2 * y + x, core)
            ).wait_recv()
            grad_ref[...] += z_got[j].astype(jnp.float32)
            z_copy(j).wait_send()

        y_copy(j).wait_send()
        return carry

    def ends(j, carry):
        x_copy(j).wait_send()
        w_swap(2 * j).wait_send()
        w_swap(2 * j + 1).wait_send()
        return carry

    lax.fori_loop(0, heads, term, 0)
    lax.fori_loop(0, n // 2, x_phase, 0)

    @pl.when(first)
    def _():
        st_copy(1).wait_recv()

    by_role(slope_light(True), slope_light(False), slope_queries, slope_keys)

    @pl.when(jnp.logical_and(heavy, first))
    def _():
        return_cross(1)

    @pl.when(jnp.logical_and(heavy, jnp.logical_not(first)))
    def _():
        return_cross(0)

    return_own(HD, 3 * HD, stage_g, got_g, 0, g_copy)
    lax.fori_loop(0, quarter, y_phase, 0)
    lax.fori_loop(0, quarter, z_phase, 0)

    depth = w_full.shape[1]
    tile = 2 * HD

    def project(step, carry):
        columns = pl.ds(pl.multiple_of(step * tile, tile), tile)
        total = jnp.dot(
            a_ref[:, :depth], w_full[0, :, columns], preferred_element_type=jnp.float32
        ) + jnp.dot(a_ref[:, depth:], w_full[1, :, columns], preferred_element_type=jnp.float32)
        out_ref[:, columns] = total.astype(out_ref.dtype)
        return carry

    lax.fori_loop(0, out_ref.shape[1] // tile, project, 0)
    keep_out = pltpu.make_async_copy(out_ref, out_out, stored.at[0])
    keep_out.start()

    results = ((gq_ref, gq_out), (gk_ref, gk_out), (gv_ref, gv_out))

    def keep(index, head):
        source, target = results[index]
        return pltpu.make_async_copy(
            source.at[:, lanes(head)], target.at[:, lanes(head)], stored_heads.at[index, head]
        )

    def finish(step, carry):
        head = lax.rem(here + heads - step, heads)

        @pl.when(head != here)
        def _():
            for span, gone, come in (
                (pl.ds(2, 1), v_sent, v_landed), (pl.ds(0, 2), g_sent, g_landed)
            ):
                remote(
                    stage_g.at[0, span], got_g.at[head, span], gone.at[0], come.at[head],
                    (chip, other),
                ).wait_recv()

        grads = [got_g[head, i].astype(jnp.float32) for i in range(3)]

        @pl.when(light)
        def _():
            wait_cross(1, head)

            @pl.when(jnp.logical_not(first))
            def _():
                wait_cross(0, head)

        extra = [
            jnp.where(light, got_x[i, head].astype(jnp.float32), 0.0) for i in range(2)
        ]
        grads[0] = grads[0] + jnp.where(first, extra[1], 0.0)
        grads[1] = grads[1] + jnp.where(first, 0.0, extra[0])
        grads[2] = grads[2] + jnp.where(first, 0.0, extra[1])
        for gradient, source, target in ((grads[0], q_ref, gq_ref), (grads[1], k_ref, gk_ref)):
            normed, factor = normalize(source[:, lanes(head)])
            mean = jnp.mean(gradient * normed, axis=-1, keepdims=True)
            target[:, lanes(head)] = (factor * (gradient - normed * mean)).astype(target.dtype)
        gv_ref[:, lanes(head)] = grads[2].astype(gv_ref.dtype)
        for index in range(3):
            keep(index, head).start()
        return carry

    lax.fori_loop(0, heads, finish, 0)
    lax.fori_loop(0, quarter, z_sum, 0)
    grad_ref[...] = grad_ref[...] * scale
    keep_grad = pltpu.make_async_copy(grad_ref, grad_out, stored.at[1])
    keep_grad.start()
    lax.fori_loop(0, n // 2, ends, 0)

    def sends_done(head, carry):
        for index in range(3):
            keep(index, head).wait()

        @pl.when(head != here)
        def _():
            id_copy(base + head).wait_send()
            data_copy(0, head).wait_send()
            data_copy(1, head).wait_send()
            data_copy(2, head).wait_send()
            a_copy(head).wait_send()
            g_copy(head).wait_send()
            v_copy(head).wait_send()

        @pl.when(light)
        def _():
            id_copy(far + head).wait_send()
            cross_copy(0, head).wait_send()
            cross_copy(1, head).wait_send()

        @pl.when(heavy)
        def _():
            cx_copy(0, head).wait_send()
            cx_copy(1, head).wait_send()

        return carry

    lax.fori_loop(0, heads, sends_done, 0)
    w_copy.wait_send()
    keep_out.wait()
    keep_grad.wait()

    @pl.when(first)
    def _():
        st_copy(0).wait_send()
        st_copy(1).wait_send()


def layer_call(q, k, v, c, w, labels, clusters, scale):
    tokens, features = q.shape
    heads = features // HD
    n = 2 * heads
    rows = heads * (2 * tokens // clusters)
    blocks = clusters // 2
    kind = q.dtype
    wide = jnp.float32
    vmem = pl.BlockSpec(memory_space=pltpu.VMEM)
    piece = (features // (2 * n), c.shape[1])
    like = jax.ShapeDtypeStruct(q.shape, kind)
    nslots = 2 * tokens
    pair = 2 * rows
    buffers = [(q.shape, kind)] * 3 + [
        (c.shape, kind), (piece, wide),
        (q.shape, kind), (q.shape, kind), (q.shape, kind), (c.shape, kind),
        ((2,) + w.shape, kind),
        ((heads, 4, tokens, HD), kind),
        ((heads, 4, tokens, HD), kind),
        ((heads, 2, tokens, HD), kind),
        ((8, tokens), wide),
        ((n, 8, tokens), wide),
        ((n, tokens, nslots), kind),
        ((n, nslots, tokens), kind),
        ((2, pair, pair), wide),
        ((3, clusters, rows, HD), kind),
        ((3, clusters, rows, 2 * HD), kind),
        ((2, blocks, pair, pair), kind),
        ((2, blocks, pair, HD), wide),
        ((2, blocks, pair, HD), wide),
        ((clusters, rows, 4 * HD), kind),
        ((clusters, rows, 2 * HD), kind),
        ((2, pair, HD), wide),
        ((2, pair, HD), wide),
        ((heads, 1, tokens, HD), kind),
        ((heads, 3, tokens, HD), kind),
        ((2, heads, tokens, HD), kind),
        ((heads, 1, tokens, HD), kind),
        ((heads, 3, tokens, HD), kind),
        ((2, heads, tokens, HD), kind),
        (q.shape, kind),
        ((n, 2) + piece, kind),
        ((n,) + piece, kind),
        ((n // 2,) + piece, wide),
        ((n // 2,) + piece, kind),
        ((n // 2,) + piece, kind),
    ] + [((n // 4,) + piece, kind)] * 4
    one = pltpu.SemaphoreType.DMA

    def many(*count):
        return pltpu.SemaphoreType.DMA(count)

    semaphores = (
        [many(2), many(3, heads), many(5), one, one]
        + [many(3, heads)] * 2
        + [many(2, heads)] * 2
        + [many(n)] * 2
        + [many(2)] * 2
        + [many(heads)] * 6
        + [many(2, heads)] * 2
        + [many(n)] * 2
        + [many(n // 2)] * 2
        + [many(n // 4)] * 4
    )
    return pl.pallas_call(
        functools.partial(layer_kernel, heads, scale),
        out_shape=(
            like, like, like, jax.ShapeDtypeStruct(c.shape, kind),
            jax.ShapeDtypeStruct(piece, wide),
        ),
        in_specs=[pl.BlockSpec(memory_space=pl.ANY)] * 5 + [vmem],
        out_specs=(pl.BlockSpec(memory_space=pl.ANY),) * 5,
        scratch_shapes=[pltpu.VMEM(shape, dtype) for shape, dtype in buffers] + semaphores,
        compiler_params=pltpu.CompilerParams(
            collective_id=0, has_side_effects=True, vmem_limit_bytes=60 << 20
        ),
    )(q, k, v, c, w, labels)


def hand_over_kernel(count, *refs):
    sources, targets, held = refs[:count], refs[count : 2 * count], refs[2 * count : 3 * count]
    done_in, done_out = refs[3 * count :]
    loads = [pltpu.make_async_copy(sources[i], held[i], done_in.at[i]) for i in range(count)]
    stores = [pltpu.make_async_copy(held[i], targets[i], done_out.at[i]) for i in range(count)]
    for load in loads:
        load.start()
    for load, store in zip(loads, stores):
        load.wait()
        store.start()
    for store in stores:
        store.wait()


def hand_over(*arrays):
    anywhere = pl.BlockSpec(memory_space=pl.ANY)
    count = len(arrays)
    return pl.pallas_call(
        functools.partial(hand_over_kernel, count),
        out_shape=tuple(jax.ShapeDtypeStruct(a.shape, a.dtype) for a in arrays),
        in_specs=[anywhere] * count,
        out_specs=(anywhere,) * count,
        scratch_shapes=[pltpu.VMEM(a.shape, a.dtype) for a in arrays]
        + [pltpu.SemaphoreType.DMA((count,))] * 2,
    )(*arrays)


def per_device_heads(queries, key_rows, value_rows, cotangent, w_out, cluster_ids):
    tokens = queries.shape[1]
    seq_devices = lax.axis_size("seq")
    scale = 1.0 / math.sqrt(tokens * seq_devices * 2)
    grad_queries, grad_keys, grad_values, projected, weight_grad = hand_over(*layer_call(
        queries[0], key_rows[0], value_rows[0], cotangent[0], w_out, cluster_ids,
        CL_DEV * seq_devices, scale,
    ))
    return (projected[None], grad_queries[None], grad_keys[None], grad_values[None], weight_grad)


def per_device(queries, *rest):
    heads = queries.shape[2] // HD
    if lax.axis_size("dp") == 2 and lax.axis_size("seq") == 2 * heads:
        return per_device_heads(queries, *rest)
    return per_device_slots(queries, *rest)


def solution(mesh):
    in_specs = (
        P("dp", "seq", None),
        P("dp", "seq", None),
        P("dp", "seq", None),
        P("dp", "seq", None),
        P("dp", None),
        P("dp", "seq"),
    )
    out_specs = (
        P("dp", "seq", None),
        P("dp", "seq", None),
        P("dp", "seq", None),
        P("dp", "seq", None),
        P(("seq", "dp"), None),
    )
    return jax.shard_map(
        per_device, mesh=mesh, in_specs=in_specs, out_specs=out_specs, check_vma=False
    )
```

```python
import functools
import math

import jax
import jax.numpy as jnp
from jax import lax
from jax.experimental import pallas as pl
from jax.experimental.pallas import tpu as pltpu
from jax.sharding import PartitionSpec as P

MESH = pl.DeviceIdType.MESH
HD = 128
CL_DEV = 4


EPS = 1e-06


def head_norm(matrix):
    shaped = matrix.astype(jnp.float32).reshape(matrix.shape[0], matrix.shape[1] // HD, HD)
    factor = lax.rsqrt(jnp.mean(shaped * shaped, axis=-1, keepdims=True) + EPS)
    return (shaped * factor, factor)


def norm_back(gradient, normed, factor):
    shaped = gradient.astype(jnp.float32).reshape(normed.shape)
    inner = jnp.mean(shaped * normed, axis=-1, keepdims=True)
    return (factor * (shaped - normed * inner)).reshape(normed.shape[0], -1)


def split_heads(blocks):
    return blocks.reshape(blocks.shape[0], blocks.shape[1], blocks.shape[2] // HD, HD)


def attend(q_blk, k_blk, v_blk, key_valid):
    q_four, k_four, v_four = (split_heads(q_blk), split_heads(k_blk), split_heads(v_blk))
    scores = jnp.einsum(
        "cqhd,ckhd->chqk", q_four, k_four, preferred_element_type=jnp.float32
    ) / math.sqrt(HD)
    positions = jnp.arange(q_blk.shape[1])
    below_diag = positions[None, :] <= positions[:, None]
    on_diagonal = positions[None, :] == positions[:, None]
    allowed = jnp.logical_or(
        jnp.logical_and(key_valid[:, None, None, :], below_diag[None, None]),
        on_diagonal[None, None],
    )
    weights = jnp.where(allowed, jnp.exp(scores), 0.0)
    probs = weights / jnp.sum(weights, axis=-1, keepdims=True)
    probs_b = probs.astype(jnp.bfloat16)
    attn = jnp.einsum(
        "chqk,ckhd->cqhd", probs_b, v_four, preferred_element_type=jnp.float32
    ).astype(jnp.bfloat16)
    return (attn.reshape(q_blk.shape), probs, probs_b)


def attend_back(q_blk, k_blk, v_blk, probs, probs_b, attn, d_blk):
    q_four, k_four, v_four = (split_heads(q_blk), split_heads(k_blk), split_heads(v_blk))
    d_four, a_four = (split_heads(d_blk), split_heads(attn))
    grad_value = jnp.einsum(
        "chqk,cqhd->ckhd", probs_b, d_four, preferred_element_type=jnp.float32
    ).astype(jnp.bfloat16)
    grad_prob = jnp.einsum("cqhd,ckhd->chqk", d_four, v_four, preferred_element_type=jnp.float32)
    delta_row = jnp.sum(d_four.astype(jnp.float32) * a_four.astype(jnp.float32), axis=-1)
    grad_score = (probs * (grad_prob - jnp.transpose(delta_row, (0, 2, 1))[..., None])).astype(
        jnp.bfloat16
    )
    grad_qhat = jnp.einsum(
        "chqk,ckhd->cqhd", grad_score, k_four, preferred_element_type=jnp.float32
    ) / math.sqrt(HD)
    grad_khat = jnp.einsum(
        "chqk,cqhd->ckhd", grad_score, q_four, preferred_element_type=jnp.float32
    ) / math.sqrt(HD)
    shape = q_blk.shape
    return (
        grad_qhat.astype(jnp.bfloat16).reshape(shape),
        grad_khat.astype(jnp.bfloat16).reshape(shape),
        grad_value.reshape(shape),
    )


def per_device_slots(queries, key_rows, value_rows, cotangent, w_out, cluster_ids):
    token_count = queries.shape[1]
    features = queries.shape[2]
    seq_devices = lax.axis_size("seq")
    data_devices = lax.axis_size("dp")
    capacity = 2 * token_count // (CL_DEV * seq_devices)
    total_slots = 2 * token_count
    labels = cluster_ids[0]
    positions = jnp.arange(token_count)
    matching = labels[:, None] == labels[None, :]
    earlier = positions[None, :] < positions[:, None]
    ranks = jnp.sum(jnp.logical_and(matching, earlier), axis=1)
    slot_index = labels * capacity + ranks

    def pack(matrix):
        empty = jnp.zeros((total_slots, matrix.shape[1]), matrix.dtype)
        return (
            empty.at[slot_index].set(matrix).reshape(seq_devices, CL_DEV, capacity, matrix.shape[1])
        )

    def unpack(returned):
        return returned.reshape(total_slots, -1)[slot_index]

    taken_slots = (
        jnp.zeros((total_slots,), jnp.bfloat16)
        .at[slot_index]
        .set(1.0)
        .reshape(seq_devices, CL_DEV, capacity)
    )
    q_norm, q_factor = head_norm(queries[0])
    k_norm, k_factor = head_norm(key_rows[0])
    q_hat = q_norm.reshape(token_count, features).astype(jnp.bfloat16)
    k_hat = k_norm.reshape(token_count, features).astype(jnp.bfloat16)
    cotan = cotangent[0]
    w_full = lax.all_gather(w_out, "dp", axis=0, tiled=True)
    received = (
        lax.all_to_all(pack(q_hat), "seq", split_axis=0, concat_axis=2, tiled=True),
        lax.all_to_all(pack(k_hat), "seq", split_axis=0, concat_axis=2, tiled=True),
        lax.all_to_all(pack(value_rows[0]), "seq", split_axis=0, concat_axis=2, tiled=True),
        lax.all_to_all(taken_slots, "seq", split_axis=0, concat_axis=2, tiled=True),
    )
    q_blk, k_blk, v_blk = (received[0][0], received[1][0], received[2][0])
    key_valid = received[3][0] > 0
    attn_blk, probs, probs_b = attend(q_blk, k_blk, v_blk, key_valid)
    attn_back = lax.all_to_all(attn_blk[None], "seq", split_axis=2, concat_axis=0, tiled=True)
    attn = unpack(attn_back)
    grad_attn = lax.dot_general(
        cotan, w_full, (((1,), (1,)), ((), ())), preferred_element_type=jnp.float32
    ).astype(jnp.bfloat16)
    grad_recv = lax.all_to_all(pack(grad_attn), "seq", split_axis=0, concat_axis=2, tiled=True)
    grad_qblk, grad_kblk, grad_vblk = attend_back(
        q_blk, k_blk, v_blk, probs, probs_b, attn_blk, grad_recv[0]
    )
    grads_back = (
        lax.all_to_all(grad_qblk[None], "seq", split_axis=2, concat_axis=0, tiled=True),
        lax.all_to_all(grad_kblk[None], "seq", split_axis=2, concat_axis=0, tiled=True),
        lax.all_to_all(grad_vblk[None], "seq", split_axis=2, concat_axis=0, tiled=True),
    )
    grad_qhat, grad_khat, grad_values = (
        unpack(grads_back[0]),
        unpack(grads_back[1]),
        unpack(grads_back[2]),
    )
    projected = jnp.dot(attn, w_full, preferred_element_type=jnp.float32).astype(jnp.bfloat16)
    grad_queries = norm_back(grad_qhat, q_norm, q_factor).astype(jnp.bfloat16)
    grad_keys = norm_back(grad_khat, k_norm, k_factor).astype(jnp.bfloat16)
    local_term = lax.dot_general(
        attn, cotan, (((0,), (0,)), ((), ())), preferred_element_type=jnp.float32
    )
    summed = lax.psum_scatter(local_term, ("seq", "dp"), scatter_dimension=0, tiled=True)
    weight_grad = summed / math.sqrt(token_count * seq_devices * data_devices)
    return (projected[None], grad_queries[None], grad_keys[None], grad_values[None], weight_grad)


def remote(source, target, sent, landed, device):
    return pltpu.make_async_remote_copy(
        src_ref=source,
        dst_ref=target,
        send_sem=sent,
        recv_sem=landed,
        device_id=device,
        device_id_type=MESH,
    )


def normalize(rows):
    wide = rows.astype(jnp.float32)
    factor = lax.rsqrt(jnp.mean(wide * wide, axis=-1, keepdims=True) + EPS)
    return wide * factor, factor


def lanes(head):
    return pl.ds(pl.multiple_of(head * HD, HD), HD)


def dot(a, b, ca, cb):
    return lax.dot_general(a, b, (((ca,), (cb,)), ((), ())), preferred_element_type=jnp.float32)


def layer_kernel(
    heads, scale,
    q_in, k_in, v_in, c_in, w_in, labels_ref,
    gq_out, gk_out, gv_out, out_out, grad_out,
    gq_ref, gk_ref, gv_ref, out_ref, grad_ref,
    q_ref, k_ref, v_ref, c_ref, w_full, x_ref, full, xfull, ids_ref, slots,
    onehot_t, onehot, allow_ref, qk, gv, e_ref, num, den, own_out, cross_out, st_mine, st_got,
    stage_a, stage_g, stage_x, got_a, got_g, got_x,
    a_ref, w_ref, w_held, kept, x_stage, x_got, y_stage, y_got, z_stage, z_got,
    stored, stored_heads, loaded, w_sent, w_landed, sent, landed, xsent, xlanded, id_sent, id_landed, st_sent, st_landed,
    a_sent, a_landed, g_sent, g_landed, v_sent, v_landed, cx_sent, cx_landed,
    w_swap_sent, w_swap_landed, x_sent, x_landed, y_sent, y_landed, z_sent, z_landed,
):
    n = 2 * heads
    quarter = n // 4
    pairs = heads // 2
    chip, core = lax.axis_index("seq"), lax.axis_index("dp")
    other = 1 - core
    side, here = chip // heads, lax.rem(chip, heads)
    base, far = side * heads, (1 - side) * heads
    x, y, z = lax.rem(chip, 2), lax.rem(chip // 2, 2), chip // 4
    heavy = side == core
    light = jnp.logical_not(heavy)
    first = core == 0
    tokens = q_ref.shape[0]
    kind = q_ref.dtype
    clusters = qk.shape[1]
    rows_of = qk.shape[2]
    blocks = clusters // 2
    cap = rows_of // heads
    nslots = clusters * cap
    inv = 1.0 / math.sqrt(HD)
    zl = here // 4
    near_first = zl == core

    def toward(mask_a, mask_b):
        x_bit, y_bit, z_bit = [
            jnp.where(near_first, (mask_a >> b) & 1, (mask_b >> b) & 1) for b in range(3)
        ]
        return lax.rem(zl + z_bit, 2) * 4 + lax.rem(y + y_bit, 2) * 2 + lax.rem(x + x_bit, 2)

    order = tuple(zip((3, 1, 2, 0, 4, 6, 5, 7), (4, 6, 5, 7, 3, 1, 2, 0)))

    ins = ((q_in, q_ref), (k_in, k_ref), (v_in, v_ref), (c_in, c_ref), (w_in, w_full.at[core]))
    loads = [
        pltpu.make_async_copy(source, target, loaded.at[i])
        for i, (source, target) in enumerate(ins)
    ]
    for load in loads:
        load.start()

    barrier = pltpu.get_barrier_semaphore()

    def greet(step, carry):
        pl.semaphore_signal(
            barrier, inc=1, device_id=(lax.rem(chip + step, n), core), device_id_type=MESH
        )
        return carry

    lax.fori_loop(1, n, greet, 0)
    pl.semaphore_signal(barrier, inc=1, device_id=(chip, other), device_id_type=MESH)

    wide = jnp.broadcast_to(labels_ref[...].astype(jnp.float32), (tokens, tokens))
    before = lax.broadcasted_iota(jnp.int32, wide.shape, 0) < lax.broadcasted_iota(
        jnp.int32, wide.shape, 1
    )
    same = jnp.logical_and(wide.T == wide, before)
    rank = jnp.sum(jnp.where(same, 1.0, 0.0), axis=0, keepdims=True)
    ids_ref[...] = jnp.broadcast_to(wide[0:1] * cap + rank, ids_ref.shape)
    slots[chip] = ids_ref[...]

    pl.semaphore_wait(barrier, n)
    w_copy = remote(w_in, w_full.at[core], w_sent, w_landed, (chip, other))
    w_copy.start()

    spans = (pl.ds(0, 2), pl.ds(2, 1), pl.ds(3, 1))

    def data_copy(wave, head):
        span = spans[wave]
        return remote(
            x_ref.at[head, span], full.at[here, span], sent.at[wave, head],
            landed.at[wave, here], (base + head, core),
        )

    def cross_copy(wave, head):
        row = core if wave == 0 else 3 - core
        return remote(
            x_ref.at[head, row], xfull.at[here, wave],
            xsent.at[wave, head], xlanded.at[wave, here], (far + head, core),
        )

    def id_copy(peer):
        return remote(ids_ref, slots.at[chip], id_sent.at[peer], id_landed.at[chip], (peer, core))

    def send_ids(step, carry):
        head = lax.rem(here + step, heads)

        @pl.when(step > 0)
        def _():
            id_copy(base + head).start()

        @pl.when(light)
        def _():
            id_copy(far + head).start()

        return carry

    lax.fori_loop(0, heads, send_ids, 0)
    for load in loads[:2]:
        load.wait()

    per_core = heads // 2

    def prepare(wave, head):
        if wave == 0:
            x_ref[head, 0] = normalize(q_ref[:, lanes(head)])[0].astype(kind)
            x_ref[head, 1] = normalize(k_ref[:, lanes(head)])[0].astype(kind)
        elif wave == 1:
            x_ref[head, 2] = v_ref[:, lanes(head)]
        else:
            w_rows = w_full[head // per_core, lanes(lax.rem(head, per_core)), :]
            x_ref[head, 3] = dot(c_ref[...], w_rows, 1, 1).astype(kind)

    def send_data(wave, head):
        @pl.when(head != here)
        def _():
            data_copy(wave, head).start()

    for wave in range(3):
        if wave == 1:
            for load in loads[2:]:
                load.wait()
        if wave == 2:
            remote(w_in, w_full.at[other], w_sent, w_landed, (chip, other)).wait_recv()
        to_cross = (light, jnp.logical_and(light, other == 0), jnp.logical_and(light, first))[wave]
        for masks in order:
            head = toward(*masks)
            prepare(wave, head)

            @pl.when(to_cross)
            def _(head=head, wave=wave):
                cross_copy(min(wave, 1), head).start()

            @pl.when(heavy)
            def _(head=head, wave=wave):
                send_data(wave, head)

        @pl.when(light)
        def _(wave=wave):
            for masks in order:
                send_data(wave, toward(*masks))

    full[here] = x_ref[here]

    def wait_ids(peer):
        remote(ids_ref, slots.at[peer], id_sent.at[0], id_landed.at[peer], (chip, other)).wait_recv()

    def mark(peer):
        slot_row = slots[peer]
        down = lax.broadcasted_iota(jnp.int32, (nslots, tokens), 0).astype(jnp.float32)
        hot = jnp.where(down == slot_row[0:1], 1.0, 0.0)
        along = lax.broadcasted_iota(jnp.int32, (tokens, nslots), 1).astype(jnp.float32)
        onehot_t[peer] = jnp.where(along == slot_row.T[:, 0:1], 1.0, 0.0).astype(kind)
        onehot[peer] = hot.astype(kind)
        valid = jnp.broadcast_to(jnp.sum(hot, axis=1, keepdims=True), (nslots, HD))
        return valid.reshape(clusters, cap, HD)

    def pack_one(peer, rows):
        packed = dot(onehot[peer], rows, 1, 0)
        return packed.reshape(clusters, cap, packed.shape[1])

    def pair_rows(pair):
        return pl.ds(pl.multiple_of(pair * 2 * cap, 2 * cap), 2 * cap)

    def pair_toward(step):
        z_bit = lax.rem(step // 2 + jnp.where(near_first, 0, 1), 2)
        y_bit = lax.rem(step + jnp.where(near_first, 1, 0) * (1 - step // 2), 2)
        return lax.rem(zl + z_bit, 2) * 2 + lax.rem(y + y_bit, 2)

    def pack_own(wave):
        span = spans[wave]

        def body(step, carry):
            pair = pair_toward(step)
            parts, valids = [], []
            for index in range(2):
                source = 2 * pair + index

                @pl.when(source != here)
                def _():
                    if wave == 0:
                        wait_ids(base + source)
                    remote(
                        x_ref.at[0, span], full.at[source, span], sent.at[wave, 0],
                        landed.at[wave, source], (chip, other),
                    ).wait_recv()

                if wave == 0:
                    valids.append(mark(base + source))
                if wave == 0:
                    rows = jnp.concatenate([full[source, 0], full[source, 1]], axis=1)
                else:
                    rows = full[source, wave + 1]
                parts.append(pack_one(base + source, rows))
            both = jnp.concatenate(parts, axis=1).astype(kind)
            rows = pair_rows(pair)
            if wave == 0:
                qk[0, :, rows, :] = both[:, :, 0:HD]
                qk[1, :, rows, :] = both[:, :, HD:]
                gv[1, :, rows, HD:] = jnp.concatenate(valids, axis=1).astype(kind)
            else:
                gv[2 - wave, :, rows, 0:HD] = both
            return carry

        lax.fori_loop(0, pairs, body, 0)

    def pack_cross(wave):
        def body(step, carry):
            pair = pair_toward(step)
            parts, valids = [], []
            for index in range(2):
                source = 2 * pair + index
                if wave == 0:
                    wait_ids(far + source)
                remote(
                    x_ref.at[0, wave], xfull.at[source, wave], xsent.at[wave, 0],
                    xlanded.at[wave, source], (chip, other),
                ).wait_recv()
                if wave == 0:
                    valids.append(mark(far + source))
                parts.append(pack_one(far + source, xfull[source, wave]))
            both = jnp.concatenate(parts, axis=1).astype(kind)
            rows = pair_rows(pair)
            if wave == 0:
                qk[2, :, rows, :] = both
                gv[2, :, rows, HD:] = jnp.concatenate(valids, axis=1).astype(kind)
            else:
                gv[2, :, rows, 0:HD] = both
            return carry

        lax.fori_loop(0, pairs, body, 0)

    size = 2 * rows_of
    down = lax.broadcasted_iota(jnp.int32, (size, size), 0)
    along = lax.broadcasted_iota(jnp.int32, (size, size), 1)
    lane = lax.broadcasted_iota(jnp.int32, (size, HD), 1)
    group = 16

    one_cluster = (down < rows_of) == (along < rows_of)
    allow_ref[0] = jnp.where(jnp.logical_and(one_cluster, along <= down), 1.0, 0.0)
    allow_ref[1] = jnp.where(one_cluster, 1.0, 0.0)

    def of(ref, index, block, low, high):
        part = ref[index, pl.ds(2 * block, 2), :, low:high]
        return part.reshape(size, high - low)

    def put(ref, block, low, value):
        width = value.shape[1]
        ref[pl.ds(2 * block, 2), :, low : low + width] = value.astype(kind).reshape(
            2, rows_of, width
        )

    def scores(which, qi, ki):
        def body(step, carry):
            def one(block):
                found = dot(of(qk, qi, block, 0, HD), of(qk, ki, block, 0, HD), 1, 1)
                return block, (jnp.exp(found * inv) * allow_ref[which]).astype(kind)

            for block, weights in each(step, one):
                e_ref[which, block] = weights
            return carry

        lax.fori_loop(0, rounds, body, 0)

    def gather(which, block, vi):
        both = dot(e_ref[which, block], of(gv, vi, block, 0, 2 * HD), 1, 0)
        return both[:, :HD], both[:, HD:]

    def inner(block, grads, top):
        return jnp.sum(
            of(gv, grads, block, 0, HD).astype(jnp.float32) * top, axis=1, keepdims=True
        )

    def settle(target, block, rows, top, total):
        factor = 1.0 / jnp.where(total > 0, total, 1.0)
        den[rows, block] = jnp.broadcast_to(factor, (size, HD))
        put(target, block, 0, top * factor)

    def pick(found, block):
        return jnp.sum(jnp.where(lane == block, found, 0.0), axis=1, keepdims=True)

    shared_rows = heavy.astype(jnp.int32)
    rounds = blocks // group
    nothing = jnp.zeros((size, HD), jnp.float32)

    def each(step, one):
        return [one(step * group + i) for i in range(group)]

    def diagonal_whole(step, carry):
        for block, top, total in each(step, lambda block: (block,) + gather(0, block, 1)):
            num[0, block] = top
            settle(own_out, block, 0, top, total)
        return carry

    def diagonal_part(step, carry):
        for block, top, total in each(step, lambda block: (block,) + gather(0, block, 1)):
            num[0, block] = top
            carry = jnp.where(lane == block, total, carry)
        return carry

    def across_keys(step, carry):
        def one(block):
            top, total = gather(0, block, 1)
            top_x, total_x = gather(1, block, 2)
            return block, top + top_x, total + total_x

        for block, top, total in each(step, one):
            num[0, block] = top
            settle(own_out, block, 0, top, total)
        return carry

    def across_queries(step, carry):
        for block, top, total in each(step, lambda block: (block,) + gather(1, block, 1)):
            num[1, block] = top
            carry = jnp.where(lane == block, total, carry)
        return carry

    def st_copy(index):
        return remote(
            st_mine.at[index], st_got.at[index], st_sent.at[index], st_landed.at[index],
            (far + here, core),
        )

    def settle_shared(target):
        def body(step, carry):
            both = st_mine[0] + st_got[0]

            def one(block):
                return block, num[shared_rows, block], pick(both, block)

            for block, top, total in each(step, one):
                settle(target, block, shared_rows, top, total)
            return carry

        return body

    def shared_inner(step, carry):
        def one(block):
            return block, inner(block, 2 * shared_rows, num[shared_rows, block])

        for block, product in each(step, one):
            carry = jnp.where(lane == block, product, carry)
        return carry

    def scaled(block, rows, gi):
        return (of(gv, gi, block, 0, HD).astype(jnp.float32) * den[rows, block]).astype(kind)

    def value_light(step, carry):
        for block, found in each(
            step, lambda block: (block, dot(e_ref[0, block], scaled(block, 0, 0), 0, 0))
        ):
            put(own_out, block, 3 * HD, found)
        return carry

    def value_keys(step, carry):
        def one(block):
            grads = scaled(block, 0, 0)
            return block, dot(e_ref[0, block], grads, 0, 0), dot(e_ref[1, block], grads, 0, 0)

        for block, near, away in each(step, one):
            put(own_out, block, 3 * HD, near)
            put(cross_out, block, HD, away)
        return carry

    def value_queries(step, carry):
        def one(block):
            near = dot(e_ref[0, block], scaled(block, 0, 0), 0, 0)
            return block, near + dot(e_ref[1, block], scaled(block, 1, 2), 0, 0)

        for block, found in each(step, one):
            put(own_out, block, 3 * HD, found)
        return carry

    def slopes(block, which, rows, qi, ki, vi, gi, shared=False):
        product = dot(scaled(block, rows, gi), of(gv, vi, block, 0, HD), 1, 1)
        if shared:
            total = pick(st_mine[1] + st_got[1], block)
        else:
            total = inner(block, gi, num[rows, block])
        factor = den[rows, block]
        delta = total * factor * factor
        slope = (e_ref[which, block].astype(jnp.float32) * (product - delta)).astype(kind)
        return (
            dot(slope, of(qk, ki, block, 0, HD), 1, 0) * inv,
            dot(slope, of(qk, qi, block, 0, HD), 0, 0) * inv,
        )

    def slope_light(shared):
        def body(step, carry):
            def one(block):
                return (block,) + slopes(block, 0, 0, 0, 1, 1, 0, shared)

            for block, grad_q, grad_k in each(step, one):
                put(own_out, block, HD, grad_q)
                put(own_out, block, 2 * HD, grad_k)
            return carry

        return body

    def slope_keys(step, carry):
        def one(block):
            return (block,) + slopes(block, 0, 0, 0, 1, 1, 0) + slopes(block, 1, 0, 0, 2, 2, 0)

        for block, grad_q, grad_k, cross_q, cross_k in each(step, one):
            put(own_out, block, HD, grad_q + cross_q)
            put(own_out, block, 2 * HD, grad_k)
            put(cross_out, block, 0, cross_k)
        return carry

    def slope_queries(step, carry):
        def one(block):
            near = slopes(block, 0, 0, 0, 1, 1, 0)
            return (block,) + near + slopes(block, 1, 1, 2, 1, 1, 2, True)

        for block, grad_q, grad_k, cross_q, cross_k in each(step, one):
            put(own_out, block, HD, grad_q)
            put(own_out, block, 2 * HD, grad_k + cross_k)
            put(cross_out, block, HD, cross_q)
        return carry

    def by_role(light_queries, light_keys, heavy_queries, heavy_keys):
        for role, sequence, body in (
            (light, first, light_queries), (light, other == 0, light_keys),
            (heavy, first, heavy_queries), (heavy, other == 0, heavy_keys),
        ):
            @pl.when(jnp.logical_and(role, sequence))
            def _(body=body):
                lax.fori_loop(0, rounds, body, 0)

    def unpack(peer, ref, pair, low, high, index):
        both = ref[:, pair_rows(pair), low:high].astype(jnp.float32)
        part = both[:, index * cap : (index + 1) * cap, :].reshape(nslots, high - low)
        return dot(onehot_t[peer], part.astype(kind), 1, 0).astype(kind)

    def a_copy(head):
        return remote(
            stage_a.at[head, 0], got_a.at[here, 0], a_sent.at[head], a_landed.at[here],
            (base + head, core),
        )

    def g_copy(head):
        return remote(
            stage_g.at[head, pl.ds(0, 2)], got_g.at[here, pl.ds(0, 2)], g_sent.at[head],
            g_landed.at[here], (base + head, core),
        )

    def v_copy(head):
        return remote(
            stage_g.at[head, 2], got_g.at[here, 2], v_sent.at[head], v_landed.at[here], (base + head, core),
        )

    def cx_copy(index, head):
        return remote(
            stage_x.at[index, head], got_x.at[index, here], cx_sent.at[index, head],
            cx_landed.at[index, here], (far + head, core),
        )

    def return_own(low, high, stage, got, at, copy):
        def body(step, carry):
            pair = pair_toward(step)
            for index in range(2):
                target = 2 * pair + index
                found = unpack(base + target, own_out, pair, low, high, index)
                for part in range((high - low) // HD):
                    stage[target, at + part] = found[:, part * HD : (part + 1) * HD]

                @pl.when(target != here)
                def _():
                    copy(target).start()

                @pl.when(target == here)
                def _():
                    for part in range((high - low) // HD):
                        got[target, at + part] = stage[target, at + part]

            return carry

        lax.fori_loop(0, pairs, body, 0, unroll=True)

    def return_cross(part):
        def body(step, carry):
            pair = pair_toward(step)
            for index in range(2):
                target = 2 * pair + index
                stage_x[part, target] = unpack(
                    far + target, cross_out, pair, part * HD, (part + 1) * HD, index
                )
                cx_copy(part, target).start()
            return carry

        lax.fori_loop(0, pairs, body, 0, unroll=True)

    pack_own(0)
    scores(0, 0, 1)

    @pl.when(heavy)
    def _():
        pack_cross(0)
        scores(1, 2 * other, 1 + core)

    @pl.when(jnp.logical_and(heavy, other == 0))
    def _():
        pack_cross(1)

    pack_own(1)

    def return_attn():
        return_own(0, HD, stage_a, got_a, 0, a_copy)

    @pl.when(first)
    def _():
        @pl.when(heavy)
        def _():
            st_mine[0] = lax.fori_loop(0, rounds, across_queries, nothing)
            st_copy(0).start()
            lax.fori_loop(0, rounds, diagonal_whole, 0)
            return_attn()
            st_copy(0).wait_recv()
            lax.fori_loop(0, rounds, settle_shared(cross_out), 0)
            return_cross(0)
            pack_cross(1)

        @pl.when(light)
        def _():
            st_mine[0] = lax.fori_loop(0, rounds, diagonal_part, nothing)
            st_copy(0).start()
            st_copy(0).wait_recv()
            lax.fori_loop(0, rounds, settle_shared(own_out), 0)
            return_attn()

    @pl.when(other == 0)
    def _():
        @pl.when(heavy)
        def _():
            lax.fori_loop(0, rounds, across_keys, 0)

        @pl.when(light)
        def _():
            lax.fori_loop(0, rounds, diagonal_whole, 0)

        return_attn()

    pack_own(2)

    @pl.when(first)
    def _():
        st_mine[1] = lax.fori_loop(0, rounds, shared_inner, nothing)
        st_copy(1).start()

    by_role(value_light, value_light, value_queries, value_keys)

    @pl.when(jnp.logical_and(heavy, jnp.logical_not(first)))
    def _():
        return_cross(1)

    return_own(3 * HD, 4 * HD, stage_g, got_g, 2, v_copy)

    piece = w_ref.shape[2]

    def w_swap(peer):
        return remote(
            w_ref.at[peer, other], w_held.at[peer], w_swap_sent.at[peer], w_swap_landed.at[peer],
            (chip, other),
        )

    turn, turn_next = jnp.where(first, x, y), jnp.where(first, y, x)
    step_x, step_y = chip + 1 - 2 * x, chip + 2 - 4 * y

    def piece_of(j, bit):
        return (j // 2) * 4 + jnp.where(
            first, 2 * lax.rem(j, 2) + bit, lax.rem(j, 2) + 2 * bit
        )

    def x_copy(j):
        return remote(
            x_stage.at[j], x_got.at[j], x_sent.at[j], x_landed.at[j],
            (jnp.where(first, step_x, step_y), core),
        )

    def y_copy(j):
        return remote(
            y_stage.at[j], y_got.at[j], y_sent.at[j], y_landed.at[j],
            (jnp.where(first, step_y, step_x), core),
        )

    def z_copy(j):
        return remote(
            z_stage.at[j], z_got.at[z], z_sent.at[j], z_landed.at[z], (4 * j + 2 * y + x, core)
        )

    def wait_cross(part, head):
        remote(
            stage_x.at[part, 0], got_x.at[part, head], cx_sent.at[part, 0],
            cx_landed.at[part, head], (chip, other),
        ).wait_recv()

    def term(step, carry):
        head = lax.rem(here + heads - step, heads)

        @pl.when(head != here)
        def _():
            remote(
                stage_a.at[0, 0], got_a.at[head, 0], a_sent.at[0], a_landed.at[head], (chip, other)
            ).wait_recv()

        @pl.when(jnp.logical_and(first, light))
        def _():
            wait_cross(0, head)
            a_ref[:, lanes(head)] = (
                got_a[head, 0].astype(jnp.float32) + got_x[0, head].astype(jnp.float32)
            ).astype(kind)

        @pl.when(jnp.logical_not(jnp.logical_and(first, light)))
        def _():
            a_ref[:, lanes(head)] = got_a[head, 0]

        total = dot(a_ref[:, lanes(head)], c_ref[...], 0, 0)
        for index in range(4):
            w_ref[2 * head + index // 2, index % 2] = total[
                index * piece : (index + 1) * piece
            ].astype(w_ref.dtype)
        w_swap(2 * head).start()
        w_swap(2 * head + 1).start()
        return carry

    def both_cores(peer):
        w_swap(peer).wait_recv()
        return w_ref[peer, core].astype(jnp.float32) + w_held[peer].astype(jnp.float32)

    def x_phase(j, carry):
        x_stage[j] = both_cores(piece_of(j, 1 - turn)).astype(x_stage.dtype)
        x_copy(j).start()
        kept[j] = both_cores(piece_of(j, turn))
        return carry

    def y_phase(j, carry):
        away, stay = 2 * j + 1 - turn_next, 2 * j + turn_next
        x_copy(away).wait_recv()
        y_stage[j] = (kept[away] + x_got[away].astype(jnp.float32)).astype(y_stage.dtype)
        y_copy(j).start()
        x_copy(stay).wait_recv()
        kept[stay] += x_got[stay].astype(jnp.float32)
        return carry

    def z_phase(j, carry):
        y_copy(j).wait_recv()
        total = kept[2 * j + turn_next] + y_got[j].astype(jnp.float32)

        @pl.when(j != z)
        def _():
            z_stage[j] = total.astype(z_stage.dtype)
            z_copy(j).start()

        @pl.when(j == z)
        def _():
            grad_ref[...] = total

        return carry

    def z_sum(j, carry):
        @pl.when(j != z)
        def _():
            remote(
                z_stage.at[j], z_got.at[j], z_sent.at[j], z_landed.at[j], (4 * j + 2 * y + x, core)
            ).wait_recv()
            grad_ref[...] += z_got[j].astype(jnp.float32)
            z_copy(j).wait_send()

        y_copy(j).wait_send()
        return carry

    def ends(j, carry):
        x_copy(j).wait_send()
        w_swap(2 * j).wait_send()
        w_swap(2 * j + 1).wait_send()
        return carry

    lax.fori_loop(0, heads, term, 0)
    lax.fori_loop(0, n // 2, x_phase, 0)

    @pl.when(first)
    def _():
        st_copy(1).wait_recv()

    by_role(slope_light(True), slope_light(False), slope_queries, slope_keys)

    @pl.when(jnp.logical_and(heavy, first))
    def _():
        return_cross(1)

    @pl.when(jnp.logical_and(heavy, jnp.logical_not(first)))
    def _():
        return_cross(0)

    return_own(HD, 3 * HD, stage_g, got_g, 0, g_copy)
    lax.fori_loop(0, quarter, y_phase, 0)
    lax.fori_loop(0, quarter, z_phase, 0)

    depth = w_full.shape[1]
    tile = 2 * HD

    def project(step, carry):
        columns = pl.ds(pl.multiple_of(step * tile, tile), tile)
        total = jnp.dot(
            a_ref[:, :depth], w_full[0, :, columns], preferred_element_type=jnp.float32
        ) + jnp.dot(a_ref[:, depth:], w_full[1, :, columns], preferred_element_type=jnp.float32)
        out_ref[:, columns] = total.astype(out_ref.dtype)
        return carry

    lax.fori_loop(0, out_ref.shape[1] // tile, project, 0)
    keep_out = pltpu.make_async_copy(out_ref, out_out, stored.at[0])
    keep_out.start()

    results = ((gq_ref, gq_out), (gk_ref, gk_out), (gv_ref, gv_out))

    def keep(index, head):
        source, target = results[index]
        return pltpu.make_async_copy(
            source.at[:, lanes(head)], target.at[:, lanes(head)], stored_heads.at[index, head]
        )

    def finish(step, carry):
        head = lax.rem(here + heads - step, heads)

        @pl.when(head != here)
        def _():
            for span, gone, come in (
                (pl.ds(2, 1), v_sent, v_landed), (pl.ds(0, 2), g_sent, g_landed)
            ):
                remote(
                    stage_g.at[0, span], got_g.at[head, span], gone.at[0], come.at[head],
                    (chip, other),
                ).wait_recv()

        grads = [got_g[head, i].astype(jnp.float32) for i in range(3)]

        @pl.when(light)
        def _():
            wait_cross(1, head)

            @pl.when(jnp.logical_not(first))
            def _():
                wait_cross(0, head)

        extra = [
            jnp.where(light, got_x[i, head].astype(jnp.float32), 0.0) for i in range(2)
        ]
        grads[0] = grads[0] + jnp.where(first, extra[1], 0.0)
        grads[1] = grads[1] + jnp.where(first, 0.0, extra[0])
        grads[2] = grads[2] + jnp.where(first, 0.0, extra[1])
        for gradient, source, target in ((grads[0], q_ref, gq_ref), (grads[1], k_ref, gk_ref)):
            normed, factor = normalize(source[:, lanes(head)])
            mean = jnp.mean(gradient * normed, axis=-1, keepdims=True)
            target[:, lanes(head)] = (factor * (gradient - normed * mean)).astype(target.dtype)
        gv_ref[:, lanes(head)] = grads[2].astype(gv_ref.dtype)
        for index in range(3):
            keep(index, head).start()
        return carry

    lax.fori_loop(0, heads, finish, 0)
    lax.fori_loop(0, quarter, z_sum, 0)
    grad_ref[...] = grad_ref[...] * scale
    keep_grad = pltpu.make_async_copy(grad_ref, grad_out, stored.at[1])
    keep_grad.start()
    lax.fori_loop(0, n // 2, ends, 0)

    def sends_done(head, carry):
        for index in range(3):
            keep(index, head).wait()

        @pl.when(head != here)
        def _():
            id_copy(base + head).wait_send()
            data_copy(0, head).wait_send()
            data_copy(1, head).wait_send()
            data_copy(2, head).wait_send()
            a_copy(head).wait_send()
            g_copy(head).wait_send()
            v_copy(head).wait_send()

        @pl.when(light)
        def _():
            id_copy(far + head).wait_send()
            cross_copy(0, head).wait_send()
            cross_copy(1, head).wait_send()

        @pl.when(heavy)
        def _():
            cx_copy(0, head).wait_send()
            cx_copy(1, head).wait_send()

        return carry

    lax.fori_loop(0, heads, sends_done, 0)
    w_copy.wait_send()
    keep_out.wait()
    keep_grad.wait()

    @pl.when(first)
    def _():
        st_copy(0).wait_send()
        st_copy(1).wait_send()


def layer_call(q, k, v, c, w, labels, clusters, scale):
    tokens, features = q.shape
    heads = features // HD
    n = 2 * heads
    rows = heads * (2 * tokens // clusters)
    blocks = clusters // 2
    kind = q.dtype
    wide = jnp.float32
    vmem = pl.BlockSpec(memory_space=pltpu.VMEM)
    piece = (features // (2 * n), c.shape[1])
    like = jax.ShapeDtypeStruct(q.shape, kind)
    nslots = 2 * tokens
    pair = 2 * rows
    buffers = [(q.shape, kind)] * 3 + [
        (c.shape, kind), (piece, wide),
        (q.shape, kind), (q.shape, kind), (q.shape, kind), (c.shape, kind),
        ((2,) + w.shape, kind),
        ((heads, 4, tokens, HD), kind),
        ((heads, 4, tokens, HD), kind),
        ((heads, 2, tokens, HD), kind),
        ((8, tokens), wide),
        ((n, 8, tokens), wide),
        ((n, tokens, nslots), kind),
        ((n, nslots, tokens), kind),
        ((2, pair, pair), wide),
        ((3, clusters, rows, HD), kind),
        ((3, clusters, rows, 2 * HD), kind),
        ((2, blocks, pair, pair), kind),
        ((2, blocks, pair, HD), wide),
        ((2, blocks, pair, HD), wide),
        ((clusters, rows, 4 * HD), kind),
        ((clusters, rows, 2 * HD), kind),
        ((2, pair, HD), wide),
        ((2, pair, HD), wide),
        ((heads, 1, tokens, HD), kind),
        ((heads, 3, tokens, HD), kind),
        ((2, heads, tokens, HD), kind),
        ((heads, 1, tokens, HD), kind),
        ((heads, 3, tokens, HD), kind),
        ((2, heads, tokens, HD), kind),
        (q.shape, kind),
        ((n, 2) + piece, kind),
        ((n,) + piece, kind),
        ((n // 2,) + piece, wide),
        ((n // 2,) + piece, kind),
        ((n // 2,) + piece, kind),
    ] + [((n // 4,) + piece, kind)] * 4
    one = pltpu.SemaphoreType.DMA

    def many(*count):
        return pltpu.SemaphoreType.DMA(count)

    semaphores = (
        [many(2), many(3, heads), many(5), one, one]
        + [many(3, heads)] * 2
        + [many(2, heads)] * 2
        + [many(n)] * 2
        + [many(2)] * 2
        + [many(heads)] * 6
        + [many(2, heads)] * 2
        + [many(n)] * 2
        + [many(n // 2)] * 2
        + [many(n // 4)] * 4
    )
    return pl.pallas_call(
        functools.partial(layer_kernel, heads, scale),
        out_shape=(
            like, like, like, jax.ShapeDtypeStruct(c.shape, kind),
            jax.ShapeDtypeStruct(piece, wide),
        ),
        in_specs=[pl.BlockSpec(memory_space=pl.ANY)] * 5 + [vmem],
        out_specs=(pl.BlockSpec(memory_space=pl.ANY),) * 5,
        scratch_shapes=[pltpu.VMEM(shape, dtype) for shape, dtype in buffers] + semaphores,
        compiler_params=pltpu.CompilerParams(
            collective_id=0, has_side_effects=True, vmem_limit_bytes=60 << 20
        ),
    )(q, k, v, c, w, labels)


def hand_over_kernel(count, *refs):
    sources, targets, held = refs[:count], refs[count : 2 * count], refs[2 * count : 3 * count]
    done_in, done_out = refs[3 * count :]
    loads = [pltpu.make_async_copy(sources[i], held[i], done_in.at[i]) for i in range(count)]
    stores = [pltpu.make_async_copy(held[i], targets[i], done_out.at[i]) for i in range(count)]
    for load in loads:
        load.start()
    for load, store in zip(loads, stores):
        load.wait()
        store.start()
    for store in stores:
        store.wait()


def hand_over(*arrays):
    anywhere = pl.BlockSpec(memory_space=pl.ANY)
    count = len(arrays)
    return pl.pallas_call(
        functools.partial(hand_over_kernel, count),
        out_shape=tuple(jax.ShapeDtypeStruct(a.shape, a.dtype) for a in arrays),
        in_specs=[anywhere] * count,
        out_specs=(anywhere,) * count,
        scratch_shapes=[pltpu.VMEM(a.shape, a.dtype) for a in arrays]
        + [pltpu.SemaphoreType.DMA((count,))] * 2,
    )(*arrays)


def per_device_heads(queries, key_rows, value_rows, cotangent, w_out, cluster_ids):
    tokens = queries.shape[1]
    seq_devices = lax.axis_size("seq")
    scale = 1.0 / math.sqrt(tokens * seq_devices * 2)
    grad_queries, grad_keys, grad_values, projected, weight_grad = hand_over(*layer_call(
        queries[0], key_rows[0], value_rows[0], cotangent[0], w_out, cluster_ids,
        CL_DEV * seq_devices, scale,
    ))
    return (projected[None], grad_queries[None], grad_keys[None], grad_values[None], weight_grad)


def per_device(queries, *rest):
    heads = queries.shape[2] // HD
    if lax.axis_size("dp") == 2 and lax.axis_size("seq") == 2 * heads:
        return per_device_heads(queries, *rest)
    return per_device_slots(queries, *rest)


def solution(mesh):
    in_specs = (
        P("dp", "seq", None),
        P("dp", "seq", None),
        P("dp", "seq", None),
        P("dp", "seq", None),
        P("dp", None),
        P("dp", "seq"),
    )
    out_specs = (
        P("dp", "seq", None),
        P("dp", "seq", None),
        P("dp", "seq", None),
        P("dp", "seq", None),
        P(("seq", "dp"), None),
    )
    return jax.shard_map(
        per_device, mesh=mesh, in_specs=in_specs, out_specs=out_specs, check_vma=False
    )
```

```python
import functools
import math

import jax
import jax.numpy as jnp
from jax import lax
from jax.experimental import pallas as pl
from jax.experimental.pallas import tpu as pltpu
from jax.sharding import PartitionSpec as P

MESH = pl.DeviceIdType.MESH
HD = 128
CL_DEV = 4


EPS = 1e-06


def head_norm(matrix):
    shaped = matrix.astype(jnp.float32).reshape(matrix.shape[0], matrix.shape[1] // HD, HD)
    factor = lax.rsqrt(jnp.mean(shaped * shaped, axis=-1, keepdims=True) + EPS)
    return (shaped * factor, factor)


def norm_back(gradient, normed, factor):
    shaped = gradient.astype(jnp.float32).reshape(normed.shape)
    inner = jnp.mean(shaped * normed, axis=-1, keepdims=True)
    return (factor * (shaped - normed * inner)).reshape(normed.shape[0], -1)


def split_heads(blocks):
    return blocks.reshape(blocks.shape[0], blocks.shape[1], blocks.shape[2] // HD, HD)


def attend(q_blk, k_blk, v_blk, key_valid):
    q_four, k_four, v_four = (split_heads(q_blk), split_heads(k_blk), split_heads(v_blk))
    scores = jnp.einsum(
        "cqhd,ckhd->chqk", q_four, k_four, preferred_element_type=jnp.float32
    ) / math.sqrt(HD)
    positions = jnp.arange(q_blk.shape[1])
    below_diag = positions[None, :] <= positions[:, None]
    on_diagonal = positions[None, :] == positions[:, None]
    allowed = jnp.logical_or(
        jnp.logical_and(key_valid[:, None, None, :], below_diag[None, None]),
        on_diagonal[None, None],
    )
    weights = jnp.where(allowed, jnp.exp(scores), 0.0)
    probs = weights / jnp.sum(weights, axis=-1, keepdims=True)
    probs_b = probs.astype(jnp.bfloat16)
    attn = jnp.einsum(
        "chqk,ckhd->cqhd", probs_b, v_four, preferred_element_type=jnp.float32
    ).astype(jnp.bfloat16)
    return (attn.reshape(q_blk.shape), probs, probs_b)


def attend_back(q_blk, k_blk, v_blk, probs, probs_b, attn, d_blk):
    q_four, k_four, v_four = (split_heads(q_blk), split_heads(k_blk), split_heads(v_blk))
    d_four, a_four = (split_heads(d_blk), split_heads(attn))
    grad_value = jnp.einsum(
        "chqk,cqhd->ckhd", probs_b, d_four, preferred_element_type=jnp.float32
    ).astype(jnp.bfloat16)
    grad_prob = jnp.einsum("cqhd,ckhd->chqk", d_four, v_four, preferred_element_type=jnp.float32)
    delta_row = jnp.sum(d_four.astype(jnp.float32) * a_four.astype(jnp.float32), axis=-1)
    grad_score = (probs * (grad_prob - jnp.transpose(delta_row, (0, 2, 1))[..., None])).astype(
        jnp.bfloat16
    )
    grad_qhat = jnp.einsum(
        "chqk,ckhd->cqhd", grad_score, k_four, preferred_element_type=jnp.float32
    ) / math.sqrt(HD)
    grad_khat = jnp.einsum(
        "chqk,cqhd->ckhd", grad_score, q_four, preferred_element_type=jnp.float32
    ) / math.sqrt(HD)
    shape = q_blk.shape
    return (
        grad_qhat.astype(jnp.bfloat16).reshape(shape),
        grad_khat.astype(jnp.bfloat16).reshape(shape),
        grad_value.reshape(shape),
    )


def per_device_slots(queries, key_rows, value_rows, cotangent, w_out, cluster_ids):
    token_count = queries.shape[1]
    features = queries.shape[2]
    seq_devices = lax.axis_size("seq")
    data_devices = lax.axis_size("dp")
    capacity = 2 * token_count // (CL_DEV * seq_devices)
    total_slots = 2 * token_count
    labels = cluster_ids[0]
    positions = jnp.arange(token_count)
    matching = labels[:, None] == labels[None, :]
    earlier = positions[None, :] < positions[:, None]
    ranks = jnp.sum(jnp.logical_and(matching, earlier), axis=1)
    slot_index = labels * capacity + ranks

    def pack(matrix):
        empty = jnp.zeros((total_slots, matrix.shape[1]), matrix.dtype)
        return (
            empty.at[slot_index].set(matrix).reshape(seq_devices, CL_DEV, capacity, matrix.shape[1])
        )

    def unpack(returned):
        return returned.reshape(total_slots, -1)[slot_index]

    taken_slots = (
        jnp.zeros((total_slots,), jnp.bfloat16)
        .at[slot_index]
        .set(1.0)
        .reshape(seq_devices, CL_DEV, capacity)
    )
    q_norm, q_factor = head_norm(queries[0])
    k_norm, k_factor = head_norm(key_rows[0])
    q_hat = q_norm.reshape(token_count, features).astype(jnp.bfloat16)
    k_hat = k_norm.reshape(token_count, features).astype(jnp.bfloat16)
    cotan = cotangent[0]
    w_full = lax.all_gather(w_out, "dp", axis=0, tiled=True)
    received = (
        lax.all_to_all(pack(q_hat), "seq", split_axis=0, concat_axis=2, tiled=True),
        lax.all_to_all(pack(k_hat), "seq", split_axis=0, concat_axis=2, tiled=True),
        lax.all_to_all(pack(value_rows[0]), "seq", split_axis=0, concat_axis=2, tiled=True),
        lax.all_to_all(taken_slots, "seq", split_axis=0, concat_axis=2, tiled=True),
    )
    q_blk, k_blk, v_blk = (received[0][0], received[1][0], received[2][0])
    key_valid = received[3][0] > 0
    attn_blk, probs, probs_b = attend(q_blk, k_blk, v_blk, key_valid)
    attn_back = lax.all_to_all(attn_blk[None], "seq", split_axis=2, concat_axis=0, tiled=True)
    attn = unpack(attn_back)
    grad_attn = lax.dot_general(
        cotan, w_full, (((1,), (1,)), ((), ())), preferred_element_type=jnp.float32
    ).astype(jnp.bfloat16)
    grad_recv = lax.all_to_all(pack(grad_attn), "seq", split_axis=0, concat_axis=2, tiled=True)
    grad_qblk, grad_kblk, grad_vblk = attend_back(
        q_blk, k_blk, v_blk, probs, probs_b, attn_blk, grad_recv[0]
    )
    grads_back = (
        lax.all_to_all(grad_qblk[None], "seq", split_axis=2, concat_axis=0, tiled=True),
        lax.all_to_all(grad_kblk[None], "seq", split_axis=2, concat_axis=0, tiled=True),
        lax.all_to_all(grad_vblk[None], "seq", split_axis=2, concat_axis=0, tiled=True),
    )
    grad_qhat, grad_khat, grad_values = (
        unpack(grads_back[0]),
        unpack(grads_back[1]),
        unpack(grads_back[2]),
    )
    projected = jnp.dot(attn, w_full, preferred_element_type=jnp.float32).astype(jnp.bfloat16)
    grad_queries = norm_back(grad_qhat, q_norm, q_factor).astype(jnp.bfloat16)
    grad_keys = norm_back(grad_khat, k_norm, k_factor).astype(jnp.bfloat16)
    local_term = lax.dot_general(
        attn, cotan, (((0,), (0,)), ((), ())), preferred_element_type=jnp.float32
    )
    summed = lax.psum_scatter(local_term, ("seq", "dp"), scatter_dimension=0, tiled=True)
    weight_grad = summed / math.sqrt(token_count * seq_devices * data_devices)
    return (projected[None], grad_queries[None], grad_keys[None], grad_values[None], weight_grad)


def remote(source, target, sent, landed, device):
    return pltpu.make_async_remote_copy(
        src_ref=source,
        dst_ref=target,
        send_sem=sent,
        recv_sem=landed,
        device_id=device,
        device_id_type=MESH,
    )


def normalize(rows):
    wide = rows.astype(jnp.float32)
    factor = lax.rsqrt(jnp.mean(wide * wide, axis=-1, keepdims=True) + EPS)
    return wide * factor, factor


def lanes(head):
    return pl.ds(pl.multiple_of(head * HD, HD), HD)


def dot(a, b, ca, cb):
    return lax.dot_general(a, b, (((ca,), (cb,)), ((), ())), preferred_element_type=jnp.float32)


def layer_kernel(
    heads, scale,
    q_in, k_in, v_in, c_in, w_in, labels_ref,
    gq_out, gk_out, gv_out, out_out, grad_out,
    gq_ref, gk_ref, gv_ref, out_ref, grad_ref,
    q_ref, k_ref, v_ref, c_ref, w_full, x_ref, full, xfull, ids_ref, slots,
    onehot_t, onehot, allow_ref, qk, gv, e_ref, num, den, own_out, cross_out, st_mine, st_got,
    stage_a, stage_g, stage_x, got_a, got_g, got_x,
    a_ref, w_ref, w_held, kept, x_stage, x_got, y_stage, y_got, z_stage, z_got,
    stored, stored_heads, loaded, w_sent, w_landed, sent, landed, xsent, xlanded, id_sent, id_landed, st_sent, st_landed,
    a_sent, a_landed, g_sent, g_landed, v_sent, v_landed, cx_sent, cx_landed,
    w_swap_sent, w_swap_landed, x_sent, x_landed, y_sent, y_landed, z_sent, z_landed,
):
    n = 2 * heads
    quarter = n // 4
    pairs = heads // 2
    chip, core = lax.axis_index("seq"), lax.axis_index("dp")
    other = 1 - core
    side, here = chip // heads, lax.rem(chip, heads)
    base, far = side * heads, (1 - side) * heads
    x, y, z = lax.rem(chip, 2), lax.rem(chip // 2, 2), chip // 4
    heavy = side == core
    light = jnp.logical_not(heavy)
    first = core == 0
    tokens = q_ref.shape[0]
    kind = q_ref.dtype
    clusters = qk.shape[1]
    rows_of = qk.shape[2]
    blocks = clusters // 2
    cap = rows_of // heads
    nslots = clusters * cap
    inv = 1.0 / math.sqrt(HD)
    zl = here // 4
    near_first = zl == core

    def toward(mask_a, mask_b):
        x_bit, y_bit, z_bit = [
            jnp.where(near_first, (mask_a >> b) & 1, (mask_b >> b) & 1) for b in range(3)
        ]
        return lax.rem(zl + z_bit, 2) * 4 + lax.rem(y + y_bit, 2) * 2 + lax.rem(x + x_bit, 2)

    order = tuple(zip((3, 1, 2, 0, 4, 6, 5, 7), (4, 6, 5, 7, 3, 1, 2, 0)))

    ins = ((q_in, q_ref), (k_in, k_ref), (v_in, v_ref), (c_in, c_ref), (w_in, w_full.at[core]))
    loads = [
        pltpu.make_async_copy(source, target, loaded.at[i])
        for i, (source, target) in enumerate(ins)
    ]
    for load in loads:
        load.start()

    barrier = pltpu.get_barrier_semaphore()

    def greet(step, carry):
        pl.semaphore_signal(
            barrier, inc=1, device_id=(lax.rem(chip + step, n), core), device_id_type=MESH
        )
        return carry

    lax.fori_loop(1, n, greet, 0)
    pl.semaphore_signal(barrier, inc=1, device_id=(chip, other), device_id_type=MESH)

    wide = jnp.broadcast_to(labels_ref[...].astype(jnp.float32), (tokens, tokens))
    before = lax.broadcasted_iota(jnp.int32, wide.shape, 0) < lax.broadcasted_iota(
        jnp.int32, wide.shape, 1
    )
    same = jnp.logical_and(wide.T == wide, before)
    rank = jnp.sum(jnp.where(same, 1.0, 0.0), axis=0, keepdims=True)
    ids_ref[...] = jnp.broadcast_to(wide[0:1] * cap + rank, ids_ref.shape)
    slots[chip] = ids_ref[...]

    pl.semaphore_wait(barrier, n)
    w_copy = remote(w_in, w_full.at[core], w_sent, w_landed, (chip, other))
    w_copy.start()

    spans = (pl.ds(0, 2), pl.ds(2, 1), pl.ds(3, 1))

    def data_copy(wave, head):
        span = spans[wave]
        return remote(
            x_ref.at[head, span], full.at[here, span], sent.at[wave, head],
            landed.at[wave, here], (base + head, core),
        )

    def cross_copy(wave, head):
        row = core if wave == 0 else 3 - core
        return remote(
            x_ref.at[head, row], xfull.at[here, wave],
            xsent.at[wave, head], xlanded.at[wave, here], (far + head, core),
        )

    def id_copy(peer):
        return remote(ids_ref, slots.at[chip], id_sent.at[peer], id_landed.at[chip], (peer, core))

    def send_ids(step, carry):
        head = lax.rem(here + step, heads)

        @pl.when(step > 0)
        def _():
            id_copy(base + head).start()

        @pl.when(light)
        def _():
            id_copy(far + head).start()

        return carry

    lax.fori_loop(0, heads, send_ids, 0)
    for load in loads[:2]:
        load.wait()

    per_core = heads // 2

    def prepare(wave, head):
        if wave == 0:
            x_ref[head, 0] = normalize(q_ref[:, lanes(head)])[0].astype(kind)
            x_ref[head, 1] = normalize(k_ref[:, lanes(head)])[0].astype(kind)
        elif wave == 1:
            x_ref[head, 2] = v_ref[:, lanes(head)]
        else:
            w_rows = w_full[head // per_core, lanes(lax.rem(head, per_core)), :]
            x_ref[head, 3] = dot(c_ref[...], w_rows, 1, 1).astype(kind)

    def send_data(wave, head):
        @pl.when(head != here)
        def _():
            data_copy(wave, head).start()

    for wave in range(3):
        if wave == 1:
            for load in loads[2:]:
                load.wait()
        if wave == 2:
            remote(w_in, w_full.at[other], w_sent, w_landed, (chip, other)).wait_recv()
        to_cross = (light, jnp.logical_and(light, other == 0), jnp.logical_and(light, first))[wave]
        for masks in order:
            head = toward(*masks)
            prepare(wave, head)

            @pl.when(to_cross)
            def _(head=head, wave=wave):
                cross_copy(min(wave, 1), head).start()

            @pl.when(heavy)
            def _(head=head, wave=wave):
                send_data(wave, head)

        @pl.when(light)
        def _(wave=wave):
            for masks in order:
                send_data(wave, toward(*masks))

    full[here] = x_ref[here]

    def wait_ids(peer):
        remote(ids_ref, slots.at[peer], id_sent.at[0], id_landed.at[peer], (chip, other)).wait_recv()

    def mark(peer):
        slot_row = slots[peer]
        down = lax.broadcasted_iota(jnp.int32, (nslots, tokens), 0).astype(jnp.float32)
        hot = jnp.where(down == slot_row[0:1], 1.0, 0.0)
        along = lax.broadcasted_iota(jnp.int32, (tokens, nslots), 1).astype(jnp.float32)
        onehot_t[peer] = jnp.where(along == slot_row.T[:, 0:1], 1.0, 0.0).astype(kind)
        onehot[peer] = hot.astype(kind)
        valid = jnp.broadcast_to(jnp.sum(hot, axis=1, keepdims=True), (nslots, HD))
        return valid.reshape(clusters, cap, HD)

    def pack_one(peer, rows):
        packed = dot(onehot[peer], rows, 1, 0)
        return packed.reshape(clusters, cap, packed.shape[1])

    def pair_rows(pair):
        return pl.ds(pl.multiple_of(pair * 2 * cap, 2 * cap), 2 * cap)

    def pair_toward(step):
        z_bit = lax.rem(step // 2 + jnp.where(near_first, 0, 1), 2)
        y_bit = lax.rem(step + jnp.where(near_first, 1, 0) * (1 - step // 2), 2)
        return lax.rem(zl + z_bit, 2) * 2 + lax.rem(y + y_bit, 2)

    def pack_own(wave):
        span = spans[wave]

        def body(step, carry):
            pair = pair_toward(step)
            parts, valids = [], []
            for index in range(2):
                source = 2 * pair + index

                @pl.when(source != here)
                def _():
                    if wave == 0:
                        wait_ids(base + source)
                    remote(
                        x_ref.at[0, span], full.at[source, span], sent.at[wave, 0],
                        landed.at[wave, source], (chip, other),
                    ).wait_recv()

                if wave == 0:
                    valids.append(mark(base + source))
                if wave == 0:
                    rows = jnp.concatenate([full[source, 0], full[source, 1]], axis=1)
                else:
                    rows = full[source, wave + 1]
                parts.append(pack_one(base + source, rows))
            both = jnp.concatenate(parts, axis=1).astype(kind)
            rows = pair_rows(pair)
            if wave == 0:
                qk[0, :, rows, :] = both[:, :, 0:HD]
                qk[1, :, rows, :] = both[:, :, HD:]
                gv[1, :, rows, HD:] = jnp.concatenate(valids, axis=1).astype(kind)
            else:
                gv[2 - wave, :, rows, 0:HD] = both
            return carry

        lax.fori_loop(0, pairs, body, 0)

    def pack_cross(wave):
        def body(step, carry):
            pair = pair_toward(step)
            parts, valids = [], []
            for index in range(2):
                source = 2 * pair + index
                if wave == 0:
                    wait_ids(far + source)
                remote(
                    x_ref.at[0, wave], xfull.at[source, wave], xsent.at[wave, 0],
                    xlanded.at[wave, source], (chip, other),
                ).wait_recv()
                if wave == 0:
                    valids.append(mark(far + source))
                parts.append(pack_one(far + source, xfull[source, wave]))
            both = jnp.concatenate(parts, axis=1).astype(kind)
            rows = pair_rows(pair)
            if wave == 0:
                qk[2, :, rows, :] = both
                gv[2, :, rows, HD:] = jnp.concatenate(valids, axis=1).astype(kind)
            else:
                gv[2, :, rows, 0:HD] = both
            return carry

        lax.fori_loop(0, pairs, body, 0)

    size = 2 * rows_of
    down = lax.broadcasted_iota(jnp.int32, (size, size), 0)
    along = lax.broadcasted_iota(jnp.int32, (size, size), 1)
    lane = lax.broadcasted_iota(jnp.int32, (size, HD), 1)
    group = 16

    one_cluster = (down < rows_of) == (along < rows_of)
    allow_ref[0] = jnp.where(jnp.logical_and(one_cluster, along <= down), 1.0, 0.0)
    allow_ref[1] = jnp.where(one_cluster, 1.0, 0.0)

    def of(ref, index, block, low, high):
        part = ref[index, pl.ds(2 * block, 2), :, low:high]
        return part.reshape(size, high - low)

    def put(ref, block, low, value):
        width = value.shape[1]
        ref[pl.ds(2 * block, 2), :, low : low + width] = value.astype(kind).reshape(
            2, rows_of, width
        )

    def scores(which, qi, ki):
        def body(step, carry):
            def one(block):
                found = dot(of(qk, qi, block, 0, HD), of(qk, ki, block, 0, HD), 1, 1)
                return block, (jnp.exp(found * inv) * allow_ref[which]).astype(kind)

            for block, weights in each(step, one):
                e_ref[which, block] = weights
            return carry

        lax.fori_loop(0, rounds, body, 0)

    def gather(which, block, vi):
        both = dot(e_ref[which, block], of(gv, vi, block, 0, 2 * HD), 1, 0)
        return both[:, :HD], both[:, HD:]

    def inner(block, grads, top):
        return jnp.sum(
            of(gv, grads, block, 0, HD).astype(jnp.float32) * top, axis=1, keepdims=True
        )

    def settle(target, block, rows, top, total):
        factor = 1.0 / jnp.where(total > 0, total, 1.0)
        den[rows, block] = jnp.broadcast_to(factor, (size, HD))
        put(target, block, 0, top * factor)

    def pick(found, block):
        return jnp.sum(jnp.where(lane == block, found, 0.0), axis=1, keepdims=True)

    shared_rows = heavy.astype(jnp.int32)
    rounds = blocks // group
    nothing = jnp.zeros((size, HD), jnp.float32)

    def each(step, one):
        return [one(step * group + i) for i in range(group)]

    def diagonal_whole(step, carry):
        for block, top, total in each(step, lambda block: (block,) + gather(0, block, 1)):
            num[0, block] = top
            settle(own_out, block, 0, top, total)
        return carry

    def diagonal_part(step, carry):
        for block, top, total in each(step, lambda block: (block,) + gather(0, block, 1)):
            num[0, block] = top
            carry = jnp.where(lane == block, total, carry)
        return carry

    def across_keys(step, carry):
        def one(block):
            top, total = gather(0, block, 1)
            top_x, total_x = gather(1, block, 2)
            return block, top + top_x, total + total_x

        for block, top, total in each(step, one):
            num[0, block] = top
            settle(own_out, block, 0, top, total)
        return carry

    def across_queries(step, carry):
        for block, top, total in each(step, lambda block: (block,) + gather(1, block, 1)):
            num[1, block] = top
            carry = jnp.where(lane == block, total, carry)
        return carry

    def st_copy(index):
        return remote(
            st_mine.at[index], st_got.at[index], st_sent.at[index], st_landed.at[index],
            (far + here, core),
        )

    def settle_shared(target):
        def body(step, carry):
            both = st_mine[0] + st_got[0]

            def one(block):
                return block, num[shared_rows, block], pick(both, block)

            for block, top, total in each(step, one):
                settle(target, block, shared_rows, top, total)
            return carry

        return body

    def shared_inner(step, carry):
        def one(block):
            return block, inner(block, 2 * shared_rows, num[shared_rows, block])

        for block, product in each(step, one):
            carry = jnp.where(lane == block, product, carry)
        return carry

    def scaled(block, rows, gi):
        return (of(gv, gi, block, 0, HD).astype(jnp.float32) * den[rows, block]).astype(kind)

    def value_light(step, carry):
        for block, found in each(
            step, lambda block: (block, dot(e_ref[0, block], scaled(block, 0, 0), 0, 0))
        ):
            put(own_out, block, 3 * HD, found)
        return carry

    def value_keys(step, carry):
        def one(block):
            grads = scaled(block, 0, 0)
            return block, dot(e_ref[0, block], grads, 0, 0), dot(e_ref[1, block], grads, 0, 0)

        for block, near, away in each(step, one):
            put(own_out, block, 3 * HD, near)
            put(cross_out, block, HD, away)
        return carry

    def value_queries(step, carry):
        def one(block):
            near = dot(e_ref[0, block], scaled(block, 0, 0), 0, 0)
            return block, near + dot(e_ref[1, block], scaled(block, 1, 2), 0, 0)

        for block, found in each(step, one):
            put(own_out, block, 3 * HD, found)
        return carry

    def slopes(block, which, rows, qi, ki, vi, gi, shared=False):
        product = dot(scaled(block, rows, gi), of(gv, vi, block, 0, HD), 1, 1)
        if shared:
            total = pick(st_mine[1] + st_got[1], block)
        else:
            total = inner(block, gi, num[rows, block])
        factor = den[rows, block]
        delta = total * factor * factor
        slope = (e_ref[which, block].astype(jnp.float32) * (product - delta)).astype(kind)
        return (
            dot(slope, of(qk, ki, block, 0, HD), 1, 0) * inv,
            dot(slope, of(qk, qi, block, 0, HD), 0, 0) * inv,
        )

    def slope_light(shared):
        def body(step, carry):
            def one(block):
                return (block,) + slopes(block, 0, 0, 0, 1, 1, 0, shared)

            for block, grad_q, grad_k in each(step, one):
                put(own_out, block, HD, grad_q)
                put(own_out, block, 2 * HD, grad_k)
            return carry

        return body

    def slope_keys(step, carry):
        def one(block):
            return (block,) + slopes(block, 0, 0, 0, 1, 1, 0) + slopes(block, 1, 0, 0, 2, 2, 0)

        for block, grad_q, grad_k, cross_q, cross_k in each(step, one):
            put(own_out, block, HD, grad_q + cross_q)
            put(own_out, block, 2 * HD, grad_k)
            put(cross_out, block, 0, cross_k)
        return carry

    def slope_queries(step, carry):
        def one(block):
            near = slopes(block, 0, 0, 0, 1, 1, 0)
            return (block,) + near + slopes(block, 1, 1, 2, 1, 1, 2, True)

        for block, grad_q, grad_k, cross_q, cross_k in each(step, one):
            put(own_out, block, HD, grad_q)
            put(own_out, block, 2 * HD, grad_k + cross_k)
            put(cross_out, block, HD, cross_q)
        return carry

    def by_role(light_queries, light_keys, heavy_queries, heavy_keys):
        for role, sequence, body in (
            (light, first, light_queries), (light, other == 0, light_keys),
            (heavy, first, heavy_queries), (heavy, other == 0, heavy_keys),
        ):
            @pl.when(jnp.logical_and(role, sequence))
            def _(body=body):
                lax.fori_loop(0, rounds, body, 0)

    def unpack(peer, ref, pair, low, high, index):
        both = ref[:, pair_rows(pair), low:high].astype(jnp.float32)
        part = both[:, index * cap : (index + 1) * cap, :].reshape(nslots, high - low)
        return dot(onehot_t[peer], part.astype(kind), 1, 0).astype(kind)

    def a_copy(head):
        return remote(
            stage_a.at[head, 0], got_a.at[here, 0], a_sent.at[head], a_landed.at[here],
            (base + head, core),
        )

    def g_copy(head):
        return remote(
            stage_g.at[head, pl.ds(0, 2)], got_g.at[here, pl.ds(0, 2)], g_sent.at[head],
            g_landed.at[here], (base + head, core),
        )

    def v_copy(head):
        return remote(
            stage_g.at[head, 2], got_g.at[here, 2], v_sent.at[head], v_landed.at[here], (base + head, core),
        )

    def cx_copy(index, head):
        return remote(
            stage_x.at[index, head], got_x.at[index, here], cx_sent.at[index, head],
            cx_landed.at[index, here], (far + head, core),
        )

    def return_own(low, high, stage, got, at, copy):
        def body(step, carry):
            pair = pair_toward(step)
            for index in range(2):
                target = 2 * pair + index
                found = unpack(base + target, own_out, pair, low, high, index)
                for part in range((high - low) // HD):
                    stage[target, at + part] = found[:, part * HD : (part + 1) * HD]

                @pl.when(target != here)
                def _():
                    copy(target).start()

                @pl.when(target == here)
                def _():
                    for part in range((high - low) // HD):
                        got[target, at + part] = stage[target, at + part]

            return carry

        lax.fori_loop(0, pairs, body, 0, unroll=True)

    def return_cross(part):
        def body(step, carry):
            pair = pair_toward(step)
            for index in range(2):
                target = 2 * pair + index
                stage_x[part, target] = unpack(
                    far + target, cross_out, pair, part * HD, (part + 1) * HD, index
                )
                cx_copy(part, target).start()
            return carry

        lax.fori_loop(0, pairs, body, 0, unroll=True)

    pack_own(0)
    scores(0, 0, 1)

    @pl.when(heavy)
    def _():
        pack_cross(0)
        scores(1, 2 * other, 1 + core)

    @pl.when(jnp.logical_and(heavy, other == 0))
    def _():
        pack_cross(1)

    pack_own(1)

    def return_attn():
        return_own(0, HD, stage_a, got_a, 0, a_copy)

    @pl.when(first)
    def _():
        @pl.when(heavy)
        def _():
            st_mine[0] = lax.fori_loop(0, rounds, across_queries, nothing)
            st_copy(0).start()
            lax.fori_loop(0, rounds, diagonal_whole, 0)
            return_attn()
            st_copy(0).wait_recv()
            lax.fori_loop(0, rounds, settle_shared(cross_out), 0)
            return_cross(0)
            pack_cross(1)

        @pl.when(light)
        def _():
            st_mine[0] = lax.fori_loop(0, rounds, diagonal_part, nothing)
            st_copy(0).start()
            st_copy(0).wait_recv()
            lax.fori_loop(0, rounds, settle_shared(own_out), 0)
            return_attn()

    @pl.when(other == 0)
    def _():
        @pl.when(heavy)
        def _():
            lax.fori_loop(0, rounds, across_keys, 0)

        @pl.when(light)
        def _():
            lax.fori_loop(0, rounds, diagonal_whole, 0)

        return_attn()

    pack_own(2)

    @pl.when(first)
    def _():
        st_mine[1] = lax.fori_loop(0, rounds, shared_inner, nothing)
        st_copy(1).start()

    by_role(value_light, value_light, value_queries, value_keys)

    @pl.when(jnp.logical_and(heavy, jnp.logical_not(first)))
    def _():
        return_cross(1)

    return_own(3 * HD, 4 * HD, stage_g, got_g, 2, v_copy)

    piece = w_ref.shape[2]

    def w_swap(peer):
        return remote(
            w_ref.at[peer, other], w_held.at[peer], w_swap_sent.at[peer], w_swap_landed.at[peer],
            (chip, other),
        )

    turn, turn_next = jnp.where(first, x, y), jnp.where(first, y, x)
    step_x, step_y = chip + 1 - 2 * x, chip + 2 - 4 * y

    def piece_of(j, bit):
        return (j // 2) * 4 + jnp.where(
            first, 2 * lax.rem(j, 2) + bit, lax.rem(j, 2) + 2 * bit
        )

    def x_copy(j):
        return remote(
            x_stage.at[j], x_got.at[j], x_sent.at[j], x_landed.at[j],
            (jnp.where(first, step_x, step_y), core),
        )

    def y_copy(j):
        return remote(
            y_stage.at[j], y_got.at[j], y_sent.at[j], y_landed.at[j],
            (jnp.where(first, step_y, step_x), core),
        )

    def z_copy(j):
        return remote(
            z_stage.at[j], z_got.at[z], z_sent.at[j], z_landed.at[z], (4 * j + 2 * y + x, core)
        )

    def wait_cross(part, head):
        remote(
            stage_x.at[part, 0], got_x.at[part, head], cx_sent.at[part, 0],
            cx_landed.at[part, head], (chip, other),
        ).wait_recv()

    def term(step, carry):
        head = lax.rem(here + heads - step, heads)

        @pl.when(head != here)
        def _():
            remote(
                stage_a.at[0, 0], got_a.at[head, 0], a_sent.at[0], a_landed.at[head], (chip, other)
            ).wait_recv()

        @pl.when(jnp.logical_and(first, light))
        def _():
            wait_cross(0, head)
            a_ref[:, lanes(head)] = (
                got_a[head, 0].astype(jnp.float32) + got_x[0, head].astype(jnp.float32)
            ).astype(kind)

        @pl.when(jnp.logical_not(jnp.logical_and(first, light)))
        def _():
            a_ref[:, lanes(head)] = got_a[head, 0]

        total = dot(a_ref[:, lanes(head)], c_ref[...], 0, 0)
        for index in range(4):
            w_ref[2 * head + index // 2, index % 2] = total[
                index * piece : (index + 1) * piece
            ].astype(w_ref.dtype)
        w_swap(2 * head).start()
        w_swap(2 * head + 1).start()
        return carry

    def both_cores(peer):
        w_swap(peer).wait_recv()
        return w_ref[peer, core].astype(jnp.float32) + w_held[peer].astype(jnp.float32)

    def x_phase(j, carry):
        x_stage[j] = both_cores(piece_of(j, 1 - turn)).astype(x_stage.dtype)
        x_copy(j).start()
        kept[j] = both_cores(piece_of(j, turn))
        return carry

    def y_phase(j, carry):
        away, stay = 2 * j + 1 - turn_next, 2 * j + turn_next
        x_copy(away).wait_recv()
        y_stage[j] = (kept[away] + x_got[away].astype(jnp.float32)).astype(y_stage.dtype)
        y_copy(j).start()
        x_copy(stay).wait_recv()
        kept[stay] += x_got[stay].astype(jnp.float32)
        return carry

    def z_phase(j, carry):
        y_copy(j).wait_recv()
        total = kept[2 * j + turn_next] + y_got[j].astype(jnp.float32)

        @pl.when(j != z)
        def _():
            z_stage[j] = total.astype(z_stage.dtype)
            z_copy(j).start()

        @pl.when(j == z)
        def _():
            grad_ref[...] = total

        return carry

    def z_sum(j, carry):
        @pl.when(j != z)
        def _():
            remote(
                z_stage.at[j], z_got.at[j], z_sent.at[j], z_landed.at[j], (4 * j + 2 * y + x, core)
            ).wait_recv()
            grad_ref[...] += z_got[j].astype(jnp.float32)
            z_copy(j).wait_send()

        y_copy(j).wait_send()
        return carry

    def ends(j, carry):
        x_copy(j).wait_send()
        w_swap(2 * j).wait_send()
        w_swap(2 * j + 1).wait_send()
        return carry

    lax.fori_loop(0, heads, term, 0, unroll=2)
    lax.fori_loop(0, n // 2, x_phase, 0, unroll=4)

    @pl.when(first)
    def _():
        st_copy(1).wait_recv()

    by_role(slope_light(True), slope_light(False), slope_queries, slope_keys)

    @pl.when(jnp.logical_and(heavy, first))
    def _():
        return_cross(1)

    @pl.when(jnp.logical_and(heavy, jnp.logical_not(first)))
    def _():
        return_cross(0)

    return_own(HD, 3 * HD, stage_g, got_g, 0, g_copy)
    lax.fori_loop(0, quarter, y_phase, 0)
    lax.fori_loop(0, quarter, z_phase, 0)

    depth = w_full.shape[1]
    tile = 2 * HD

    def project(step, carry):
        columns = pl.ds(pl.multiple_of(step * tile, tile), tile)
        total = jnp.dot(
            a_ref[:, :depth], w_full[0, :, columns], preferred_element_type=jnp.float32
        ) + jnp.dot(a_ref[:, depth:], w_full[1, :, columns], preferred_element_type=jnp.float32)
        out_ref[:, columns] = total.astype(out_ref.dtype)
        return carry

    lax.fori_loop(0, out_ref.shape[1] // tile, project, 0, unroll=True)
    keep_out = pltpu.make_async_copy(out_ref, out_out, stored.at[0])
    keep_out.start()

    results = ((gq_ref, gq_out), (gk_ref, gk_out), (gv_ref, gv_out))

    def keep(index, head):
        source, target = results[index]
        return pltpu.make_async_copy(
            source.at[:, lanes(head)], target.at[:, lanes(head)], stored_heads.at[index, head]
        )

    def finish(step, carry):
        head = lax.rem(here + heads - step, heads)

        @pl.when(head != here)
        def _():
            for span, gone, come in (
                (pl.ds(2, 1), v_sent, v_landed), (pl.ds(0, 2), g_sent, g_landed)
            ):
                remote(
                    stage_g.at[0, span], got_g.at[head, span], gone.at[0], come.at[head],
                    (chip, other),
                ).wait_recv()

        grads = [got_g[head, i].astype(jnp.float32) for i in range(3)]

        @pl.when(light)
        def _():
            wait_cross(1, head)

            @pl.when(jnp.logical_not(first))
            def _():
                wait_cross(0, head)

        extra = [
            jnp.where(light, got_x[i, head].astype(jnp.float32), 0.0) for i in range(2)
        ]
        grads[0] = grads[0] + jnp.where(first, extra[1], 0.0)
        grads[1] = grads[1] + jnp.where(first, 0.0, extra[0])
        grads[2] = grads[2] + jnp.where(first, 0.0, extra[1])
        for gradient, source, target in ((grads[0], q_ref, gq_ref), (grads[1], k_ref, gk_ref)):
            normed, factor = normalize(source[:, lanes(head)])
            mean = jnp.mean(gradient * normed, axis=-1, keepdims=True)
            target[:, lanes(head)] = (factor * (gradient - normed * mean)).astype(target.dtype)
        gv_ref[:, lanes(head)] = grads[2].astype(gv_ref.dtype)
        for index in range(3):
            keep(index, head).start()
        return carry

    lax.fori_loop(0, heads, finish, 0, unroll=2)
    lax.fori_loop(0, quarter, z_sum, 0)
    grad_ref[...] = grad_ref[...] * scale
    keep_grad = pltpu.make_async_copy(grad_ref, grad_out, stored.at[1])
    keep_grad.start()
    lax.fori_loop(0, n // 2, ends, 0)

    def sends_done(head, carry):
        for index in range(3):
            keep(index, head).wait()

        @pl.when(head != here)
        def _():
            id_copy(base + head).wait_send()
            data_copy(0, head).wait_send()
            data_copy(1, head).wait_send()
            data_copy(2, head).wait_send()
            a_copy(head).wait_send()
            g_copy(head).wait_send()
            v_copy(head).wait_send()

        @pl.when(light)
        def _():
            id_copy(far + head).wait_send()
            cross_copy(0, head).wait_send()
            cross_copy(1, head).wait_send()

        @pl.when(heavy)
        def _():
            cx_copy(0, head).wait_send()
            cx_copy(1, head).wait_send()

        return carry

    lax.fori_loop(0, heads, sends_done, 0)
    w_copy.wait_send()
    keep_out.wait()
    keep_grad.wait()

    @pl.when(first)
    def _():
        st_copy(0).wait_send()
        st_copy(1).wait_send()


def layer_call(q, k, v, c, w, labels, clusters, scale):
    tokens, features = q.shape
    heads = features // HD
    n = 2 * heads
    rows = heads * (2 * tokens // clusters)
    blocks = clusters // 2
    kind = q.dtype
    wide = jnp.float32
    vmem = pl.BlockSpec(memory_space=pltpu.VMEM)
    piece = (features // (2 * n), c.shape[1])
    like = jax.ShapeDtypeStruct(q.shape, kind)
    nslots = 2 * tokens
    pair = 2 * rows
    buffers = [(q.shape, kind)] * 3 + [
        (c.shape, kind), (piece, wide),
        (q.shape, kind), (q.shape, kind), (q.shape, kind), (c.shape, kind),
        ((2,) + w.shape, kind),
        ((heads, 4, tokens, HD), kind),
        ((heads, 4, tokens, HD), kind),
        ((heads, 2, tokens, HD), kind),
        ((8, tokens), wide),
        ((n, 8, tokens), wide),
        ((n, tokens, nslots), kind),
        ((n, nslots, tokens), kind),
        ((2, pair, pair), wide),
        ((3, clusters, rows, HD), kind),
        ((3, clusters, rows, 2 * HD), kind),
        ((2, blocks, pair, pair), kind),
        ((2, blocks, pair, HD), wide),
        ((2, blocks, pair, HD), wide),
        ((clusters, rows, 4 * HD), kind),
        ((clusters, rows, 2 * HD), kind),
        ((2, pair, HD), wide),
        ((2, pair, HD), wide),
        ((heads, 1, tokens, HD), kind),
        ((heads, 3, tokens, HD), kind),
        ((2, heads, tokens, HD), kind),
        ((heads, 1, tokens, HD), kind),
        ((heads, 3, tokens, HD), kind),
        ((2, heads, tokens, HD), kind),
        (q.shape, kind),
        ((n, 2) + piece, kind),
        ((n,) + piece, kind),
        ((n // 2,) + piece, wide),
        ((n // 2,) + piece, kind),
        ((n // 2,) + piece, kind),
    ] + [((n // 4,) + piece, kind)] * 4
    one = pltpu.SemaphoreType.DMA

    def many(*count):
        return pltpu.SemaphoreType.DMA(count)

    semaphores = (
        [many(2), many(3, heads), many(5), one, one]
        + [many(3, heads)] * 2
        + [many(2, heads)] * 2
        + [many(n)] * 2
        + [many(2)] * 2
        + [many(heads)] * 6
        + [many(2, heads)] * 2
        + [many(n)] * 2
        + [many(n // 2)] * 2
        + [many(n // 4)] * 4
    )
    return pl.pallas_call(
        functools.partial(layer_kernel, heads, scale),
        out_shape=(
            like, like, like, jax.ShapeDtypeStruct(c.shape, kind),
            jax.ShapeDtypeStruct(piece, wide),
        ),
        in_specs=[pl.BlockSpec(memory_space=pl.ANY)] * 5 + [vmem],
        out_specs=(pl.BlockSpec(memory_space=pl.ANY),) * 5,
        scratch_shapes=[pltpu.VMEM(shape, dtype) for shape, dtype in buffers] + semaphores,
        compiler_params=pltpu.CompilerParams(
            collective_id=0, has_side_effects=True, vmem_limit_bytes=60 << 20
        ),
    )(q, k, v, c, w, labels)


def hand_over_kernel(count, *refs):
    sources, targets, held = refs[:count], refs[count : 2 * count], refs[2 * count : 3 * count]
    done_in, done_out = refs[3 * count :]
    loads = [pltpu.make_async_copy(sources[i], held[i], done_in.at[i]) for i in range(count)]
    stores = [pltpu.make_async_copy(held[i], targets[i], done_out.at[i]) for i in range(count)]
    for load in loads:
        load.start()
    for load, store in zip(loads, stores):
        load.wait()
        store.start()
    for store in stores:
        store.wait()


def hand_over(*arrays):
    anywhere = pl.BlockSpec(memory_space=pl.ANY)
    count = len(arrays)
    return pl.pallas_call(
        functools.partial(hand_over_kernel, count),
        out_shape=tuple(jax.ShapeDtypeStruct(a.shape, a.dtype) for a in arrays),
        in_specs=[anywhere] * count,
        out_specs=(anywhere,) * count,
        scratch_shapes=[pltpu.VMEM(a.shape, a.dtype) for a in arrays]
        + [pltpu.SemaphoreType.DMA((count,))] * 2,
    )(*arrays)


def per_device_heads(queries, key_rows, value_rows, cotangent, w_out, cluster_ids):
    tokens = queries.shape[1]
    seq_devices = lax.axis_size("seq")
    scale = 1.0 / math.sqrt(tokens * seq_devices * 2)
    grad_queries, grad_keys, grad_values, projected, weight_grad = hand_over(*layer_call(
        queries[0], key_rows[0], value_rows[0], cotangent[0], w_out, cluster_ids,
        CL_DEV * seq_devices, scale,
    ))
    return (projected[None], grad_queries[None], grad_keys[None], grad_values[None], weight_grad)


def per_device(queries, *rest):
    heads = queries.shape[2] // HD
    if lax.axis_size("dp") == 2 and lax.axis_size("seq") == 2 * heads:
        return per_device_heads(queries, *rest)
    return per_device_slots(queries, *rest)


def solution(mesh):
    in_specs = (
        P("dp", "seq", None),
        P("dp", "seq", None),
        P("dp", "seq", None),
        P("dp", "seq", None),
        P("dp", None),
        P("dp", "seq"),
    )
    out_specs = (
        P("dp", "seq", None),
        P("dp", "seq", None),
        P("dp", "seq", None),
        P("dp", "seq", None),
        P(("seq", "dp"), None),
    )
    return jax.shard_map(
        per_device, mesh=mesh, in_specs=in_specs, out_specs=out_specs, check_vma=False
    )
```
